128 devices in a mesh: seq: 64 (over x_lo, z, y, core), col: 2 (over x_hi).
Axes of the slice: x: 4 (x_hi: 2, x_lo: 2; x = x_hi * 2 + x_lo), y: 4, z: 4, core: 2. Of those that a mesh axis runs over, the one named last changes fastest.
Arguments:
- tokens: bfloat16 [65536, 512], P('seq', 'col'), may hold values from -50 to 50
- cotangent: bfloat16 [65536, 512], P('seq', 'col'), may hold values from -6 to 6
- weight_in: bfloat16 [512, 4, 4, 128], P(None, None, 'col'), may hold values from -0.25 to 0.25
- weight_out: bfloat16 [4, 128, 512], P('col'), may hold values from -0.25 to 0.25
- history_ids: int32 [65536], replicated, may hold values from 0 to 31, never falling along the last dimension, each value on 1 to 4096 neighbouring positions
Outputs:
- out: bfloat16 [65536, 512], P('seq', 'col')
- grad_tokens: bfloat16 [65536, 512], P('seq', 'col')
- grad_weight_in: float32 [512, 4, 4, 128], P(None, None, 'col')
- grad_weight_out: float32 [4, 128, 512], P('col')
The draws below stay inside these ranges and needn't reach their ends.
Inputs may be any that keep to these rules, and one draw needn't show every extreme that they name: history_ids never fall along the stream; every id occurs; each history holds 1 to 4096 tokens and one holds exactly 4096.
All inputs are finite; a program needn't handle non-finite values.
Results may differ from the reference program's by a relative error of at most 0.0092.
Values may be sent and summed in bfloat16 or wider, within the bound.
A program may use at most 192 MiB of HBM per device.

```python
import math
import jax
import jax.numpy as jnp
import numpy as np
from jax import lax

D = 512
HEADS = 4
HEAD = 128
MAXLEN = 4096
TOKENS = 65536
HISTS = 32


def draw_tokens(key, part):
    first, second, third = jax.random.split(jax.random.fold_in(key, 11), 3)
    row_factor = jnp.exp(jax.random.uniform(second, (TOKENS, 1), jnp.float32, 0.0, jnp.log(10.0))) / jnp.sqrt(10.0)
    col_factor = jnp.exp(jax.random.uniform(third, (1, D), jnp.float32, 0.0, jnp.log(10.0))) / jnp.sqrt(10.0)
    base = jax.random.truncated_normal(first, -4.0, 4.0, (TOKENS, D), jnp.float32)
    return (base * row_factor * col_factor).astype(jnp.bfloat16)


def shard_levels(key, extent, shards, smallest, high):
    gain = 1.0
    for position, blocks in shards:
        steps = jax.random.uniform(jax.random.fold_in(jax.random.fold_in(key, 6), position), (blocks,), jnp.float32, smallest / len(shards), high / len(shards))
        gain = gain * jnp.repeat(jnp.exp(steps), extent[position] // blocks).reshape((-1,) + (1,) * (len(extent) - 1 - position))
    return gain


def profile(number_of, total, bound, slope):
    loads = [(1 << 20) // math.isqrt(standing ** slope) + 1 for standing in range(2, number_of + 1)]
    spare, counts = total - bound - (number_of - 1), [1] * (number_of - 1)
    while spare > 0:
        free = [i for i in range(number_of - 1) if counts[i] < bound]
        whole, left = sum([loads[i] for i in free]), spare
        for i in free:
            extra = min(bound - counts[i], max(1, left * loads[i] // whole), spare)
            counts[i] = counts[i] + extra
            spare = spare - extra
    return np.array([bound] + counts)


def ragged_sizes(key, number_of, total, reach, lean):
    if number_of == 2:
        one = jax.random.randint(key, (), max(1, total - reach), min(reach, total - 1) + 1)
        return jnp.stack([one, total - one])
    lengths = jnp.asarray(profile(number_of, total, reach, lean), jnp.int32)
    pairs = (number_of - 1) // 2
    source_of, taker = lengths[1:1 + 2 * pairs:2], lengths[2:2 + 2 * pairs:2]
    slack = jnp.minimum(source_of - 1, reach - taker)
    moved = jax.random.randint(jax.random.fold_in(key, 1), (pairs,), 0, 1 << 20) % (slack + 1)
    lengths = lengths.at[1:1 + 2 * pairs:2].set(source_of - moved).at[2:2 + 2 * pairs:2].set(taker + moved)
    return lengths[jax.random.permutation(jax.random.fold_in(key, 2), number_of)]


def normal_values(stream_key, shape, scale, bound, cuts=(), held_as=jnp.bfloat16):
    drawn = scale * jax.random.normal(stream_key, shape, jnp.float32)
    if cuts:
        drawn = drawn * shard_levels(stream_key, shape, cuts, -0.22, 0.18)
    return jnp.clip(drawn, -bound, bound).astype(held_as)


def setup_inputs(seed: int = 0) -> dict:
    seeds = jax.random.split(jax.random.key(seed), 6)
    tokens = draw_tokens(jax.random.fold_in(seeds[5], 71), 0)
    cotangent = normal_values(seeds[1], (TOKENS, D), 1.0, 6.0, ((0, 64), (1, 2)))
    weight_in = normal_values(seeds[2], (D, 4, HEADS, HEAD), D ** -0.5, 0.25, ((2, 2),))
    weight_out = normal_values(seeds[3], (HEADS, HEAD, D), D ** -0.5, 0.25, ((0, 2),))
    history_ids = jnp.searchsorted(jnp.cumsum(ragged_sizes(seeds[4], HISTS, TOKENS, MAXLEN, 2)), jnp.arange(TOKENS), side="right").astype(jnp.int32)
    return dict(tokens=tokens, cotangent=cotangent, weight_in=weight_in, weight_out=weight_out, history_ids=history_ids)


epsilon = 1e-05
head_floor = 1.0

def layer_norm(values, offset):
    center = values - lax.optimization_barrier(jnp.mean(values, axis=-1, keepdims=True))
    inv_std = lax.rsqrt(lax.optimization_barrier(jnp.mean(center * center, axis=-1, keepdims=True)) + offset)
    return (center * inv_std, inv_std)

def silu_slope(inputs):
    gate_value = jax.nn.sigmoid(inputs)
    return gate_value * (1.0 + inputs * (1.0 - gate_value))

def norm_back(grad_in, normed, inv_std):
    return inv_std * (grad_in - lax.optimization_barrier(jnp.mean(grad_in, axis=-1, keepdims=True)) - normed * lax.optimization_barrier(jnp.mean(grad_in * normed, axis=-1, keepdims=True)))

def narrow(values):
    return lax.optimization_barrier(values.astype(jnp.bfloat16)).astype(jnp.float32)

def reference(tokens, cotangent, weight_in, weight_out, history_ids):
    block_rows = math.gcd(TOKENS, 512)
    reach_back = (MAXLEN - 1 + block_rows - 1) // block_rows * block_rows
    key_window = min(reach_back + block_rows, TOKENS)
    block_count = TOKENS // block_rows
    score_scale = HEAD ** (-0.5)
    features = tokens.astype(jnp.float32)
    normed, inv_std = layer_norm(features, epsilon)
    normed_b = narrow(normed)
    pre_act = jnp.einsum('td,dphe->tphe', normed_b, weight_in.astype(jnp.float32))
    project = narrow(jax.nn.silu(pre_act))
    up_part = project[:, 0]
    value_part = project[:, 1]
    query_part = project[:, 2]
    key_part = project[:, 3]

    def pieces(block_index):
        q_start = (block_index * block_rows).astype(jnp.int32)
        k_start = jnp.clip(q_start + block_rows - key_window, 0, TOKENS - key_window).astype(jnp.int32)
        query_block = lax.dynamic_slice_in_dim(query_part, q_start, block_rows)
        key_block = lax.dynamic_slice_in_dim(key_part, k_start, key_window)
        value_block = lax.dynamic_slice_in_dim(value_part, k_start, key_window)
        ids_query = lax.dynamic_slice_in_dim(history_ids, q_start, block_rows)
        ids_key = lax.dynamic_slice_in_dim(history_ids, k_start, key_window)
        pos_query = q_start + jnp.arange(block_rows, dtype=jnp.int32)
        pos_key = k_start + jnp.arange(key_window, dtype=jnp.int32)
        allowed = ((ids_query[:, None] == ids_key[None, :]) & (pos_key[None, :] <= pos_query[:, None])).astype(jnp.float32)
        scores = score_scale * jnp.einsum('ihe,jhe->hij', query_block, key_block)
        weights_att = narrow(jax.nn.silu(scores) * allowed[None])
        return (q_start, k_start, query_block, key_block, value_block, allowed, scores, weights_att)

    def forward_block(block_index):
        parts = pieces(block_index)
        return jnp.einsum('hij,jhe->ihe', parts[7], parts[4])
    attended = lax.map(forward_block, jnp.arange(block_count, dtype=jnp.int32)).reshape(TOKENS, HEADS, HEAD)
    head_normed, head_scale = layer_norm(attended, head_floor)
    gated = narrow(head_normed * up_part)
    out_part = jnp.einsum('the,hed->td', gated, weight_out.astype(jnp.float32))
    out = (features + out_part).astype(jnp.bfloat16)
    grad_full = cotangent.astype(jnp.float32)
    grad_gated = jnp.einsum('td,hed->the', grad_full, weight_out.astype(jnp.float32))
    grad_up = grad_gated * head_normed
    grad_heads = norm_back(grad_gated * up_part, head_normed, head_scale)
    grad_narrow = narrow(grad_heads)

    def backward_block(sums_carry, block_index):
        grad_key, grad_value = sums_carry
        q_start, k_start, query_block, key_block, value_block, allowed, scores, weights_att = pieces(block_index)
        grad_block = lax.dynamic_slice_in_dim(grad_narrow, q_start, block_rows)
        grad_scores = narrow(score_scale * allowed[None] * silu_slope(scores) * jnp.einsum('ihe,jhe->hij', grad_block, value_block))
        grad_query = jnp.einsum('hij,jhe->ihe', grad_scores, key_block)
        key_add = jnp.einsum('hij,ihe->jhe', grad_scores, query_block)
        value_add = jnp.einsum('hij,ihe->jhe', weights_att, grad_block)
        grad_key = lax.dynamic_update_slice_in_dim(grad_key, lax.dynamic_slice_in_dim(grad_key, k_start, key_window) + key_add, k_start, 0)
        grad_value = lax.dynamic_update_slice_in_dim(grad_value, lax.dynamic_slice_in_dim(grad_value, k_start, key_window) + value_add, k_start, 0)
        return ((grad_key, grad_value), grad_query)
    empty_grad = jnp.zeros((TOKENS, HEADS, HEAD), jnp.float32)
    (grad_key, grad_value), grad_query = lax.scan(backward_block, (empty_grad, empty_grad), jnp.arange(block_count, dtype=jnp.int32))
    grad_query = grad_query.reshape(TOKENS, HEADS, HEAD)
    grad_proj = jnp.stack([grad_up, grad_value, grad_query, grad_key], axis=1)
    grad_pre = narrow(grad_proj * silu_slope(pre_act))
    inv_root = 1.0 / math.sqrt(TOKENS)
    grad_weight_in = jnp.einsum('td,tphe->dphe', normed_b, grad_pre) * inv_root
    grad_weight_out = jnp.einsum('the,td->hed', gated, grad_full) * inv_root
    grad_normed = jnp.einsum('tphe,dphe->td', grad_pre, weight_in.astype(jnp.float32))
    grad_tokens = (norm_back(grad_normed, normed, inv_std) + grad_full).astype(jnp.bfloat16)
    return (out, grad_tokens, grad_weight_in, grad_weight_out)
```

```python
import functools
import math

import jax
import jax.numpy as jnp
from jax import lax
from jax.experimental import pallas as pl
from jax.experimental.pallas import tpu as pltpu
from jax.sharding import PartitionSpec as P

MESH = pl.DeviceIdType.MESH
F32 = jnp.float32
BF16 = jnp.bfloat16

T = 1024
R = 2 * T
D = 512
E = 128
HALF = D // 2
CH = 256
NCH = T // CH
TQ = 512
TK = 512
WIN = 3 * R
EPS = 1e-5
FLOOR = 1.0
SCALE = E**-0.5
OUT_OF_MASK = -32.0
GR = D + E
YR = GR // 4
XR = YR // 2

NT = (((1,), (1,)), ((), ()))
TN = (((0,), (0,)), ((), ()))


def dot(a, b, dims=(((1,), (0,)), ((), ()))):
    return lax.dot_general(a, b, dims, preferred_element_type=F32)


def place():
    s = lax.axis_index("seq")
    c = lax.axis_index("col")
    return s, c


def greet(partners):
    barrier = pltpu.get_barrier_semaphore()
    for partner in partners:
        pl.semaphore_signal(barrier, inc=1, device_id=partner, device_id_type=MESH)
    pl.semaphore_wait(barrier, len(partners))


def send(src, dst, send_sem, recv_sem, device):
    copy = pltpu.make_async_remote_copy(
        src_ref=src,
        dst_ref=dst,
        send_sem=send_sem,
        recv_sem=recv_sem,
        device_id=device,
        device_id_type=MESH,
    )
    copy.start()
    return copy


def rows_at(start, size):
    return pl.ds(pl.multiple_of(start, size), size)


def project_kernel(
    tok_ref, cot_ref, w_ref, nb_ref, rs_ref, q_ref, up_ref, kv_ref, cg_ref, xg, ss, rs, kss, krs
):
    s, c = place()
    core = lax.rem(s, 2)
    other = (s + 1 - 2 * core, c)
    far = (s, 1 - c)
    n = lax.axis_size("seq")
    ahead = [(lax.rem(s + 2 * k, n), c) for k in (1, 2)]
    behind = [(lax.rem(s + n - 2 * k, n), c) for k in (1, 2)]
    greet([other, far] + ahead + behind)

    base = core * T
    obase = (1 - core) * T

    copies = []
    x_copies = {}
    for kind, (src, buf) in enumerate(((tok_ref, xg), (cot_ref, cg_ref))):
        for i in range(NCH):
            dst = buf.at[c, rows_at(base + i * CH, CH)]
            x_copies[kind, i] = send(
                src.at[pl.ds(i * CH, CH)], dst, ss.at[kind, 0, i], rs.at[kind, 0, i], far
            )
    o_copies = {}
    for kind, (src, buf) in enumerate(((tok_ref, xg), (cot_ref, cg_ref))):
        for i in range(NCH):
            dst = buf.at[c, rows_at(base + i * CH, CH)]
            o_copies[kind, i] = send(
                src.at[pl.ds(i * CH, CH)], dst, ss.at[kind, 1, i], rs.at[kind, 1, i], other
            )
    for i in range(NCH):
        xg[c, rows_at(base + i * CH, CH)] = tok_ref[pl.ds(i * CH, CH)]
        cg_ref[c, rows_at(base + i * CH, CH)] = cot_ref[pl.ds(i * CH, CH)]

    def forward(kind, i):
        buf = (xg, cg_ref)[kind]
        x_copies[kind, i].wait_recv()
        where = buf.at[1 - c, rows_at(base + i * CH, CH)]
        return send(where, where, ss.at[kind, 2, i], rs.at[kind, 2, i], other)

    def compute(start, slot):
        rr = rows_at(start, CH)
        x0 = xg[0, rr].astype(F32)
        x1 = xg[1, rr].astype(F32)
        mean = (jnp.sum(x0, -1, keepdims=True) + jnp.sum(x1, -1, keepdims=True)) * (1.0 / D)
        x0 = x0 - mean
        x1 = x1 - mean
        var = (
            jnp.sum(x0 * x0, -1, keepdims=True) + jnp.sum(x1 * x1, -1, keepdims=True)
        ) * (1.0 / D)
        inv = lax.rsqrt(var + EPS)
        n0 = (x0 * inv).astype(BF16)
        n1 = (x1 * inv).astype(BF16)
        nb_ref[rr, :HALF] = n0
        nb_ref[rr, HALF:] = n1
        rs_ref[rr] = jnp.broadcast_to(inv, (CH, E))
        half = 0.5 * (dot(n0, w_ref[:HALF]) + dot(n1, w_ref[HALF:]))
        proj = (half + half * jnp.tanh(half)).astype(BF16)
        up_ref[rr] = proj[:, :E]
        q_ref[rr] = proj[:, 2 * E : 3 * E]
        kv_ref[2, rr, :E] = proj[:, 3 * E :]
        kv_ref[2, rr, E:] = proj[:, E : 2 * E]
        for k in (0, 1):
            copies.append(
                send(
                    kv_ref.at[2, rr],
                    kv_ref.at[1 - k, rr],
                    kss.at[k, slot],
                    krs.at[k, slot],
                    ahead[k],
                )
            )

    f_copies = {}
    for i in range(NCH):
        f_copies[0, i] = forward(0, i)
        compute(base + i * CH, i)
        o_copies[0, i].wait_recv()
        f_copies[0, i].wait_recv()
        compute(obase + i * CH, NCH + i)
    for i in range(NCH):
        f_copies[1, i] = forward(1, i)
    for i in range(NCH):
        o_copies[1, i].wait_recv()
        f_copies[1, i].wait_recv()
    for copy in list(x_copies.values()) + list(o_copies.values()) + list(f_copies.values()):
        copy.wait_send()
    for copy in copies:
        copy.wait()


def project(tokens, cotangent, w):
    vm = pl.BlockSpec(memory_space=pltpu.VMEM)
    return pl.pallas_call(
        project_kernel,
        out_shape=(
            jax.ShapeDtypeStruct((R, D), BF16),
            jax.ShapeDtypeStruct((R, E), F32),
            jax.ShapeDtypeStruct((R, E), BF16),
            jax.ShapeDtypeStruct((R, E), BF16),
            jax.ShapeDtypeStruct((3, R, 2 * E), BF16),
            jax.ShapeDtypeStruct((2, R, HALF), BF16),
        ),
        in_specs=[vm] * 3,
        out_specs=(vm,) * 6,
        scratch_shapes=[
            pltpu.VMEM((2, R, HALF), BF16),
            pltpu.SemaphoreType.DMA((2, 3, NCH)),
            pltpu.SemaphoreType.DMA((2, 3, NCH)),
            pltpu.SemaphoreType.DMA((2, 2 * NCH)),
            pltpu.SemaphoreType.DMA((2, 2 * NCH)),
        ],
        compiler_params=pltpu.CompilerParams(
            collective_id=0, has_side_effects=True, vmem_limit_bytes=56 * 1024 * 1024
        ),
        cost_estimate=pl.CostEstimate(flops=2 * R * D * D, bytes_accessed=16 << 20, transcendentals=R * D),
        name="gather_project",
    )(tokens, cotangent, w)


def attention_kernel(
    lo_ref, q_ref, kv_ref, up_ref, cg_ref, wo_ref, id_ref,
    op_ref, gated_ref, dup_ref, dq_ref, dkv_ref, dfar_ref,
    idc, acc,
):
    for j in range(WIN // E):
        row = id_ref[0:1, j * E : (j + 1) * E]
        idc[j * E : (j + 1) * E, :] = jnp.broadcast_to(row, (E, E)).T

    @pl.loop(0, WIN // TK)
    def _(j):
        acc[rows_at(j * TK, TK), :] = jnp.zeros((TK, 2 * E), F32)

    def spread(column, width):
        return jnp.concatenate([column] * (width // E), axis=1)

    first = 2 * R // TK

    @pl.loop(0, R // TQ)
    def _(t):
        rr = rows_at(t * TQ, TQ)
        q = q_ref[rr, :]
        wr = rows_at(2 * R + t * TQ, TQ)
        idq_col = idc[wr, :]
        idq_row = id_ref[0:1, wr]
        low = lo_ref[t]
        last = first + t * TQ // TK

        def forward(kt, total, causal):
            kr = rows_at(kt * TK, TK)
            half = dot(q, kv_ref[kr, :E], NT) * (0.5 * SCALE)
            ok = spread(idq_col, TK) == id_ref[0:1, kr]
            if causal:
                ri = lax.broadcasted_iota(jnp.int32, (TQ, TK), 0)
                ci = lax.broadcasted_iota(jnp.int32, (TQ, TK), 1)
                ok = ok & (ci <= ri)
            half = jnp.where(ok, half, OUT_OF_MASK)
            weights = (half + half * jnp.tanh(half)).astype(BF16)
            return total + dot(weights, kv_ref[kr, E:])

        att = lax.fori_loop(
            low, last, functools.partial(forward, causal=False), jnp.zeros((TQ, E), F32)
        )
        att = forward(last, att, True)

        center = att - jnp.mean(att, -1, keepdims=True)
        scale = lax.rsqrt(jnp.mean(center * center, -1, keepdims=True) + FLOOR)
        hn = center * scale
        up = up_ref[rr, :].astype(F32)
        gated = (hn * up).astype(BF16)
        gated_ref[rr, :] = gated
        op_ref[0, rr, :] = dot(gated, wo_ref[:, :HALF]).astype(BF16)
        op_ref[1, rr, :] = dot(gated, wo_ref[:, HALF:]).astype(BF16)
        gg = dot(cg_ref[0, rr, :], wo_ref[:, :HALF], NT) + dot(cg_ref[1, rr, :], wo_ref[:, HALF:], NT)
        dup_ref[rr, :] = gg * hn
        b = gg * up
        grad = (
            scale
            * (b - jnp.mean(b, -1, keepdims=True) - hn * jnp.mean(b * hn, -1, keepdims=True))
        ).astype(BF16)

        def backward(kt, total, causal):
            kr = rows_at(kt * TK, TK)
            k = kv_ref[kr, :E]
            half = dot(k, q, NT) * (0.5 * SCALE)
            ok = spread(idc[kr, :], TQ) == idq_row
            if causal:
                ri = lax.broadcasted_iota(jnp.int32, (TK, TQ), 0)
                ci = lax.broadcasted_iota(jnp.int32, (TK, TQ), 1)
                ok = ok & (ri <= ci)
            half = jnp.where(ok, half, OUT_OF_MASK)
            tan = jnp.tanh(half)
            weights = half + half * tan
            tan = 0.5 * tan
            slope = (0.5 + tan) + weights * (0.5 - tan)
            ds = (slope * dot(kv_ref[kr, E:], grad, NT)).astype(BF16)
            acc[kr, :E] += dot(ds, q)
            acc[kr, E:] += dot(weights.astype(BF16), grad)
            return total + dot(ds, k, TN)

        dq = lax.fori_loop(
            low, last, functools.partial(backward, causal=False), jnp.zeros((TQ, E), F32)
        )
        dq_ref[rr, :] = backward(last, dq, True) * SCALE

    @pl.loop(0, R // TK)
    def _(j):
        rr = rows_at(j * TK, TK)
        own = rows_at(2 * R + j * TK, TK)
        dkv_ref[rr, :E] = acc[own, :E] * SCALE
        dkv_ref[rr, E:] = acc[own, E:]
        for k in range(2):
            src = rows_at(k * R + j * TK, TK)
            dfar_ref[k, rr, :E] = (acc[src, :E] * SCALE).astype(BF16)
            dfar_ref[k, rr, E:] = acc[src, E:].astype(BF16)


def attention(lo, q, kv, up, cg, wo, ids):
    vm = pl.BlockSpec(memory_space=pltpu.VMEM)
    return pl.pallas_call(
        attention_kernel,
        out_shape=(
            jax.ShapeDtypeStruct((2, R, HALF), BF16),
            jax.ShapeDtypeStruct((R, E), BF16),
            jax.ShapeDtypeStruct((R, E), F32),
            jax.ShapeDtypeStruct((R, E), F32),
            jax.ShapeDtypeStruct((R, 2 * E), F32),
            jax.ShapeDtypeStruct((2, R, 2 * E), BF16),
        ),
        in_specs=[pl.BlockSpec(memory_space=pltpu.SMEM)] + [vm] * 6,
        out_specs=(vm,) * 6,
        scratch_shapes=[
            pltpu.VMEM((WIN, E), jnp.int32),
            pltpu.VMEM((WIN, 2 * E), F32),
        ],
        compiler_params=pltpu.CompilerParams(vmem_limit_bytes=56 * 1024 * 1024),
        cost_estimate=pl.CostEstimate(
            flops=7 * 2 * R * R * 2 * E, bytes_accessed=16 << 20, transcendentals=4 * R * R
        ),
        name="attention",
    )(lo, q, kv, up, cg, wo, ids)


SR = 512
NSR = R // SR
SC = 256
NSC = T // SC


def gradient_kernel(
    tok_ref, cot_ref, w_ref, nb_ref, rs_ref, cg_ref, gated_ref, op_ref, dup_ref, dq_ref, dkv_ref, dfar_ref,
    out_ref, gt_ref, gw_ref,
    back, slope, gp, part, chip_sum, to_col, from_col,
    gw, ybuf, yrecv, zacc, zbuf, zrecv, xacc, xbuf, xrecv, all_bf,
    bss, brs, sss, srs, ass, ars,
):
    s, c = place()
    n = lax.axis_size("seq")
    core = lax.rem(s, 2)
    y = lax.rem(lax.div(s, 2), 4)
    z = lax.rem(lax.div(s, 8), 4)
    xl = lax.div(s, 32)
    other = (s + 1 - 2 * core, c)
    far = (s, 1 - c)
    ahead = [(lax.rem(s + 2 * k, n), c) for k in (1, 2)]
    behind = [(lax.rem(s + n - 2 * k, n), c) for k in (1, 2)]
    ys = [lax.rem(y + k, 4) for k in (1, 2, 3)]
    zs = [lax.rem(z + k, 4) for k in (1, 2, 3)]
    yds = [(s + 2 * (v - y), c) for v in ys]
    zds = [(s + 8 * (v - z), c) for v in zs]
    xd = (s + 32 * (1 - 2 * xl), c)
    greet([other, far, xd] + ahead + behind + yds + zds)

    base = core * T
    obase = (1 - core) * T

    def to_core(kind, i):
        src = (op_ref, part)[kind].at[:, rows_at(obase + i * SC, SC)]
        dst = chip_sum.at[kind, :, pl.ds(i * SC, SC)]
        return send(src, dst, sss.at[kind, 0, i], srs.at[kind, 0, i], other)

    def across(kind, i, copy):
        copy.wait_recv()
        src = (op_ref, part)[kind]
        here = pl.ds(i * SC, SC)
        mine = src[1 - c, rows_at(base + i * SC, SC)].astype(F32)
        to_col[kind, here] = (mine + chip_sum[kind, 1 - c, here].astype(F32)).astype(BF16)
        return send(
            to_col.at[kind, here], from_col.at[kind, here], sss.at[kind, 1, i], srs.at[kind, 1, i], far
        )

    def finish(kind, i, copy):
        copy.wait_recv()
        here = pl.ds(i * SC, SC)
        src, own, out = ((op_ref, tok_ref, out_ref), (part, cot_ref, gt_ref))[kind]
        total = src[c, rows_at(base + i * SC, SC)].astype(F32)
        total = total + chip_sum[kind, c, here].astype(F32)
        total = total + from_col[kind, here].astype(F32)
        out[here] = (own[here].astype(F32) + total).astype(BF16)

    done = []
    out_core = [to_core(0, i) for i in range(NSC)]
    returned = []
    for i in range(NSR):
        rr = pl.ds(i * SR, SR)
        for k in (0, 1):
            returned.append(
                send(dfar_ref.at[1 - k, rr], back.at[k, rr], bss.at[k, i], brs.at[k, i], behind[k])
            )
    done += out_core + returned

    @pl.loop(0, R // SR)
    def _(i):
        rr = rows_at(i * SR, SR)
        half = 0.5 * dot(nb_ref[rr, :], w_ref[...])
        tan = jnp.tanh(half)
        silu = half + half * tan
        tan = 0.5 * tan
        sl = (0.5 + tan) + silu * (0.5 - tan)
        gp[rr, :E] = (dup_ref[rr, :] * sl[:, :E]).astype(BF16)
        gp[rr, 2 * E : 3 * E] = (dq_ref[rr, :] * sl[:, 2 * E : 3 * E]).astype(BF16)
        slope[rr, :E] = sl[:, 3 * E :]
        slope[rr, E:] = sl[:, E : 2 * E]

    out_far = [across(0, i, out_core[i]) for i in range(NSC)]
    done += out_far

    gw[D:, :HALF] = dot(gated_ref[...], cg_ref[0], TN)
    gw[D:, HALF:] = dot(gated_ref[...], cg_ref[1], TN)

    for i in range(NSR):
        rr = pl.ds(i * SR, SR)
        for k in (0, 1):
            returned[2 * i + k].wait_recv()
        g = dkv_ref[rr, :] + back[0, rr].astype(F32) + back[1, rr].astype(F32)
        g = (g * slope[rr, :]).astype(BF16)
        gp[rr, 3 * E :] = g[:, :E]
        gp[rr, E : 2 * E] = g[:, E:]

    for j in range(2):
        half = slice(j * HALF, (j + 1) * HALF)
        gw[:D, half] = dot(nb_ref[...], gp[:, half], TN)

    ybuf[...] = gw[...].astype(BF16)
    y_copies = [
        send(ybuf.at[rows_at(ys[k] * YR, YR)], yrecv.at[k], ass.at[0, k], ars.at[0, k], yds[k])
        for k in range(3)
    ]

    def tokens_back(i):
        rr = pl.ds(i * SR, SR)
        g = dot(gp[rr, :], w_ref[...], NT)
        nb = nb_ref[rr, :].astype(F32)
        inv = rs_ref[rr, 0:1]
        g = inv * (g - jnp.mean(g, -1, keepdims=True) - nb * jnp.mean(g * nb, -1, keepdims=True))
        part[0, rr] = g[:, :HALF].astype(BF16)
        part[1, rr] = g[:, HALF:].astype(BF16)

    for i in range(NSR):
        tokens_back(i)
    gt_core = [to_core(1, i) for i in range(NSC)]

    for copy in y_copies:
        copy.wait_recv()
    total = gw[rows_at(y * YR, YR), :]
    for k in range(3):
        total = total + yrecv[k].astype(F32)
    for j in range(4):
        zacc[j] = total[:, j * E : (j + 1) * E]
        zbuf[j] = total[:, j * E : (j + 1) * E].astype(BF16)
    z_copies = [
        send(zbuf.at[zs[k]], zrecv.at[k], ass.at[1, k], ars.at[1, k], zds[k]) for k in range(3)
    ]
    gt_far = [across(1, i, gt_core[i]) for i in range(NSC)]
    for copy in z_copies:
        copy.wait_recv()
    total = zacc[z]
    for k in range(3):
        total = total + zrecv[k].astype(F32)
    xacc[...] = total
    xbuf[...] = total.astype(BF16)
    x_copy = send(
        xbuf.at[rows_at((1 - xl) * XR, XR)], xrecv, ass.at[2, 0], ars.at[2, 0], xd
    )
    x_copy.wait_recv()
    mine = rows_at(xl * XR, XR)
    all_bf[core, y, z, mine] = (xacc[mine, :] + xrecv[...].astype(F32)).astype(BF16)
    done += y_copies + z_copies + [x_copy]

    spot = all_bf.at[core, y, z, mine]
    g_copy = send(spot, spot, ass.at[3, 0], ars.at[3, 0], xd)
    g_copy.wait_recv()
    spot = all_bf.at[core, y, z]
    gz = [send(spot, spot, ass.at[4, k], ars.at[4, k], zds[k]) for k in range(3)]
    for copy in gz:
        copy.wait_recv()
    spot = all_bf.at[core, y]
    gy = [send(spot, spot, ass.at[5, k], ars.at[5, k], yds[k]) for k in range(3)]
    gc = [send(spot, spot, ass.at[6, 0], ars.at[6, 0], other)]
    for k in range(3):
        gy[k].wait_recv()
        spot = all_bf.at[core, lax.rem(y + 3 - k, 4)]
        gc.append(send(spot, spot, ass.at[6, k + 1], ars.at[6, k + 1], other))
    done += [g_copy] + gz + gy + gc

    for i in range(NSC):
        finish(0, i, out_far[i])
    for i in range(NSC):
        finish(1, i, gt_far[i])
    done += gt_core + gt_far
    for copy in gc:
        copy.wait_recv()
    for h in range(2):
        for v in range(4):
            for j in range(4):
                gw_ref[h, v * YR : (v + 1) * YR, j * E : (j + 1) * E] = (
                    all_bf[h, v, j].astype(F32) * (1.0 / 256.0)
                )
    for copy in done:
        copy.wait_send()


def gradients(*operands):
    vm = pl.BlockSpec(memory_space=pltpu.VMEM)
    dma = pltpu.SemaphoreType.DMA
    return pl.pallas_call(
        gradient_kernel,
        out_shape=(
            jax.ShapeDtypeStruct((T, HALF), BF16),
            jax.ShapeDtypeStruct((T, HALF), BF16),
            jax.ShapeDtypeStruct((2, GR, D), F32),
        ),
        in_specs=[vm] * 12,
        out_specs=(vm,) * 3,
        scratch_shapes=[
            pltpu.VMEM((2, R, 2 * E), BF16),
            pltpu.VMEM((R, 2 * E), F32),
            pltpu.VMEM((R, 4 * E), BF16),
            pltpu.VMEM((2, R, HALF), BF16),
            pltpu.VMEM((2, 2, T, HALF), BF16),
            pltpu.VMEM((2, T, HALF), BF16),
            pltpu.VMEM((2, T, HALF), BF16),
            pltpu.VMEM((GR, D), F32),
            pltpu.VMEM((GR, D), BF16),
            pltpu.VMEM((3, YR, D), BF16),
            pltpu.VMEM((4, YR, E), F32),
            pltpu.VMEM((4, YR, E), BF16),
            pltpu.VMEM((3, YR, E), BF16),
            pltpu.VMEM((YR, E), F32),
            pltpu.VMEM((YR, E), BF16),
            pltpu.VMEM((XR, E), BF16),
            pltpu.VMEM((2, 4, 4, YR, E), BF16),
            dma((2, NSR)),
            dma((2, NSR)),
            dma((2, 2, NSC)),
            dma((2, 2, NSC)),
            dma((7, 4)),
            dma((7, 4)),
        ],
        compiler_params=pltpu.CompilerParams(
            collective_id=1, has_side_effects=True, vmem_limit_bytes=56 * 1024 * 1024
        ),
        cost_estimate=pl.CostEstimate(
            flops=7 * R * D * D, bytes_accessed=16 << 20, transcendentals=R * D
        ),
        name="gradients",
    )(*operands)


def shards(tokens, cotangent, weight_in, weight_out, history_ids):
    s = lax.axis_index("seq")
    core = s % 2
    chip = s // 2
    w = lax.dynamic_index_in_dim(weight_in, core, 2, keepdims=False).reshape(D, 4 * E)
    wo = lax.dynamic_index_in_dim(weight_out, core, 0, keepdims=False)
    padded = jnp.concatenate([jnp.full((2 * R,), -1, jnp.int32), history_ids])
    ids = lax.dynamic_slice_in_dim(padded, chip * R, WIN)
    firsts = lax.slice_in_dim(ids, 2 * R, WIN, TQ)
    lo = jnp.sum((ids[None, :] < firsts[:, None]).astype(jnp.int32), axis=1) // TK

    nb, inv, q, up, kv, cg = project(tokens, cotangent, w)
    op, gated, dup, dq, dkv, dfar = attention(
        lo, q, kv.reshape(WIN, 2 * E), up, cg, wo, ids.reshape(1, WIN)
    )
    out, gt, gw = gradients(
        tokens, cotangent, w, nb, inv, cg, gated, op, dup, dq, dkv, dfar
    )
    gwi = gw[:, :D].reshape(2, D, 4, E).transpose(1, 2, 0, 3)
    return out, gt, gwi, gw[:, D:]


def solution(mesh):
    placed = (
        P("seq", "col"),
        P("seq", "col"),
        P(None, None, "col", None),
        P("col", None, None),
        P(),
    )
    return jax.shard_map(
        shards,
        mesh=mesh,
        in_specs=placed,
        out_specs=(
            P("seq", "col"),
            P("seq", "col"),
            P(None, None, "col", None),
            P("col", None, None),
        ),
        check_vma=False,
    )
```

```python
import functools
import math

import jax
import jax.numpy as jnp
from jax import lax
from jax.experimental import pallas as pl
from jax.experimental.pallas import tpu as pltpu
from jax.sharding import PartitionSpec as P

MESH = pl.DeviceIdType.MESH
F32 = jnp.float32
BF16 = jnp.bfloat16

T = 1024
R = 2 * T
D = 512
E = 128
HALF = D // 2
CH = 256
NCH = T // CH
TQ = 512
TK = 512
WIN = 3 * R
EPS = 1e-5
FLOOR = 1.0
SCALE = E**-0.5
OUT_OF_MASK = -32.0
SLOTS = R // CH
AROUND = (0, 1, 2, 4, 6)
CHIPS = 32
VMEM_LIMIT = 56 * 1024 * 1024

NT = (((1,), (1,)), ((), ()))
TN = (((0,), (0,)), ((), ()))


def dot(a, b, dims=(((1,), (0,)), ((), ()))):
    return lax.dot_general(a, b, dims, preferred_element_type=F32)


def guarded(on, act):
    if on is None:
        act()
    else:
        pl.when(on)(act)


class Copy:
    def __init__(self, src, dst, sems, at, device, on=None, arrives=None):
        self.on, self.arrives = on, arrives
        self.copy = pltpu.make_async_remote_copy(
            src_ref=src,
            dst_ref=dst,
            send_sem=sems[0].at[at],
            recv_sem=sems[1].at[at],
            device_id=device,
            device_id_type=MESH,
        )

    def start(self):
        guarded(self.on, self.copy.start)
        return self

    def wait_recv(self):
        guarded(self.arrives, self.copy.wait_recv)

    def wait_send(self):
        guarded(self.on, self.copy.wait_send)


def rows_at(start, size):
    return pl.ds(pl.multiple_of(start, size), size)


class Place:
    def __init__(self):
        s, c = lax.axis_index("seq"), lax.axis_index("col")
        self.s, self.c = s, c
        self.core = lax.rem(s, 2)
        self.chip = lax.div(s, 2)
        self.y = lax.rem(self.chip, 4)
        self.z = lax.rem(lax.div(s, 8), 4)
        self.xl = lax.div(s, 32)
        self.other = (s + 1 - 2 * self.core, c)
        aside = s + 32 - 64 * self.xl
        same = self.xl == 0
        self.xplus = (aside, jnp.where(same, c, 1 - c))
        self.xminus = (aside, jnp.where(same, 1 - c, c))
        self.xpeer = (aside, c)

    def at_chip(self, chip):
        return (2 * lax.rem(chip + 2 * CHIPS, CHIPS) + self.core, self.c)

    def in_ring(self, step):
        return self.chip - self.y + lax.rem(self.y + 4 + step, 4)


def greet(senders, count):
    barrier = pltpu.get_barrier_semaphore()
    for device in senders:
        pl.semaphore_signal(barrier, inc=1, device_id=device, device_id_type=MESH)
    pl.semaphore_wait(barrier, count)


class Across:
    def __init__(self, me, src, via, dst, sems, at, turn):
        first = me.xplus if turn % 2 == 0 else me.xminus
        self.leg = Copy(src, via, sems, at + (0,), first)
        self.next = Copy(via, dst(first[1]), sems, at + (1,), first)

    def start(self):
        self.leg.start()
        return self

    def hand_on(self):
        self.leg.wait_recv()
        self.next.start()

    def wait_recv(self):
        self.next.wait_recv()

    def wait_send(self):
        self.leg.wait_send()
        self.next.wait_send()


def project_kernel(
    tok_ref, cot_ref, w_ref,
    wh_ref, nb_ref, rs_ref, q_ref, up_ref, kv_ref, cg_ref,
    xg, xvia, yvia, wf, xss, xrs, oss, ors, kss, krs,
):
    me = Place()
    c, core, chip = me.c, me.core, me.chip
    ahead = me.at_chip(chip + 1)
    round_to = me.at_chip(me.in_ring(-1))
    source = me.in_ring(1)
    handed_to = me.at_chip(source + 2)
    two_back = lax.rem(chip + CHIPS - 2, CHIPS)
    two_y = lax.rem(two_back, 4)
    hander = me.at_chip(two_back - two_y + lax.rem(two_y + 3, 4))
    greet(
        [me.other, me.xplus, me.xminus, me.at_chip(chip - 1), me.at_chip(source), hander],
        6,
    )

    base = core * T
    obase = (1 - core) * T

    bufs = (xg, cg_ref)
    srcs = (tok_ref, cot_ref)
    x_copies, o_copies, f_copies = {}, {}, {}
    for kind in (0, 1):
        for i in range(NCH):
            rr = rows_at(base + i * CH, CH)
            x_copies[kind, i] = Across(
                me, srcs[kind].at[pl.ds(i * CH, CH)], xvia.at[kind, i],
                lambda col, kind=kind, rr=rr: bufs[kind].at[1 - col, rr],
                (xss, xrs), (kind, i), i,
            )
            o_copies[kind, i] = Copy(
                srcs[kind].at[pl.ds(i * CH, CH)], bufs[kind].at[c, rr], (oss, ors), (kind, 0, i), me.other
            )
            where = bufs[kind].at[1 - c, rr]
            f_copies[kind, i] = Copy(where, where, (oss, ors), (kind, 1, i), me.other)

    for i in range(NCH):
        x_copies[0, i].start()
        o_copies[0, i].start()
    for i in range(NCH):
        xg[c, rows_at(base + i * CH, CH)] = tok_ref[pl.ds(i * CH, CH)]
        cg_ref[c, rows_at(base + i * CH, CH)] = cot_ref[pl.ds(i * CH, CH)]

    wf[...] = w_ref[...].astype(F32)
    for place, part in enumerate((0, 2, 1, 3)):
        lanes = slice(place * E, (place + 1) * E)
        first = wf[pl.ds(2 * part, D, stride=8), :]
        second = wf[pl.ds(2 * part + 1, D, stride=8), :]
        wh_ref[:, lanes] = jnp.where(core == 0, first, second).astype(BF16)

    near, hop, direct, chained = {}, {}, {}, {}
    for slot in range(SLOTS):
        rr = rows_at((base if slot < NCH else obase) + slot % NCH * CH, CH)
        mine = kv_ref.at[2, rr]
        near[slot] = Copy(
            mine, kv_ref.at[1, rr], (kss, krs), (0, slot), ahead, chip < CHIPS - 1, chip > 0
        )
        if slot in AROUND:
            hop[slot] = Copy(
                mine, yvia.at[slot], (kss, krs), (1, slot), round_to,
                chip < CHIPS - 2, source < CHIPS - 2,
            )
            direct[slot] = Copy(
                yvia.at[slot], kv_ref.at[0, rr], (kss, krs), (2, slot), handed_to,
                source < CHIPS - 2, chip > 1,
            )
        else:
            chained[slot] = Copy(
                kv_ref.at[1, rr], kv_ref.at[0, rr], (kss, krs), (2, slot), ahead,
                (chip > 0) & (chip < CHIPS - 1), chip > 1,
            )

    def compute(slot):
        rr = rows_at((base if slot < NCH else obase) + slot % NCH * CH, CH)
        x0 = xg[0, rr].astype(F32)
        x1 = xg[1, rr].astype(F32)
        mean = (jnp.sum(x0, -1, keepdims=True) + jnp.sum(x1, -1, keepdims=True)) * (1.0 / D)
        x0 = x0 - mean
        x1 = x1 - mean
        var = (
            jnp.sum(x0 * x0, -1, keepdims=True) + jnp.sum(x1 * x1, -1, keepdims=True)
        ) * (1.0 / D)
        inv = lax.rsqrt(var + EPS)
        n0 = (x0 * inv).astype(BF16)
        n1 = (x1 * inv).astype(BF16)
        nb_ref[rr, :HALF] = n0
        nb_ref[rr, HALF:] = n1
        rs_ref[rr] = jnp.broadcast_to(inv, (CH, E))
        half = 0.5 * (dot(n0, wh_ref[:HALF]) + dot(n1, wh_ref[HALF:]))
        proj = (half + half * jnp.tanh(half)).astype(BF16)
        up_ref[rr] = proj[:, :E]
        q_ref[rr] = proj[:, E : 2 * E]
        kv_ref[2, rr] = proj[:, 2 * E :]
        near[slot].start()
        if slot in AROUND:
            hop[slot].start()

    def hand_on(slot):
        if slot in AROUND:
            hop[slot].wait_recv()
            direct[slot].start()
        else:
            near[slot].wait_recv()
            chained[slot].start()

    x_copies[0, 0].hand_on()
    for i in range(NCH):
        if i < NCH - 1:
            x_copies[0, i + 1].hand_on()
        x_copies[0, i].wait_recv()
        f_copies[0, i].start()
        compute(i)
        o_copies[0, i].wait_recv()
        f_copies[0, i].wait_recv()
        compute(NCH + i)
        if i == 1:
            for j in range(NCH):
                x_copies[1, j].start()
                o_copies[1, j].start()
        if i:
            hand_on(i - 1)
            hand_on(NCH + i - 1)
    for i in range(NCH):
        x_copies[1, i].hand_on()
    hand_on(NCH - 1)
    hand_on(SLOTS - 1)
    for i in range(NCH):
        x_copies[1, i].wait_recv()
        f_copies[1, i].start()
    for i in range(NCH):
        o_copies[1, i].wait_recv()
        f_copies[1, i].wait_recv()
    for slot in range(SLOTS):
        if slot in AROUND:
            near[slot].wait_recv()
            direct[slot].wait_recv()
        else:
            chained[slot].wait_recv()
    for copies in (x_copies, o_copies, f_copies, near, hop, direct, chained):
        for copy in copies.values():
            copy.wait_send()


def project(tokens, cotangent, w):
    vm = pl.BlockSpec(memory_space=pltpu.VMEM)
    dma = pltpu.SemaphoreType.DMA
    return pl.pallas_call(
        project_kernel,
        out_shape=(
            jax.ShapeDtypeStruct((D, 4 * E), BF16),
            jax.ShapeDtypeStruct((R, D), BF16),
            jax.ShapeDtypeStruct((R, E), F32),
            jax.ShapeDtypeStruct((R, E), BF16),
            jax.ShapeDtypeStruct((R, E), BF16),
            jax.ShapeDtypeStruct((3, R, 2 * E), BF16),
            jax.ShapeDtypeStruct((2, R, HALF), BF16),
        ),
        in_specs=[vm] * 3,
        out_specs=(vm,) * 7,
        scratch_shapes=[
            pltpu.VMEM((2, R, HALF), BF16),
            pltpu.VMEM((2, NCH, CH, HALF), BF16),
            pltpu.VMEM((SLOTS, CH, 2 * E), BF16),
            pltpu.VMEM((8 * D, E), F32),
            dma((2, NCH, 2)),
            dma((2, NCH, 2)),
            dma((2, 2, NCH)),
            dma((2, 2, NCH)),
            dma((3, SLOTS)),
            dma((3, SLOTS)),
        ],
        compiler_params=pltpu.CompilerParams(
            collective_id=0, has_side_effects=True, vmem_limit_bytes=VMEM_LIMIT
        ),
        cost_estimate=pl.CostEstimate(
            flops=2 * R * D * D, bytes_accessed=16 << 20, transcendentals=R * D
        ),
        name="gather_project",
    )(tokens, cotangent, w)


def attention_kernel(
    q_ref, kv_ref, up_ref, cg_ref, wo_all, all_ids,
    op_ref, gated_ref, dup_ref, dq_ref, dkv_ref, dfar_ref,
    id_ref, idc, acc,
):
    s = lax.axis_index("seq")
    chip = lax.div(s, 2)
    wo_ref = wo_all.at[lax.rem(s, 2)]
    windows = []
    for b in range(3):
        source = chip - 2 + b
        ids = all_ids[rows_at(jnp.maximum(source, 0) * (R // E), R // E), :]
        ids = jnp.where(source >= 0, ids, -1)
        windows.append(ids)
        for j in range(R // E):
            at = b * R + j * E
            row = ids[j : j + 1, :]
            id_ref[0:1, at : at + E] = row
            idc[at : at + E, :] = jnp.broadcast_to(row, (E, E)).T

    @pl.loop(0, WIN // TK)
    def _(j):
        acc[rows_at(j * TK, TK), :] = jnp.zeros((TK, 2 * E), F32)

    def spread(column, width):
        return jnp.concatenate([column] * (width // E), axis=1)

    first = 2 * R // TK

    @pl.loop(0, R // TQ)
    def _(t):
        rr = rows_at(t * TQ, TQ)
        q = q_ref[rr, :]
        wr = rows_at(2 * R + t * TQ, TQ)
        idq_col = idc[wr, :]
        idq_row = id_ref[0:1, wr]
        start = idq_row[0, 0]
        low = sum(jnp.sum((ids < start).astype(jnp.int32)) for ids in windows) // TK
        last = first + t * TQ // TK

        def forward(kt, total, causal):
            kr = rows_at(kt * TK, TK)
            half = dot(q, kv_ref[kr, E:], NT) * (0.5 * SCALE)
            ok = spread(idq_col, TK) == id_ref[0:1, kr]
            if causal:
                ri = lax.broadcasted_iota(jnp.int32, (TQ, TK), 0)
                ci = lax.broadcasted_iota(jnp.int32, (TQ, TK), 1)
                ok = ok & (ci <= ri)
            half = jnp.where(ok, half, OUT_OF_MASK)
            weights = (half + half * jnp.tanh(half)).astype(BF16)
            return total + dot(weights, kv_ref[kr, :E])

        att = lax.fori_loop(
            low, last, functools.partial(forward, causal=False), jnp.zeros((TQ, E), F32)
        )
        att = forward(last, att, True)

        center = att - jnp.mean(att, -1, keepdims=True)
        scale = lax.rsqrt(jnp.mean(center * center, -1, keepdims=True) + FLOOR)
        hn = center * scale
        up = up_ref[rr, :].astype(F32)
        gated = (hn * up).astype(BF16)
        gated_ref[rr, :] = gated
        op_ref[0, rr, :] = dot(gated, wo_ref[:, :HALF]).astype(BF16)
        op_ref[1, rr, :] = dot(gated, wo_ref[:, HALF:]).astype(BF16)
        gg = dot(cg_ref[0, rr, :], wo_ref[:, :HALF], NT) + dot(cg_ref[1, rr, :], wo_ref[:, HALF:], NT)
        dup_ref[rr, :] = gg * hn
        b = gg * up
        grad = (
            scale
            * (b - jnp.mean(b, -1, keepdims=True) - hn * jnp.mean(b * hn, -1, keepdims=True))
        ).astype(BF16)

        def backward(kt, total, causal):
            kr = rows_at(kt * TK, TK)
            k = kv_ref[kr, E:]
            half = dot(k, q, NT) * (0.5 * SCALE)
            ok = spread(idc[kr, :], TQ) == idq_row
            if causal:
                ri = lax.broadcasted_iota(jnp.int32, (TK, TQ), 0)
                ci = lax.broadcasted_iota(jnp.int32, (TK, TQ), 1)
                ok = ok & (ri <= ci)
            half = jnp.where(ok, half, OUT_OF_MASK)
            tan = jnp.tanh(half)
            weights = half + half * tan
            tan = 0.5 * tan
            slope = (0.5 + tan) + weights * (0.5 - tan)
            ds = (slope * dot(kv_ref[kr, :E], grad, NT)).astype(BF16)
            acc[kr, E:] += dot(ds, q)
            acc[kr, :E] += dot(weights.astype(BF16), grad)
            return total + dot(ds, k, TN)

        dq = lax.fori_loop(
            low, last, functools.partial(backward, causal=False), jnp.zeros((TQ, E), F32)
        )
        dq_ref[rr, :] = backward(last, dq, True) * SCALE

    @pl.loop(0, R // TK)
    def _(j):
        rr = rows_at(j * TK, TK)
        own = rows_at(2 * R + j * TK, TK)
        dkv_ref[rr, :E] = acc[own, :E]
        dkv_ref[rr, E:] = acc[own, E:] * SCALE
        for k in range(2):
            src = rows_at(k * R + j * TK, TK)
            dfar_ref[k, rr, :E] = acc[src, :E].astype(BF16)
            dfar_ref[k, rr, E:] = (acc[src, E:] * SCALE).astype(BF16)


def attention(q, kv, up, cg, wo, ids):
    vm = pl.BlockSpec(memory_space=pltpu.VMEM)
    return pl.pallas_call(
        attention_kernel,
        out_shape=(
            jax.ShapeDtypeStruct((2, R, HALF), BF16),
            jax.ShapeDtypeStruct((R, E), BF16),
            jax.ShapeDtypeStruct((R, E), F32),
            jax.ShapeDtypeStruct((R, E), F32),
            jax.ShapeDtypeStruct((R, 2 * E), F32),
            jax.ShapeDtypeStruct((2, R, 2 * E), BF16),
        ),
        in_specs=[vm] * 6,
        out_specs=(vm,) * 6,
        scratch_shapes=[
            pltpu.VMEM((1, WIN), jnp.int32),
            pltpu.VMEM((WIN, E), jnp.int32),
            pltpu.VMEM((WIN, 2 * E), F32),
        ],
        compiler_params=pltpu.CompilerParams(vmem_limit_bytes=VMEM_LIMIT),
        cost_estimate=pl.CostEstimate(
            flops=7 * 2 * R * R * 2 * E, bytes_accessed=16 << 20, transcendentals=4 * R * R
        ),
        name="attention",
    )(q, kv, up, cg, wo, ids)


class Summed:
    def __init__(self, me, rows, grads, bufs, sems, at):
        self.me, self.rows, self.grads, self.bufs = me, rows, grads, bufs
        self.sems, self.at = sems, at
        self.done = []

    def copy(self, src, dst, stage, k, device):
        copy = Copy(src, dst, self.sems, (self.at, stage, k), device).start()
        self.done.append(copy)
        return copy

    def peers(self, here, step):
        s, c = self.me.s, self.me.c
        there = [lax.rem(here + k, 4) for k in (1, 2, 3)]
        return [(v, (s + step * (v - here), c)) for v in there]

    def start(self):
        zbuf, zrecv = self.bufs[0:2]
        n = self.rows // 4
        zbuf[...] = self.grads[...].astype(BF16)
        self.zc = [
            self.copy(zbuf.at[rows_at(v * n, n)], zrecv.at[k], 0, k, device)
            for k, (v, device) in enumerate(self.peers(self.me.z, 8))
        ]

    def over_y(self):
        zrecv, yacc, ybuf, yrecv = self.bufs[1:5]
        n, m = self.rows // 4, self.rows // 16
        for copy in self.zc:
            copy.wait_recv()
        total = self.grads[rows_at(self.me.z * n, n), :]
        for k in range(3):
            total = total + zrecv[k].astype(F32)
        yacc[...] = total
        ybuf[...] = total.astype(BF16)
        self.yc = [
            self.copy(ybuf.at[rows_at(v * m, m)], yrecv.at[k], 1, k, device)
            for k, (v, device) in enumerate(self.peers(self.me.y, 2))
        ]

    def over_x(self):
        yacc, _, yrecv, xacc, xbuf, xrecv = self.bufs[2:8]
        m = self.rows // 16
        for copy in self.yc:
            copy.wait_recv()
        total = yacc[rows_at(self.me.y * m, m), :]
        for k in range(3):
            total = total + yrecv[k].astype(F32)
        for j in range(2):
            xacc[j] = total[:, j * E : (j + 1) * E]
            xbuf[j] = total[:, j * E : (j + 1) * E].astype(BF16)
        self.xc = self.copy(xbuf.at[1 - self.me.xl], xrecv, 2, 0, self.me.xpeer)

    def back_x(self):
        xacc, _, xrecv, whole = self.bufs[5:9]
        me = self.me
        self.xc.wait_recv()
        spot = whole.at[me.core, me.z, me.y, me.xl]
        spot[...] = (xacc[me.xl] + xrecv[...].astype(F32)).astype(BF16)
        self.gx = self.copy(spot, spot, 3, 0, me.xpeer)

    def back_y(self):
        me = self.me
        self.gx.wait_recv()
        spot = self.bufs[8].at[me.core, me.z, me.y]
        self.gy = [
            self.copy(spot, spot, 4, k, device) for k, (_, device) in enumerate(self.peers(me.y, 2))
        ]

    def back_z(self):
        me = self.me
        for copy in self.gy:
            copy.wait_recv()
        spot = self.bufs[8].at[me.core, me.z]
        self.gz = [
            self.copy(spot, spot, 5, k, device) for k, (_, device) in enumerate(self.peers(me.z, 8))
        ]
        self.gc = [self.copy(spot, spot, 6, 0, me.other)]

    def back_core(self):
        me = self.me
        for k in range(3):
            self.gz[k].wait_recv()
            spot = self.bufs[8].at[me.core, lax.rem(me.z + 3 - k, 4)]
            self.gc.append(self.copy(spot, spot, 6, k + 1, me.other))

    def finish(self):
        for copy in self.gc:
            copy.wait_recv()

    def wait_send(self):
        for copy in self.done:
            copy.wait_send()

    @staticmethod
    def scratch(rows):
        n, m = rows // 4, rows // 16
        return [
            pltpu.VMEM((rows, 2 * E), BF16),
            pltpu.VMEM((3, n, 2 * E), BF16),
            pltpu.VMEM((n, 2 * E), F32),
            pltpu.VMEM((n, 2 * E), BF16),
            pltpu.VMEM((3, m, 2 * E), BF16),
            pltpu.VMEM((2, m, E), F32),
            pltpu.VMEM((2, m, E), BF16),
            pltpu.VMEM((m, E), BF16),
            pltpu.VMEM((2, 4, 4, 2, m, E), BF16),
        ]


EARLY = D + 2 * E
INV_ROOT = 1.0 / 256.0


def gradient_kernel(
    tok_ref, cot_ref, w_ref, nb_ref, rs_ref, cg_ref, gated_ref, op_ref, dup_ref, dq_ref, dkv_ref, dfar_ref,
    out_ref, gt_ref, gwi_ref, gwo_ref,
    hopped, back, yvia, slope, gp, part, chip_sum, to_col, xvia, from_col, early_g, late_g, *rest,
):
    early_bufs, late_bufs = rest[:9], rest[9:18]
    bss, brs, sss, srs, xss, xrs, ass, ars = rest[18:]
    me = Place()
    c, core, chip = me.c, me.core, me.chip
    behind = me.at_chip(chip - 1)
    round_to = me.at_chip(me.in_ring(1))
    source = me.in_ring(-1)
    handed_to = me.at_chip(source - 2)
    two_on = lax.rem(chip + 2, CHIPS)
    two_y = lax.rem(two_on, 4)
    hander = me.at_chip(two_on - two_y + lax.rem(two_y + 1, 4))
    early = Summed(me, EARLY, early_g, early_bufs, (ass, ars), 0)
    late = Summed(me, D, late_g, late_bufs, (ass, ars), 1)
    greet(
        [me.other, me.xplus, me.xminus, me.at_chip(chip + 1), me.at_chip(source), hander, me.xpeer]
        + [device for _, device in early.peers(me.y, 2) + early.peers(me.z, 8)],
        13,
    )

    base = core * T
    obase = (1 - core) * T

    def to_core(kind, i):
        src = (op_ref, part)[kind].at[:, rows_at(obase + i * CH, CH)]
        dst = chip_sum.at[kind, :, pl.ds(i * CH, CH)]
        return Copy(src, dst, (sss, srs), (kind, i), me.other).start()

    def across(kind, i, copy):
        copy.wait_recv()
        src = (op_ref, part)[kind]
        here = pl.ds(i * CH, CH)
        mine = src[1 - c, rows_at(base + i * CH, CH)].astype(F32)
        to_col[kind, here] = (mine + chip_sum[kind, 1 - c, here].astype(F32)).astype(BF16)
        return Across(
            me, to_col.at[kind, here], xvia.at[kind, i], lambda col: from_col.at[kind, here],
            (xss, xrs), (kind, i), i,
        ).start()

    def finish(kind, i, copy):
        copy.wait_recv()
        here = pl.ds(i * CH, CH)
        src, own, out = ((op_ref, tok_ref, out_ref), (part, cot_ref, gt_ref))[kind]
        total = src[c, rows_at(base + i * CH, CH)].astype(F32)
        total = total + chip_sum[kind, c, here].astype(F32)
        total = total + from_col[kind, here].astype(F32)
        out[here] = (own[here].astype(F32) + total).astype(BF16)

    near, hop, direct = {}, {}, {}
    for i in range(SLOTS):
        rr = pl.ds(i * CH, CH)
        near[i] = Copy(
            dfar_ref.at[1, rr] if i in AROUND else back.at[2, rr], back.at[1, rr], (bss, brs), (0, i), behind,
            chip > 0, chip < CHIPS - 1,
        )
        if i in AROUND:
            hop[i] = Copy(
                dfar_ref.at[0, rr], yvia.at[i], (bss, brs), (1, i), round_to, chip > 1, source > 1
            )
            direct[i] = Copy(
                yvia.at[i], back.at[0, rr], (bss, brs), (2, i), handed_to, source > 1, chip < CHIPS - 2
            )
        else:
            hop[i] = Copy(
                dfar_ref.at[0, rr], hopped.at[i], (bss, brs), (1, i), behind,
                chip > 1, (chip > 0) & (chip < CHIPS - 1),
            )
        hop[i].start()
        if i in AROUND:
            near[i].start()
    out_core = [to_core(0, i) for i in range(NCH)]

    SR = 512

    @pl.loop(0, R // SR)
    def _(i):
        rr = rows_at(i * SR, SR)
        half = 0.5 * dot(nb_ref[rr, :], w_ref[...])
        tan = jnp.tanh(half)
        silu = half + half * tan
        tan = 0.5 * tan
        sl = (0.5 + tan) + silu * (0.5 - tan)
        gp[rr, :E] = (dup_ref[rr, :] * sl[:, :E]).astype(BF16)
        gp[rr, E : 2 * E] = (dq_ref[rr, :] * sl[:, E : 2 * E]).astype(BF16)
        slope[rr, :] = sl[:, 2 * E :]

    early_g[:D, :] = dot(nb_ref[...], gp[:, : 2 * E], TN)
    for j in range(2):
        early_g[D + j * E : D + (j + 1) * E, :] = dot(gated_ref[...], cg_ref[j], TN)
    early.start()

    out_far = [across(0, i, out_core[i]) for i in range(NCH)]

    for i in range(SLOTS):
        rr = pl.ds(i * CH, CH)
        if i in AROUND:
            hop[i].wait_recv()
            direct[i].start()
        else:
            back[2, rr] = dfar_ref[1, rr]

            @pl.when((chip > 0) & (chip < CHIPS - 1))
            def _():
                hop[i].copy.wait_recv()
                back[2, rr] = (dfar_ref[1, rr].astype(F32) + hopped[i].astype(F32)).astype(BF16)

            near[i].start()
    for copy in out_far:
        copy.hand_on()
    early.over_y()

    for i in range(SLOTS):
        rr = pl.ds(i * CH, CH)
        near[i].wait_recv()

        @pl.when(chip == CHIPS - 1)
        def _():
            back[1, rr] = jnp.zeros((CH, 2 * E), BF16)

        g = dkv_ref[rr, :]
        if i in AROUND:
            direct[i].wait_recv()

            @pl.when(chip >= CHIPS - 2)
            def _():
                back[0, rr] = jnp.zeros((CH, 2 * E), BF16)

            g = g + back[0, rr].astype(F32)
        gp[rr, 2 * E :] = ((g + back[1, rr].astype(F32)) * slope[rr, :]).astype(BF16)

    late_g[...] = dot(nb_ref[...], gp[:, 2 * E :], TN)
    late.start()
    early.over_x()

    def tokens_back(start):
        rr = rows_at(start, CH)
        g = dot(gp[rr, :], w_ref[...], NT)
        nb = nb_ref[rr, :].astype(F32)
        inv = rs_ref[rr, 0:1]
        g = inv * (g - jnp.mean(g, -1, keepdims=True) - nb * jnp.mean(g * nb, -1, keepdims=True))
        part[0, rr] = g[:, :HALF].astype(BF16)
        part[1, rr] = g[:, HALF:].astype(BF16)

    gt_core = []
    for i in range(NCH):
        tokens_back(obase + i * CH)
        gt_core.append(to_core(1, i))
    early.back_x()
    gt_far = []
    for i in range(NCH):
        tokens_back(base + i * CH)
        gt_far.append(across(1, i, gt_core[i]))
    late.over_y()
    early.back_y()
    for copy in gt_far[:2]:
        copy.hand_on()
    late.over_x()
    early.back_z()
    for copy in gt_far[2:]:
        copy.hand_on()
    late.back_x()
    late.back_y()
    early.back_core()
    late.back_z()
    for i in range(NCH):
        finish(0, i, out_far[i])
    early.finish()
    for h in range(2):
        for z in range(4):
            for y in range(4):
                for j in range(2):
                    n = EARLY // 16
                    row = (4 * z + y) * n
                    block = early_bufs[8][h, z, y, j].astype(F32) * INV_ROOT
                    at = 0
                    while at < n:
                        d = row + at
                        end = next(b for b in (D, D + E, EARLY) if b > d)
                        size = min(n - at, end - d)
                        piece = block[at : at + size]
                        if d < D:
                            gwi_ref[pl.ds(8 * d + 4 * j + h, size, stride=8), :] = piece
                        else:
                            q, e = divmod(d - D, E)
                            gwo_ref[h, e : e + size, q * HALF + j * E : q * HALF + (j + 1) * E] = piece
                        at += size
    late.back_core()
    for i in range(NCH):
        finish(1, i, gt_far[i])
    late.finish()
    for h in range(2):
        for z in range(4):
            for y in range(4):
                for j in range(2):
                    n = D // 16
                    row = (4 * z + y) * n
                    gwi_ref[pl.ds(8 * row + 4 * j + 2 + h, n, stride=8), :] = (
                        late_bufs[8][h, z, y, j].astype(F32) * INV_ROOT
                    )
    for copies in (near, hop, direct):
        for copy in copies.values():
            copy.wait_send()
    for copy in out_core + out_far + gt_core + gt_far + [early, late]:
        copy.wait_send()


def gradients(*operands):
    vm = pl.BlockSpec(memory_space=pltpu.VMEM)
    dma = pltpu.SemaphoreType.DMA
    return pl.pallas_call(
        gradient_kernel,
        out_shape=(
            jax.ShapeDtypeStruct((T, HALF), BF16),
            jax.ShapeDtypeStruct((T, HALF), BF16),
            jax.ShapeDtypeStruct((8 * D, E), F32),
            jax.ShapeDtypeStruct((2, E, D), F32),
        ),
        in_specs=[vm] * 12,
        out_specs=(vm,) * 4,
        scratch_shapes=[
            pltpu.VMEM((SLOTS, CH, 2 * E), BF16),
            pltpu.VMEM((3, R, 2 * E), BF16),
            pltpu.VMEM((SLOTS, CH, 2 * E), BF16),
            pltpu.VMEM((R, 2 * E), F32),
            pltpu.VMEM((R, 4 * E), BF16),
            pltpu.VMEM((2, R, HALF), BF16),
            pltpu.VMEM((2, 2, T, HALF), BF16),
            pltpu.VMEM((2, T, HALF), BF16),
            pltpu.VMEM((2, NCH, CH, HALF), BF16),
            pltpu.VMEM((2, T, HALF), BF16),
            pltpu.VMEM((EARLY, 2 * E), F32),
            pltpu.VMEM((D, 2 * E), F32),
        ]
        + Summed.scratch(EARLY)
        + Summed.scratch(D)
        + [
            dma((3, SLOTS)),
            dma((3, SLOTS)),
            dma((2, NCH)),
            dma((2, NCH)),
            dma((2, NCH, 2)),
            dma((2, NCH, 2)),
            dma((2, 7, 4)),
            dma((2, 7, 4)),
        ],
        compiler_params=pltpu.CompilerParams(
            collective_id=1, has_side_effects=True, vmem_limit_bytes=VMEM_LIMIT
        ),
        cost_estimate=pl.CostEstimate(
            flops=7 * R * D * D, bytes_accessed=16 << 20, transcendentals=R * D
        ),
        name="gradients",
    )(*operands)


def shards(tokens, cotangent, weight_in, weight_out, history_ids):
    w, nb, inv, q, up, kv, cg = project(tokens, cotangent, weight_in.reshape(8 * D, E))
    op, gated, dup, dq, dkv, dfar = attention(
        q, kv.reshape(WIN, 2 * E), up, cg, weight_out, history_ids.reshape(-1, E)
    )
    out, gt, gwi, gwo = gradients(
        tokens, cotangent, w, nb, inv, cg, gated, op, dup, dq, dkv, dfar
    )
    return out, gt, gwi.reshape(D, 4, 2, E), gwo


def solution(mesh):
    placed = (
        P("seq", "col"),
        P("seq", "col"),
        P(None, None, "col", None),
        P("col", None, None),
        P(),
    )
    return jax.shard_map(
        shards,
        mesh=mesh,
        in_specs=placed,
        out_specs=(
            P("seq", "col"),
            P("seq", "col"),
            P(None, None, "col", None),
            P("col", None, None),
        ),
        check_vma=False,
    )
```

```python
import functools
import math

import jax
import jax.numpy as jnp
from jax import lax
from jax.experimental import pallas as pl
from jax.experimental.pallas import tpu as pltpu
from jax.sharding import PartitionSpec as P

MESH = pl.DeviceIdType.MESH
F32 = jnp.float32
BF16 = jnp.bfloat16

T = 1024
R = 2 * T
D = 512
E = 128
HALF = D // 2
CH = 256
NCH = T // CH
TQ = 512
TK = 512
WIN = 3 * R
EPS = 1e-5
FLOOR = 1.0
SCALE = E**-0.5
OUT_OF_MASK = -32.0
SLOTS = R // CH
AROUND = (2, 3, 5, 6, 7)
CHIPS = 32
VMEM_LIMIT = 56 * 1024 * 1024

NT = (((1,), (1,)), ((), ()))
TN = (((0,), (0,)), ((), ()))


def dot(a, b, dims=(((1,), (0,)), ((), ()))):
    return lax.dot_general(a, b, dims, preferred_element_type=F32)


def guarded(on, act):
    if on is None:
        act()
    else:
        pl.when(on)(act)


class Copy:
    def __init__(self, src, dst, sems, at, device, on=None, arrives=None):
        self.on, self.arrives = on, arrives
        self.copy = pltpu.make_async_remote_copy(
            src_ref=src,
            dst_ref=dst,
            send_sem=sems[0].at[at],
            recv_sem=sems[1].at[at],
            device_id=device,
            device_id_type=MESH,
        )

    def start(self):
        guarded(self.on, self.copy.start)
        return self

    def wait_recv(self):
        guarded(self.arrives, self.copy.wait_recv)

    def wait_send(self):
        guarded(self.on, self.copy.wait_send)


def rows_at(start, size):
    return pl.ds(pl.multiple_of(start, size), size)


class Place:
    def __init__(self):
        s, c = lax.axis_index("seq"), lax.axis_index("col")
        self.s, self.c = s, c
        self.core = lax.rem(s, 2)
        self.chip = lax.div(s, 2)
        self.y = lax.rem(self.chip, 4)
        self.z = lax.rem(lax.div(s, 8), 4)
        self.xl = lax.div(s, 32)
        self.other = (s + 1 - 2 * self.core, c)
        self.far = (s, 1 - c)
        self.xpeer = (s + 32 - 64 * self.xl, c)

    def at_chip(self, chip):
        return (2 * lax.rem(chip + 2 * CHIPS, CHIPS) + self.core, self.c)

    def in_ring(self, step):
        return self.chip - self.y + lax.rem(self.y + 4 + step, 4)


def greet(senders, count):
    barrier = pltpu.get_barrier_semaphore()
    for device in senders:
        pl.semaphore_signal(barrier, inc=1, device_id=device, device_id_type=MESH)
    pl.semaphore_wait(barrier, count)


class Near:
    def __init__(self, me, step, src, via, dst, sems, at):
        edge = 3 if step > 0 else 0
        first, last = (0, CHIPS - 1) if step > 0 else (CHIPS - 1, 0)
        cross = me.y == edge
        goes = me.chip != last
        self.comes = me.chip != first
        self.straight = Copy(src, dst, sems, (0,) + at, me.at_chip(me.chip + step), goes & ~cross, self.comes)
        beyond = me.chip > 3 if step > 0 else me.chip < CHIPS - 4
        self.aside = Copy(
            src, via, sems, (1,) + at, me.at_chip(me.chip + 4 * step), goes & cross, beyond & cross
        )
        self.onward = Copy(via, dst, sems, (0,) + at, me.at_chip(me.in_ring(step)), beyond & cross)

    def start(self):
        self.straight.start()
        self.aside.start()

    def hand_on(self):
        self.aside.wait_recv()
        self.onward.start()

    def wait_recv(self):
        self.straight.wait_recv()

    def wait_send(self):
        for copy in (self.straight, self.aside, self.onward):
            copy.wait_send()


def project_kernel(
    tok_ref, cot_ref, w_ref,
    wh_ref, nb_ref, rs_ref, q_ref, up_ref, kv_ref, cg_ref,
    xg, yvia, nvia, wv, wf, wh, nb, inv_all, qv, upv, cg, oss, ors, kss, krs, ls, lcg,
):
    me = Place()
    c, core, chip = me.c, me.core, me.chip
    ahead = me.at_chip(chip + 1)
    round_to = me.at_chip(me.in_ring(-1))
    source = me.in_ring(1)
    handed_to = me.at_chip(source + 2)
    two_back = lax.rem(chip + CHIPS - 2, CHIPS)
    two_y = lax.rem(two_back, 4)
    hander = me.at_chip(two_back - two_y + lax.rem(two_y + 3, 4))
    greet(
        [me.other, me.far, me.at_chip(chip - 1), me.at_chip(chip - 4), round_to, me.at_chip(source), hander],
        7,
    )

    base = core * T
    obase = (1 - core) * T

    bufs = (xg, cg)
    srcs = (tok_ref, cot_ref)
    x_copies, o_copies, f_copies = {}, {}, {}
    for kind in (0, 1):
        for i in range(NCH):
            rr = rows_at(base + i * CH, CH)
            x_copies[kind, i] = Copy(
                srcs[kind].at[pl.ds(i * CH, CH)], bufs[kind].at[c, rr], (oss, ors), (kind, 2, i), me.far
            )
            o_copies[kind, i] = Copy(
                srcs[kind].at[pl.ds(i * CH, CH)], bufs[kind].at[c, rr], (oss, ors), (kind, 0, i), me.other
            )
            where = bufs[kind].at[1 - c, rr]
            f_copies[kind, i] = Copy(where, where, (oss, ors), (kind, 1, i), me.other)

    for i in range(NCH):
        x_copies[0, i].start()
        o_copies[0, i].start()
    loads = [
        pltpu.make_async_copy(src, dst, lcg.at[k])
        for k, (src, dst) in enumerate(
            (
                (w_ref, wv),
                (tok_ref, xg.at[c, rows_at(base, T)]),
                (cot_ref, cg.at[c, rows_at(base, T)]),
            )
        )
    ]
    for copy in loads:
        copy.start()
    for copy in loads:
        copy.wait()
    stores = []

    def store(k, slot, src, dst):
        copy = pltpu.make_async_copy(src, dst, ls.at[k, slot])
        copy.start()
        stores.append(copy)

    wf[...] = wv[...].astype(F32)
    for place, part in enumerate((0, 2, 1, 3)):
        lanes = slice(place * E, (place + 1) * E)
        first = wf[pl.ds(2 * part, D, stride=8), :]
        second = wf[pl.ds(2 * part + 1, D, stride=8), :]
        wh[:, lanes] = jnp.where(core == 0, first, second).astype(BF16)
    store(4, 0, wh, wh_ref)

    near, hop, direct, chained = {}, {}, {}, {}
    for slot in range(SLOTS):
        rr = rows_at((base if slot < NCH else obase) + slot % NCH * CH, CH)
        mine = kv_ref.at[2, rr]
        near[slot] = Near(me, 1, mine, nvia.at[slot], kv_ref.at[1, rr], (kss, krs), (slot,))
        if slot in AROUND:
            hop[slot] = Copy(
                mine, yvia.at[slot], (kss, krs), (2, slot), round_to,
                chip < CHIPS - 2, source < CHIPS - 2,
            )
            direct[slot] = Copy(
                yvia.at[slot], kv_ref.at[0, rr], (kss, krs), (3, slot), handed_to,
                source < CHIPS - 2, chip > 1,
            )
        else:
            chained[slot] = Copy(
                kv_ref.at[1, rr], kv_ref.at[0, rr], (kss, krs), (3, slot), ahead,
                (chip > 0) & (chip < CHIPS - 1), chip > 1,
            )

    def compute(slot):
        rr = rows_at((base if slot < NCH else obase) + slot % NCH * CH, CH)
        x0 = xg[0, rr].astype(F32)
        x1 = xg[1, rr].astype(F32)
        mean = (jnp.sum(x0, -1, keepdims=True) + jnp.sum(x1, -1, keepdims=True)) * (1.0 / D)
        x0 = x0 - mean
        x1 = x1 - mean
        var = (
            jnp.sum(x0 * x0, -1, keepdims=True) + jnp.sum(x1 * x1, -1, keepdims=True)
        ) * (1.0 / D)
        inv = lax.rsqrt(var + EPS)
        n0 = (x0 * inv).astype(BF16)
        n1 = (x1 * inv).astype(BF16)
        half = 0.5 * (dot(n0, wh[:HALF]) + dot(n1, wh[HALF:]))
        proj = (half + half * jnp.tanh(half)).astype(BF16)
        kv_ref[2, rr] = proj[:, 2 * E :]
        near[slot].start()
        if slot in AROUND:
            hop[slot].start()
        nb[rr, :HALF] = n0
        nb[rr, HALF:] = n1
        inv_all[rr] = jnp.broadcast_to(inv, (CH, E))
        upv[rr] = proj[:, :E]
        qv[rr] = proj[:, E : 2 * E]
        for k, (src, dst) in enumerate(((nb, nb_ref), (inv_all, rs_ref), (upv, up_ref), (qv, q_ref))):
            store(k, slot, src.at[rr], dst.at[rr])

    def hand_on(slot):
        if slot in AROUND:
            hop[slot].wait_recv()
            direct[slot].start()
        else:
            near[slot].wait_recv()
            chained[slot].start()

    for i in range(NCH):
        x_copies[0, i].wait_recv()
        f_copies[0, i].start()
        compute(i)
        o_copies[0, i].wait_recv()
        f_copies[0, i].wait_recv()
        compute(NCH + i)
        if i:
            for slot in (i - 1, NCH + i - 1):
                near[slot].hand_on()
                if slot in AROUND:
                    hand_on(slot)
    for i in range(NCH):
        x_copies[1, i].start()
        o_copies[1, i].start()
    for slot in (NCH - 1, SLOTS - 1):
        near[slot].hand_on()
        if slot in AROUND:
            hand_on(slot)
    for slot in (0, NCH, 1):
        hand_on(slot)
    for i in range(NCH):
        x_copies[1, i].wait_recv()
        f_copies[1, i].start()
    for i in range(NCH):
        o_copies[1, i].wait_recv()
        f_copies[1, i].wait_recv()
    copy = pltpu.make_async_copy(cg, cg_ref, lcg.at[3])
    copy.start()
    stores.append(copy)
    for slot in range(SLOTS):
        if slot in AROUND:
            near[slot].wait_recv()
            direct[slot].wait_recv()
        else:
            chained[slot].wait_recv()
    for copies in (x_copies, o_copies, f_copies, near, hop, direct, chained):
        for copy in copies.values():
            copy.wait_send()
    for copy in stores:
        copy.wait()


def project(tokens, cotangent, w):
    vm = pl.BlockSpec(memory_space=pltpu.VMEM)
    hbm = pl.BlockSpec(memory_space=pl.ANY)
    dma = pltpu.SemaphoreType.DMA
    return pl.pallas_call(
        project_kernel,
        out_shape=(
            jax.ShapeDtypeStruct((D, 4 * E), BF16),
            jax.ShapeDtypeStruct((R, D), BF16),
            jax.ShapeDtypeStruct((R, E), F32),
            jax.ShapeDtypeStruct((R, E), BF16),
            jax.ShapeDtypeStruct((R, E), BF16),
            jax.ShapeDtypeStruct((3, R, 2 * E), BF16),
            jax.ShapeDtypeStruct((2, R, HALF), BF16),
        ),
        in_specs=[hbm] * 3,
        out_specs=(hbm,) * 5 + (vm, hbm),
        scratch_shapes=[
            pltpu.VMEM((2, R, HALF), BF16),
            pltpu.VMEM((SLOTS, CH, 2 * E), BF16),
            pltpu.VMEM((SLOTS, CH, 2 * E), BF16),
            pltpu.VMEM((8 * D, E), BF16),
            pltpu.VMEM((8 * D, E), F32),
            pltpu.VMEM((D, 4 * E), BF16),
            pltpu.VMEM((R, D), BF16),
            pltpu.VMEM((R, E), F32),
            pltpu.VMEM((R, E), BF16),
            pltpu.VMEM((R, E), BF16),
            pltpu.VMEM((2, R, HALF), BF16),
            dma((2, 3, NCH)),
            dma((2, 3, NCH)),
            dma((4, SLOTS)),
            dma((4, SLOTS)),
            dma((5, SLOTS)),
            dma((4,)),
        ],
        compiler_params=pltpu.CompilerParams(
            collective_id=0, has_side_effects=True, vmem_limit_bytes=VMEM_LIMIT
        ),
        cost_estimate=pl.CostEstimate(
            flops=2 * R * D * D, bytes_accessed=16 << 20, transcendentals=R * D
        ),
        name="gather_project",
    )(tokens, cotangent, w)


def attention_kernel(
    q_ref, kv_ref, up_ref, cg_ref, wo_all, all_ids,
    op_ref, gated_ref, dup_ref, dq_ref, dkv_ref, dfar_ref,
    id_ref, idc, acc,
):
    s = lax.axis_index("seq")
    chip = lax.div(s, 2)
    wo_ref = wo_all.at[lax.rem(s, 2)]
    t = pl.program_id(0)

    @pl.when(t == 0)
    def _():
        for b in range(3):
            source = chip - 2 + b
            ids = all_ids[rows_at(jnp.maximum(source, 0) * (R // E), R // E), :]
            ids = jnp.where(source >= 0, ids, -1)
            for j in range(R // E):
                at = b * R + j * E
                row = ids[j : j + 1, :]
                id_ref[0:1, at : at + E] = row
                idc[at : at + E, :] = jnp.broadcast_to(row, (E, E)).T

        @pl.loop(0, WIN // TK)
        def _(j):
            acc[rows_at(j * TK, TK), :] = jnp.zeros((TK, 2 * E), F32)

    def spread(column, width):
        return jnp.concatenate([column] * (width // E), axis=1)

    first = 2 * R // TK
    q = q_ref[...]
    wr = rows_at(2 * R + t * TQ, TQ)
    idq_col = idc[wr, :]
    idq_row = id_ref[0:1, wr]
    start = idq_row[0, 0]
    before = (id_ref[...] < start).astype(jnp.int32)
    low = jnp.sum(before) // TK
    last = first + t * TQ // TK
    uniform = start == idq_row[0, TQ - 1]
    mid = jnp.where(uniform, jnp.minimum(low + 1, last), last)

    def masked(half, ok, kt, causal, row_axis):
        if causal:
            ri = lax.broadcasted_iota(jnp.int32, half.shape, row_axis) + t * TQ
            ci = lax.broadcasted_iota(jnp.int32, half.shape, 1 - row_axis) + (kt - first) * TK
            ok = ok & (ci <= ri)
        return jnp.where(ok, half, OUT_OF_MASK)

    def forward(kt, total, mask=True, causal=False):
        kr = rows_at(kt * TK, TK)
        half = dot(q, kv_ref[kr, E:], NT) * (0.5 * SCALE)
        if mask:
            half = masked(half, spread(idq_col, TK) == id_ref[0:1, kr], kt, causal, 0)
        weights = (half + half * jnp.tanh(half)).astype(BF16)
        return total + dot(weights, kv_ref[kr, :E])

    def backward(kt, total, mask=True, causal=False):
        kr = rows_at(kt * TK, TK)
        k = kv_ref[kr, E:]
        half = dot(k, q, NT) * (0.5 * SCALE)
        if mask:
            half = masked(half, spread(idc[kr, :], TQ) == idq_row, kt, causal, 1)
        tan = jnp.tanh(half)
        weights = half + half * tan
        tan = 0.5 * tan
        slope = (0.5 + tan) + weights * (0.5 - tan)
        ds = (slope * dot(kv_ref[kr, :E], grad, NT)).astype(BF16)
        acc[kr, E:] += dot(ds, q)
        acc[kr, :E] += dot(weights.astype(BF16), grad)
        return total + dot(k.T, ds)

    def over_keys(step, shape=(TQ, E)):
        total = lax.fori_loop(low, mid, step, jnp.zeros(shape, F32))
        total = lax.fori_loop(mid, last, functools.partial(step, mask=False), total)
        for j in range(max(1, TQ // TK)):
            total = step(last + j, total, causal=True)
        return total

    att = over_keys(forward)
    center = att - jnp.mean(att, -1, keepdims=True)
    scale = lax.rsqrt(jnp.mean(center * center, -1, keepdims=True) + FLOOR)
    hn = center * scale
    up = up_ref[...].astype(F32)
    gated = (hn * up).astype(BF16)
    gated_ref[...] = gated
    op_ref[0] = dot(gated, wo_ref[:, :HALF]).astype(BF16)
    op_ref[1] = dot(gated, wo_ref[:, HALF:]).astype(BF16)
    gg = dot(cg_ref[0], wo_ref[:, :HALF], NT) + dot(cg_ref[1], wo_ref[:, HALF:], NT)
    dup_ref[...] = gg * hn
    b = gg * up
    grad = (
        scale * (b - jnp.mean(b, -1, keepdims=True) - hn * jnp.mean(b * hn, -1, keepdims=True))
    ).astype(BF16)
    dq_ref[...] = over_keys(backward, (E, TQ)).T * SCALE

    @pl.when(t == R // TQ - 1)
    def _():
        @pl.loop(0, R // TK)
        def _(j):
            rr = rows_at(j * TK, TK)
            own = rows_at(2 * R + j * TK, TK)
            dkv_ref[rr, :E] = acc[own, :E]
            dkv_ref[rr, E:] = acc[own, E:] * SCALE
            for k in range(2):
                src = rows_at(k * R + j * TK, TK)
                dfar_ref[k, rr, :E] = acc[src, :E].astype(BF16)
                dfar_ref[k, rr, E:] = (acc[src, E:] * SCALE).astype(BF16)


def attention(q, kv, up, cg, wo, ids):
    vm = pl.BlockSpec(memory_space=pltpu.VMEM)
    tile = pl.BlockSpec((TQ, E), lambda t: (t, 0))
    halves = pl.BlockSpec((2, TQ, HALF), lambda t: (0, t, 0))
    return pl.pallas_call(
        attention_kernel,
        grid=(R // TQ,),
        out_shape=(
            jax.ShapeDtypeStruct((2, R, HALF), BF16),
            jax.ShapeDtypeStruct((R, E), BF16),
            jax.ShapeDtypeStruct((R, E), F32),
            jax.ShapeDtypeStruct((R, E), F32),
            jax.ShapeDtypeStruct((R, 2 * E), F32),
            jax.ShapeDtypeStruct((2, R, 2 * E), BF16),
        ),
        in_specs=[tile, vm, tile, halves, vm, vm],
        out_specs=(
            halves,
            tile,
            tile,
            tile,
            pl.BlockSpec((R, 2 * E), lambda t: (0, 0)),
            pl.BlockSpec((2, R, 2 * E), lambda t: (0, 0, 0)),
        ),
        scratch_shapes=[
            pltpu.VMEM((1, WIN), jnp.int32),
            pltpu.VMEM((WIN, E), jnp.int32),
            pltpu.VMEM((WIN, 2 * E), F32),
        ],
        compiler_params=pltpu.CompilerParams(vmem_limit_bytes=VMEM_LIMIT),
        cost_estimate=pl.CostEstimate(
            flops=7 * 2 * R * R * 2 * E, bytes_accessed=16 << 20, transcendentals=4 * R * R
        ),
        name="attention",
    )(q, kv, up, cg, wo, ids)


class Summed:
    def __init__(self, me, rows, grads, bufs, sems, at):
        self.me, self.rows, self.grads, self.bufs = me, rows, grads, bufs
        self.sems, self.at = sems, at
        self.done = []

    def copy(self, src, dst, stage, k, device):
        copy = Copy(src, dst, self.sems, (self.at, stage, k), device).start()
        self.done.append(copy)
        return copy

    def peers(self, here, step):
        s, c = self.me.s, self.me.c
        there = [lax.rem(here + k, 4) for k in (1, 2, 3)]
        return [(v, (s + step * (v - here), c)) for v in there]

    def start(self):
        zbuf, zrecv = self.bufs[0:2]
        n = self.rows // 4
        zbuf[...] = self.grads[...].astype(BF16)
        self.zc = [
            self.copy(zbuf.at[rows_at(v * n, n)], zrecv.at[k], 0, k, device)
            for k, (v, device) in enumerate(self.peers(self.me.z, 8))
        ]

    def over_y(self):
        zrecv, yall = self.bufs[1:3]
        n = self.rows // 4
        for copy in self.zc:
            copy.wait_recv()
        total = self.grads[rows_at(self.me.z * n, n), :]
        for k in range(3):
            total = total + zrecv[k].astype(F32)
        spot = yall.at[self.me.y]
        spot[...] = total.astype(BF16)
        self.yc = [
            self.copy(spot, spot, 1, k, device) for k, (_, device) in enumerate(self.peers(self.me.y, 2))
        ]

    def over_x(self):
        yall, xall = self.bufs[2:4]
        for copy in self.yc:
            copy.wait_recv()
        total = (yall[0].astype(F32) + yall[1].astype(F32)) + (yall[2].astype(F32) + yall[3].astype(F32))
        spot = xall.at[self.me.xl]
        spot[...] = total.astype(BF16)
        self.xc = self.copy(spot, spot, 2, 0, self.me.xpeer)

    def back_z(self):
        xall, whole = self.bufs[3:5]
        me = self.me
        self.xc.wait_recv()
        spot = whole.at[me.core, me.z]
        spot[...] = (xall[0].astype(F32) + xall[1].astype(F32)).astype(BF16)
        self.gz = [
            self.copy(spot, spot, 3, k, device) for k, (_, device) in enumerate(self.peers(me.z, 8))
        ]
        self.gc = [self.copy(spot, spot, 4, 0, me.other)]

    def back_core(self):
        me = self.me
        for k in range(3):
            self.gz[k].wait_recv()
            spot = self.bufs[4].at[me.core, lax.rem(me.z + 3 - k, 4)]
            self.gc.append(self.copy(spot, spot, 4, k + 1, me.other))

    def finish(self):
        for copy in self.gc:
            copy.wait_recv()

    def wait_send(self):
        for copy in self.done:
            copy.wait_send()

    @staticmethod
    def scratch(rows):
        n = rows // 4
        return [
            pltpu.VMEM((rows, 2 * E), BF16),
            pltpu.VMEM((3, n, 2 * E), BF16),
            pltpu.VMEM((4, n, 2 * E), BF16),
            pltpu.VMEM((2, n, 2 * E), BF16),
        ]


EARLY = D + 2 * E
INV_ROOT = 1.0 / 256.0


def gradient_kernel(
    tok_in, cot_in, w_in, nb_in, rs_in, cg_in, gated_in, op_in, dup_in, dq_in, dkv_in, dfar_in,
    out_ref, gt_ref, early_all, late_all,
    tok_ref, cot_ref, w_ref, nb_ref, rs_ref, cg_ref, gated_ref, op_ref, dup_ref, dq_ref, dkv_ref, dfar_ref, ls,
    hopped, back, yvia, nvia, slope, gp, part, chip_sum, to_col, from_col, early_g, late_g, *rest,
):
    early_bufs, late_bufs = rest[:4] + (early_all,), rest[4:8] + (late_all,)
    bss, brs, sss, srs, ass, ars = rest[8:]
    me = Place()
    c, core, chip = me.c, me.core, me.chip
    behind = me.at_chip(chip - 1)
    round_to = me.at_chip(me.in_ring(1))
    source = me.in_ring(-1)
    handed_to = me.at_chip(source - 2)
    two_on = lax.rem(chip + 2, CHIPS)
    two_y = lax.rem(two_on, 4)
    hander = me.at_chip(two_on - two_y + lax.rem(two_y + 1, 4))
    early = Summed(me, EARLY, early_g, early_bufs, (ass, ars), 0)
    late = Summed(me, D, late_g, late_bufs, (ass, ars), 1)
    greet(
        [me.other, me.far, me.at_chip(chip + 1), me.at_chip(chip + 4), round_to, me.at_chip(source)]
        + [hander, me.xpeer]
        + [device for _, device in early.peers(me.y, 2) + early.peers(me.z, 8)],
        14,
    )

    base = core * T
    obase = (1 - core) * T

    order = (
        (nb_in, nb_ref), (w_in, w_ref), (dup_in, dup_ref), (dq_in, dq_ref), (gated_in, gated_ref),
        (cg_in, cg_ref), (op_in.at[:, rows_at(base, T)], op_ref), (dfar_in.at[1], dfar_ref),
        (dkv_in, dkv_ref), (rs_in, rs_ref), (tok_in, tok_ref), (cot_in, cot_ref),
    )
    loads = [pltpu.make_async_copy(src, dst, ls.at[k]) for k, (src, dst) in enumerate(order)]

    def mine_of(kind, half, i):
        if kind == 0:
            return op_ref[half, pl.ds(i * CH, CH)]
        return part[half, rows_at(base + i * CH, CH)]

    def to_core(kind, i):
        src = (op_in, part)[kind].at[:, rows_at(obase + i * CH, CH)]
        dst = chip_sum.at[kind, :, pl.ds(i * CH, CH)]
        return Copy(src, dst, (sss, srs), (kind, 0, i), me.other).start()

    def across(kind, i, copy):
        copy.wait_recv()
        here = pl.ds(i * CH, CH)
        mine = mine_of(kind, 1 - c, i).astype(F32)
        to_col[kind, here] = (mine + chip_sum[kind, 1 - c, here].astype(F32)).astype(BF16)
        return Copy(
            to_col.at[kind, here], from_col.at[kind, here], (sss, srs), (kind, 1, i), me.far
        ).start()

    def finish(kind, i, copy):
        copy.wait_recv()
        here = pl.ds(i * CH, CH)
        own, out = ((tok_ref, out_ref), (cot_ref, gt_ref))[kind]
        total = mine_of(kind, c, i).astype(F32)
        total = total + chip_sum[kind, c, here].astype(F32)
        total = total + from_col[kind, here].astype(F32)
        out[here] = (own[here].astype(F32) + total).astype(BF16)

    near, hop, direct = {}, {}, {}
    for i in range(SLOTS):
        rr = pl.ds(i * CH, CH)
        near[i] = Near(
            me, -1, dfar_in.at[1, rr] if i in AROUND else back.at[2, rr], nvia.at[i], back.at[1, rr],
            (bss, brs), (i,),
        )
        if i in AROUND:
            hop[i] = Copy(
                dfar_in.at[0, rr], yvia.at[i], (bss, brs), (2, i), round_to, chip > 1, source > 1
            )
            direct[i] = Copy(
                yvia.at[i], back.at[0, rr], (bss, brs), (3, i), handed_to, source > 1, chip < CHIPS - 2
            )
        else:
            hop[i] = Copy(
                dfar_in.at[0, rr], hopped.at[i], (bss, brs), (2, i), behind,
                chip > 1, (chip > 0) & (chip < CHIPS - 1),
            )
    joined = [i for i in range(SLOTS) if i not in AROUND]
    for i in joined:
        hop[i].start()
    for i in AROUND:
        hop[i].start()
        near[i].start()
    for copy in loads:
        copy.start()
    out_core = [to_core(0, i) for i in range(NCH)]

    SR = 512
    for copy in loads[:4]:
        copy.wait()

    @pl.loop(0, R // SR)
    def _(i):
        rr = rows_at(i * SR, SR)
        half = 0.5 * dot(nb_ref[rr, :], w_ref[...])
        tan = jnp.tanh(half)
        silu = half + half * tan
        tan = 0.5 * tan
        sl = (0.5 + tan) + silu * (0.5 - tan)
        gp[rr, :E] = (dup_ref[rr, :] * sl[:, :E]).astype(BF16)
        gp[rr, E : 2 * E] = (dq_ref[rr, :] * sl[:, E : 2 * E]).astype(BF16)
        slope[rr, :] = sl[:, 2 * E :]

    for copy in loads[4:6]:
        copy.wait()
    early_g[:D, :] = dot(nb_ref[...], gp[:, : 2 * E], TN)
    for j in range(2):
        early_g[D + j * E : D + (j + 1) * E, :] = dot(gated_ref[...], cg_ref[j], TN)
    early.start()

    for copy in loads[6:]:
        copy.wait()
    out_far = [across(0, i, out_core[i]) for i in range(NCH)]

    for i in joined:
        rr = pl.ds(i * CH, CH)
        back[2, rr] = dfar_ref[rr]

        @pl.when((chip > 0) & (chip < CHIPS - 1))
        def _():
            hop[i].copy.wait_recv()
            back[2, rr] = (dfar_ref[rr].astype(F32) + hopped[i].astype(F32)).astype(BF16)

        near[i].start()
    for i in AROUND:
        hop[i].wait_recv()
        direct[i].start()
    for i in list(AROUND) + joined:
        near[i].hand_on()
    early.over_y()

    for i in list(AROUND) + joined:
        rr = pl.ds(i * CH, CH)
        near[i].wait_recv()

        @pl.when(chip == CHIPS - 1)
        def _():
            back[1, rr] = jnp.zeros((CH, 2 * E), BF16)

        g = dkv_ref[rr, :]
        if i in AROUND:
            direct[i].wait_recv()

            @pl.when(chip >= CHIPS - 2)
            def _():
                back[0, rr] = jnp.zeros((CH, 2 * E), BF16)

            g = g + back[0, rr].astype(F32)
        gp[rr, 2 * E :] = ((g + back[1, rr].astype(F32)) * slope[rr, :]).astype(BF16)

    late_g[...] = dot(nb_ref[...], gp[:, 2 * E :], TN)
    late.start()
    early.over_x()

    def tokens_back(start):
        rr = rows_at(start, CH)
        g = dot(gp[rr, :], w_ref[...], NT)
        nb = nb_ref[rr, :].astype(F32)
        inv = rs_ref[rr, 0:1]
        g = inv * (g - jnp.mean(g, -1, keepdims=True) - nb * jnp.mean(g * nb, -1, keepdims=True))
        part[0, rr] = g[:, :HALF].astype(BF16)
        part[1, rr] = g[:, HALF:].astype(BF16)

    gt_core = []
    for i in range(NCH):
        tokens_back(obase + i * CH)
        gt_core.append(to_core(1, i))
    early.back_z()
    gt_far = []
    for i in range(NCH):
        tokens_back(base + i * CH)
        gt_far.append(across(1, i, gt_core[i]))
    late.over_y()
    for i in range(NCH):
        finish(0, i, out_far[i])
    early.back_core()
    late.over_x()
    late.back_z()
    early.finish()
    late.back_core()
    for i in range(NCH):
        finish(1, i, gt_far[i])
    late.finish()
    for copies in (near, hop, direct):
        for copy in copies.values():
            copy.wait_send()
    for copy in out_core + out_far + gt_core + gt_far + [early, late]:
        copy.wait_send()


def gradients(*operands):
    vm = pl.BlockSpec(memory_space=pltpu.VMEM)
    hbm = pl.BlockSpec(memory_space=pl.ANY)
    dma = pltpu.SemaphoreType.DMA
    loaded = [list(x.shape) for x in operands]
    loaded[7][1] = T
    loaded[11] = [R, 2 * E]
    return pl.pallas_call(
        gradient_kernel,
        out_shape=(
            jax.ShapeDtypeStruct((T, HALF), BF16),
            jax.ShapeDtypeStruct((T, HALF), BF16),
            jax.ShapeDtypeStruct((2, 4, EARLY // 4, 2 * E), BF16),
            jax.ShapeDtypeStruct((2, 4, D // 4, 2 * E), BF16),
        ),
        in_specs=[hbm] * 12,
        out_specs=(vm,) * 4,
        scratch_shapes=[pltpu.VMEM(tuple(d), x.dtype) for d, x in zip(loaded, operands)]
        + [
            dma((12,)),
            pltpu.VMEM((SLOTS, CH, 2 * E), BF16),
            pltpu.VMEM((3, R, 2 * E), BF16),
            pltpu.VMEM((SLOTS, CH, 2 * E), BF16),
            pltpu.VMEM((SLOTS, CH, 2 * E), BF16),
            pltpu.VMEM((R, 2 * E), F32),
            pltpu.VMEM((R, 4 * E), BF16),
            pltpu.VMEM((2, R, HALF), BF16),
            pltpu.VMEM((2, 2, T, HALF), BF16),
            pltpu.VMEM((2, T, HALF), BF16),
            pltpu.VMEM((2, T, HALF), BF16),
            pltpu.VMEM((EARLY, 2 * E), F32),
            pltpu.VMEM((D, 2 * E), F32),
        ]
        + Summed.scratch(EARLY)
        + Summed.scratch(D)
        + [
            dma((4, SLOTS)),
            dma((4, SLOTS)),
            dma((2, 2, NCH)),
            dma((2, 2, NCH)),
            dma((2, 5, 4)),
            dma((2, 5, 4)),
        ],
        compiler_params=pltpu.CompilerParams(
            collective_id=1, has_side_effects=True, vmem_limit_bytes=VMEM_LIMIT
        ),
        cost_estimate=pl.CostEstimate(
            flops=7 * R * D * D, bytes_accessed=16 << 20, transcendentals=R * D
        ),
        name="gradients",
    )(*operands)


def widen_kernel(out_in, gt_in, early_ref, late_ref, out_ref, gt_ref, gwi_ref, gwo_ref, ls):
    passed = [
        pltpu.make_async_copy(src, dst, ls.at[k])
        for k, (src, dst) in enumerate(((out_in, out_ref), (gt_in, gt_ref)))
    ]
    for copy in passed:
        copy.start()
    n = EARLY // 4
    for h in range(2):
        for z in range(4):
            at = 0
            while at < n:
                d = z * n + at
                end = next(b for b in (D, D + E, EARLY) if b > d)
                size = min(n - at, end - d)
                piece = early_ref[h, z, at : at + size, :].astype(F32) * INV_ROOT
                if d < D:
                    for j in range(2):
                        gwi_ref[pl.ds(8 * d + 4 * j + h, size, stride=8), :] = piece[:, j * E : (j + 1) * E]
                else:
                    q, e = divmod(d - D, E)
                    gwo_ref[h, e : e + size, q * HALF : (q + 1) * HALF] = piece
                at += size
            m = D // 4
            piece = late_ref[h, z].astype(F32) * INV_ROOT
            for j in range(2):
                gwi_ref[pl.ds(8 * z * m + 4 * j + 2 + h, m, stride=8), :] = piece[:, j * E : (j + 1) * E]
    for copy in passed:
        copy.wait()


def widen(out, gt, early, late):
    vm = pl.BlockSpec(memory_space=pltpu.VMEM)
    hbm = pl.BlockSpec(memory_space=pl.ANY)
    return pl.pallas_call(
        widen_kernel,
        out_shape=(
            jax.ShapeDtypeStruct((T, HALF), BF16),
            jax.ShapeDtypeStruct((T, HALF), BF16),
            jax.ShapeDtypeStruct((8 * D, E), F32),
            jax.ShapeDtypeStruct((2, E, D), F32),
        ),
        in_specs=[hbm, hbm, vm, vm],
        out_specs=(hbm, hbm, vm, vm),
        scratch_shapes=[pltpu.SemaphoreType.DMA((2,))],
        compiler_params=pltpu.CompilerParams(vmem_limit_bytes=VMEM_LIMIT),
        name="widen",
    )(out, gt, early, late)


def shards(tokens, cotangent, weight_in, weight_out, history_ids):
    w, nb, inv, q, up, kv, cg = project(tokens, cotangent, weight_in.reshape(8 * D, E))
    op, gated, dup, dq, dkv, dfar = attention(
        q, kv.reshape(WIN, 2 * E), up, cg, weight_out, history_ids.reshape(-1, E)
    )
    out, gt, gwi, gwo = widen(
        *gradients(tokens, cotangent, w, nb, inv, cg, gated, op, dup, dq, dkv, dfar)
    )
    return out, gt, gwi.reshape(D, 4, 2, E), gwo


def solution(mesh):
    placed = (
        P("seq", "col"),
        P("seq", "col"),
        P(None, None, "col", None),
        P("col", None, None),
        P(),
    )
    return jax.shard_map(
        shards,
        mesh=mesh,
        in_specs=placed,
        out_specs=(
            P("seq", "col"),
            P("seq", "col"),
            P(None, None, "col", None),
            P("col", None, None),
        ),
        check_vma=False,
    )
```

```python
import functools
import math

import jax
import jax.numpy as jnp
from jax import lax
from jax.experimental import pallas as pl
from jax.experimental.pallas import tpu as pltpu
from jax.sharding import PartitionSpec as P

MESH = pl.DeviceIdType.MESH
F32 = jnp.float32
BF16 = jnp.bfloat16

T = 1024
R = 2 * T
D = 512
E = 128
HALF = D // 2
CH = 256
NCH = T // CH
TQ = 512
TK = 512
WIN = 3 * R
EPS = 1e-5
FLOOR = 1.0
SCALE = E**-0.5
OUT_OF_MASK = -32.0
SLOTS = R // CH
AROUND = (2, 3, 5, 6, 7)
CHIPS = 32
VMEM_LIMIT = 56 * 1024 * 1024

NT = (((1,), (1,)), ((), ()))
TN = (((0,), (0,)), ((), ()))


def dot(a, b, dims=(((1,), (0,)), ((), ()))):
    return lax.dot_general(a, b, dims, preferred_element_type=F32)


def guarded(on, act):
    if on is None:
        act()
    else:
        pl.when(on)(act)


class Copy:
    def __init__(self, src, dst, sems, at, device, on=None, arrives=None):
        self.on, self.arrives = on, arrives
        self.copy = pltpu.make_async_remote_copy(
            src_ref=src,
            dst_ref=dst,
            send_sem=sems[0].at[at],
            recv_sem=sems[1].at[at],
            device_id=device,
            device_id_type=MESH,
        )

    def start(self):
        guarded(self.on, self.copy.start)
        return self

    def wait_recv(self):
        guarded(self.arrives, self.copy.wait_recv)

    def wait_send(self):
        guarded(self.on, self.copy.wait_send)


def rows_at(start, size):
    return pl.ds(pl.multiple_of(start, size), size)


class Place:
    def __init__(self):
        s, c = lax.axis_index("seq"), lax.axis_index("col")
        self.s, self.c = s, c
        self.core = lax.rem(s, 2)
        self.chip = lax.div(s, 2)
        self.y = lax.rem(self.chip, 4)
        self.z = lax.rem(lax.div(s, 8), 4)
        self.xl = lax.div(s, 32)
        self.other = (s + 1 - 2 * self.core, c)
        self.far = (s, 1 - c)
        self.xpeer = (s + 32 - 64 * self.xl, c)

    def at_chip(self, chip):
        return (2 * lax.rem(chip + 2 * CHIPS, CHIPS) + self.core, self.c)

    def in_ring(self, step):
        return self.chip - self.y + lax.rem(self.y + 4 + step, 4)


def greet(senders, count):
    barrier = pltpu.get_barrier_semaphore()
    for device in senders:
        pl.semaphore_signal(barrier, inc=1, device_id=device, device_id_type=MESH)
    pl.semaphore_wait(barrier, count)


class Near:
    def __init__(self, me, step, src, via, dst, sems, at):
        edge = 3 if step > 0 else 0
        first, last = (0, CHIPS - 1) if step > 0 else (CHIPS - 1, 0)
        cross = me.y == edge
        goes = me.chip != last
        self.comes = me.chip != first
        self.straight = Copy(src, dst, sems, (0,) + at, me.at_chip(me.chip + step), goes & ~cross, self.comes)
        beyond = me.chip > 3 if step > 0 else me.chip < CHIPS - 4
        self.aside = Copy(
            src, via, sems, (1,) + at, me.at_chip(me.chip + 4 * step), goes & cross, beyond & cross
        )
        self.onward = Copy(via, dst, sems, (0,) + at, me.at_chip(me.in_ring(step)), beyond & cross)

    def start(self):
        self.straight.start()
        self.aside.start()

    def hand_on(self):
        self.aside.wait_recv()
        self.onward.start()

    def wait_recv(self):
        self.straight.wait_recv()

    def wait_send(self):
        for copy in (self.straight, self.aside, self.onward):
            copy.wait_send()


def project_kernel(
    tok_ref, cot_ref, w_ref,
    wh_ref, nb_ref, rs_ref, q_ref, up_ref, kv_ref, cg_ref,
    xg, yvia, nvia, wv, wf, wh, nb, inv_all, qv, upv, cg, oss, ors, kss, krs, ls, lcg,
):
    me = Place()
    c, core, chip = me.c, me.core, me.chip
    ahead = me.at_chip(chip + 1)
    round_to = me.at_chip(me.in_ring(-1))
    source = me.in_ring(1)
    handed_to = me.at_chip(source + 2)
    two_back = lax.rem(chip + CHIPS - 2, CHIPS)
    two_y = lax.rem(two_back, 4)
    hander = me.at_chip(two_back - two_y + lax.rem(two_y + 3, 4))
    greet(
        [me.other, me.far, me.at_chip(chip - 1), me.at_chip(chip - 4), round_to, me.at_chip(source), hander],
        7,
    )

    base = core * T
    obase = (1 - core) * T

    bufs = (xg, cg)
    srcs = (tok_ref, cot_ref)
    x_copies, o_copies, f_copies = {}, {}, {}
    for kind in (0, 1):
        for i in range(NCH):
            rr = rows_at(base + i * CH, CH)
            x_copies[kind, i] = Copy(
                srcs[kind].at[pl.ds(i * CH, CH)], bufs[kind].at[c, rr], (oss, ors), (kind, 2, i), me.far
            )
            o_copies[kind, i] = Copy(
                srcs[kind].at[pl.ds(i * CH, CH)], bufs[kind].at[c, rr], (oss, ors), (kind, 0, i), me.other
            )
            where = bufs[kind].at[1 - c, rr]
            f_copies[kind, i] = Copy(where, where, (oss, ors), (kind, 1, i), me.other)

    for i in range(NCH):
        x_copies[0, i].start()
        o_copies[0, i].start()
    loads = [
        pltpu.make_async_copy(src, dst, lcg.at[k])
        for k, (src, dst) in enumerate(
            (
                (w_ref, wv),
                (tok_ref, xg.at[c, rows_at(base, T)]),
                (cot_ref, cg.at[c, rows_at(base, T)]),
            )
        )
    ]
    for copy in loads:
        copy.start()
    for copy in loads:
        copy.wait()
    stores = []

    def store(k, slot, src, dst):
        copy = pltpu.make_async_copy(src, dst, ls.at[k, slot])
        copy.start()
        stores.append(copy)

    wf[...] = wv[...].astype(F32)
    for place, part in enumerate((0, 2, 1, 3)):
        lanes = slice(place * E, (place + 1) * E)
        first = wf[pl.ds(2 * part, D, stride=8), :]
        second = wf[pl.ds(2 * part + 1, D, stride=8), :]
        wh[:, lanes] = jnp.where(core == 0, first, second).astype(BF16)
    store(4, 0, wh, wh_ref)

    near, hop, direct, chained = {}, {}, {}, {}
    for slot in range(SLOTS):
        rr = rows_at((base if slot < NCH else obase) + slot % NCH * CH, CH)
        mine = kv_ref.at[2, rr]
        near[slot] = Near(me, 1, mine, nvia.at[slot], kv_ref.at[1, rr], (kss, krs), (slot,))
        if slot in AROUND:
            hop[slot] = Copy(
                mine, yvia.at[slot], (kss, krs), (2, slot), round_to,
                chip < CHIPS - 2, source < CHIPS - 2,
            )
            direct[slot] = Copy(
                yvia.at[slot], kv_ref.at[0, rr], (kss, krs), (3, slot), handed_to,
                source < CHIPS - 2, chip > 1,
            )
        else:
            chained[slot] = Copy(
                kv_ref.at[1, rr], kv_ref.at[0, rr], (kss, krs), (3, slot), ahead,
                (chip > 0) & (chip < CHIPS - 1), chip > 1,
            )

    def compute(slot):
        rr = rows_at((base if slot < NCH else obase) + slot % NCH * CH, CH)
        x0 = xg[0, rr].astype(F32)
        x1 = xg[1, rr].astype(F32)
        mean = (jnp.sum(x0, -1, keepdims=True) + jnp.sum(x1, -1, keepdims=True)) * (1.0 / D)
        x0 = x0 - mean
        x1 = x1 - mean
        var = (
            jnp.sum(x0 * x0, -1, keepdims=True) + jnp.sum(x1 * x1, -1, keepdims=True)
        ) * (1.0 / D)
        inv = lax.rsqrt(var + EPS)
        n0 = (x0 * inv).astype(BF16)
        n1 = (x1 * inv).astype(BF16)
        half = 0.5 * (dot(n0, wh[:HALF]) + dot(n1, wh[HALF:]))
        proj = (half + half * jnp.tanh(half)).astype(BF16)
        kv_ref[2, rr] = proj[:, 2 * E :]
        near[slot].start()
        if slot in AROUND:
            hop[slot].start()
        nb[rr, :HALF] = n0
        nb[rr, HALF:] = n1
        inv_all[rr] = jnp.broadcast_to(inv, (CH, E))
        upv[rr] = proj[:, :E]
        qv[rr] = proj[:, E : 2 * E]
        for k, (src, dst) in enumerate(((nb, nb_ref), (inv_all, rs_ref), (upv, up_ref), (qv, q_ref))):
            store(k, slot, src.at[rr], dst.at[rr])

    def hand_on(slot):
        if slot in AROUND:
            hop[slot].wait_recv()
            direct[slot].start()
        else:
            near[slot].wait_recv()
            chained[slot].start()

    for i in range(NCH):
        x_copies[0, i].wait_recv()
        f_copies[0, i].start()
        compute(i)
        o_copies[0, i].wait_recv()
        f_copies[0, i].wait_recv()
        compute(NCH + i)
        if i:
            for slot in (i - 1, NCH + i - 1):
                near[slot].hand_on()
                if slot in AROUND:
                    hand_on(slot)
    for i in range(NCH):
        x_copies[1, i].start()
        o_copies[1, i].start()
    for slot in (NCH - 1, SLOTS - 1):
        near[slot].hand_on()
        if slot in AROUND:
            hand_on(slot)
    for slot in (0, NCH, 1):
        hand_on(slot)
    for i in range(NCH):
        x_copies[1, i].wait_recv()
        f_copies[1, i].start()
    for i in range(NCH):
        o_copies[1, i].wait_recv()
        f_copies[1, i].wait_recv()
    copy = pltpu.make_async_copy(cg, cg_ref, lcg.at[3])
    copy.start()
    stores.append(copy)
    for slot in range(SLOTS):
        if slot in AROUND:
            near[slot].wait_recv()
            direct[slot].wait_recv()
        else:
            chained[slot].wait_recv()
    for copies in (x_copies, o_copies, f_copies, near, hop, direct, chained):
        for copy in copies.values():
            copy.wait_send()
    for copy in stores:
        copy.wait()


def project(tokens, cotangent, w):
    vm = pl.BlockSpec(memory_space=pltpu.VMEM)
    hbm = pl.BlockSpec(memory_space=pl.ANY)
    dma = pltpu.SemaphoreType.DMA
    return pl.pallas_call(
        project_kernel,
        out_shape=(
            jax.ShapeDtypeStruct((D, 4 * E), BF16),
            jax.ShapeDtypeStruct((R, D), BF16),
            jax.ShapeDtypeStruct((R, E), F32),
            jax.ShapeDtypeStruct((R, E), BF16),
            jax.ShapeDtypeStruct((R, E), BF16),
            jax.ShapeDtypeStruct((3, R, 2 * E), BF16),
            jax.ShapeDtypeStruct((2, R, HALF), BF16),
        ),
        in_specs=[hbm] * 3,
        out_specs=(hbm,) * 5 + (vm, hbm),
        scratch_shapes=[
            pltpu.VMEM((2, R, HALF), BF16),
            pltpu.VMEM((SLOTS, CH, 2 * E), BF16),
            pltpu.VMEM((SLOTS, CH, 2 * E), BF16),
            pltpu.VMEM((8 * D, E), BF16),
            pltpu.VMEM((8 * D, E), F32),
            pltpu.VMEM((D, 4 * E), BF16),
            pltpu.VMEM((R, D), BF16),
            pltpu.VMEM((R, E), F32),
            pltpu.VMEM((R, E), BF16),
            pltpu.VMEM((R, E), BF16),
            pltpu.VMEM((2, R, HALF), BF16),
            dma((2, 3, NCH)),
            dma((2, 3, NCH)),
            dma((4, SLOTS)),
            dma((4, SLOTS)),
            dma((5, SLOTS)),
            dma((4,)),
        ],
        compiler_params=pltpu.CompilerParams(
            collective_id=0, has_side_effects=True, vmem_limit_bytes=VMEM_LIMIT
        ),
        cost_estimate=pl.CostEstimate(
            flops=2 * R * D * D, bytes_accessed=16 << 20, transcendentals=R * D
        ),
        name="gather_project",
    )(tokens, cotangent, w)


def attention_kernel(
    q_ref, kv_ref, up_ref, cg_ref, wo_all, all_ids,
    op_ref, gated_ref, dup_ref, dq_ref, dkv_ref, dfar_ref,
    id_ref, idc, acc,
):
    s = lax.axis_index("seq")
    chip = lax.div(s, 2)
    wo_ref = wo_all.at[lax.rem(s, 2)]
    t = pl.program_id(0)

    @pl.when(t == 0)
    def _():
        for b in range(3):
            source = chip - 2 + b
            ids = all_ids[rows_at(jnp.maximum(source, 0) * (R // E), R // E), :]
            ids = jnp.where(source >= 0, ids, -1)
            for j in range(R // E):
                at = b * R + j * E
                row = ids[j : j + 1, :]
                id_ref[0:1, at : at + E] = row
                idc[at : at + E, :] = jnp.broadcast_to(row, (E, E)).T

        @pl.loop(0, WIN // TK)
        def _(j):
            acc[rows_at(j * TK, TK), :] = jnp.zeros((TK, 2 * E), F32)

    def spread(column, width):
        return jnp.concatenate([column] * (width // E), axis=1)

    first = 2 * R // TK
    q = q_ref[...]
    wr = rows_at(2 * R + t * TQ, TQ)
    idq_col = idc[wr, :]
    idq_row = id_ref[0:1, wr]
    start = idq_row[0, 0]
    before = (id_ref[...] < start).astype(jnp.int32)
    low = jnp.sum(before) // TK
    last = first + t * TQ // TK
    uniform = start == idq_row[0, TQ - 1]
    mid = jnp.where(uniform, jnp.minimum(low + 1, last), last)

    def masked(half, ok, kt, causal, row_axis):
        if causal:
            ri = lax.broadcasted_iota(jnp.int32, half.shape, row_axis) + t * TQ
            ci = lax.broadcasted_iota(jnp.int32, half.shape, 1 - row_axis) + (kt - first) * TK
            ok = ok & (ci <= ri)
        return jnp.where(ok, half, OUT_OF_MASK)

    def forward(kt, total, mask=True, causal=False):
        kr = rows_at(kt * TK, TK)
        half = dot(q, kv_ref[kr, E:], NT) * (0.5 * SCALE)
        if mask:
            half = masked(half, spread(idq_col, TK) == id_ref[0:1, kr], kt, causal, 0)
        weights = (half + half * jnp.tanh(half)).astype(BF16)
        return total + dot(weights, kv_ref[kr, :E])

    def backward(kt, total, mask=True, causal=False):
        kr = rows_at(kt * TK, TK)
        k = kv_ref[kr, E:]
        half = dot(k, q, NT) * (0.5 * SCALE)
        if mask:
            half = masked(half, spread(idc[kr, :], TQ) == idq_row, kt, causal, 1)
        tan = jnp.tanh(half)
        weights = half + half * tan
        tan = 0.5 * tan
        slope = (0.5 + tan) + weights * (0.5 - tan)
        ds = (slope * dot(kv_ref[kr, :E], grad, NT)).astype(BF16)
        acc[kr, E:] += dot(ds, q)
        acc[kr, :E] += dot(weights.astype(BF16), grad)
        return total + dot(k.T, ds)

    def over_keys(step, shape=(TQ, E)):
        total = lax.fori_loop(low, mid, step, jnp.zeros(shape, F32))
        total = lax.fori_loop(mid, last, functools.partial(step, mask=False), total)
        for j in range(max(1, TQ // TK)):
            total = step(last + j, total, causal=True)
        return total

    att = over_keys(forward)
    center = att - jnp.mean(att, -1, keepdims=True)
    scale = lax.rsqrt(jnp.mean(center * center, -1, keepdims=True) + FLOOR)
    hn = center * scale
    up = up_ref[...].astype(F32)
    gated = (hn * up).astype(BF16)
    gated_ref[...] = gated
    op_ref[0] = dot(gated, wo_ref[:, :HALF]).astype(BF16)
    op_ref[1] = dot(gated, wo_ref[:, HALF:]).astype(BF16)
    gg = dot(cg_ref[0], wo_ref[:, :HALF], NT) + dot(cg_ref[1], wo_ref[:, HALF:], NT)
    dup_ref[...] = gg * hn
    b = gg * up
    grad = (
        scale * (b - jnp.mean(b, -1, keepdims=True) - hn * jnp.mean(b * hn, -1, keepdims=True))
    ).astype(BF16)
    dq_ref[...] = over_keys(backward, (E, TQ)).T * SCALE

    @pl.when(t == R // TQ - 1)
    def _():
        @pl.loop(0, R // TK)
        def _(j):
            rr = rows_at(j * TK, TK)
            own = rows_at(2 * R + j * TK, TK)
            dkv_ref[rr, :E] = acc[own, :E]
            dkv_ref[rr, E:] = acc[own, E:] * SCALE
            for k in range(2):
                src = rows_at(k * R + j * TK, TK)
                dfar_ref[k, rr, :E] = acc[src, :E].astype(BF16)
                dfar_ref[k, rr, E:] = (acc[src, E:] * SCALE).astype(BF16)


def attention(q, kv, up, cg, wo, ids):
    vm = pl.BlockSpec(memory_space=pltpu.VMEM)
    tile = pl.BlockSpec((TQ, E), lambda t: (t, 0))
    halves = pl.BlockSpec((2, TQ, HALF), lambda t: (0, t, 0))
    return pl.pallas_call(
        attention_kernel,
        grid=(R // TQ,),
        out_shape=(
            jax.ShapeDtypeStruct((2, R, HALF), BF16),
            jax.ShapeDtypeStruct((R, E), BF16),
            jax.ShapeDtypeStruct((R, E), F32),
            jax.ShapeDtypeStruct((R, E), F32),
            jax.ShapeDtypeStruct((R, 2 * E), F32),
            jax.ShapeDtypeStruct((2, R, 2 * E), BF16),
        ),
        in_specs=[tile, vm, tile, halves, vm, vm],
        out_specs=(
            halves,
            tile,
            tile,
            tile,
            pl.BlockSpec((R, 2 * E), lambda t: (0, 0)),
            pl.BlockSpec((2, R, 2 * E), lambda t: (0, 0, 0)),
        ),
        scratch_shapes=[
            pltpu.VMEM((1, WIN), jnp.int32),
            pltpu.VMEM((WIN, E), jnp.int32),
            pltpu.VMEM((WIN, 2 * E), F32),
        ],
        compiler_params=pltpu.CompilerParams(vmem_limit_bytes=VMEM_LIMIT),
        cost_estimate=pl.CostEstimate(
            flops=7 * 2 * R * R * 2 * E, bytes_accessed=16 << 20, transcendentals=4 * R * R
        ),
        name="attention",
    )(q, kv, up, cg, wo, ids)


class Summed:
    def __init__(self, me, rows, grads, bufs, sems, at):
        self.me, self.rows, self.grads, self.bufs = me, rows, grads, bufs
        self.sems, self.at = sems, at
        self.done = []

    def copy(self, src, dst, stage, k, device):
        copy = Copy(src, dst, self.sems, (self.at, stage, k), device).start()
        self.done.append(copy)
        return copy

    def peers(self, here, step):
        s, c = self.me.s, self.me.c
        there = [lax.rem(here + k, 4) for k in (1, 2, 3)]
        return [(v, (s + step * (v - here), c)) for v in there]

    def start(self):
        zbuf, zrecv = self.bufs[0:2]
        n = self.rows // 4
        zbuf[...] = self.grads[...].astype(BF16)
        self.zc = [
            self.copy(zbuf.at[rows_at(v * n, n)], zrecv.at[k], 0, k, device)
            for k, (v, device) in enumerate(self.peers(self.me.z, 8))
        ]

    def over_y(self):
        zrecv, yall = self.bufs[1:3]
        n = self.rows // 4
        for copy in self.zc:
            copy.wait_recv()
        total = self.grads[rows_at(self.me.z * n, n), :]
        for k in range(3):
            total = total + zrecv[k].astype(F32)
        spot = yall.at[self.me.y]
        spot[...] = total.astype(BF16)
        self.yc = [
            self.copy(spot, spot, 1, k, device) for k, (_, device) in enumerate(self.peers(self.me.y, 2))
        ]

    def over_x(self):
        yall, xall = self.bufs[2:4]
        for copy in self.yc:
            copy.wait_recv()
        total = (yall[0].astype(F32) + yall[1].astype(F32)) + (yall[2].astype(F32) + yall[3].astype(F32))
        spot = xall.at[self.me.xl]
        spot[...] = total.astype(BF16)
        self.xc = self.copy(spot, spot, 2, 0, self.me.xpeer)

    def back_z(self):
        xall, whole = self.bufs[3:5]
        me = self.me
        self.xc.wait_recv()
        spot = whole.at[me.core, me.z]
        spot[...] = (xall[0].astype(F32) + xall[1].astype(F32)).astype(BF16)
        self.gz = [
            self.copy(spot, spot, 3, k, device) for k, (_, device) in enumerate(self.peers(me.z, 8))
        ]
        self.gc = [self.copy(spot, spot, 4, 0, me.other)]

    def back_core(self):
        me = self.me
        for k in range(3):
            self.gz[k].wait_recv()
            spot = self.bufs[4].at[me.core, lax.rem(me.z + 3 - k, 4)]
            self.gc.append(self.copy(spot, spot, 4, k + 1, me.other))

    def finish(self):
        for copy in self.gc:
            copy.wait_recv()

    def wait_send(self):
        for copy in self.done:
            copy.wait_send()

    @staticmethod
    def scratch(rows):
        n = rows // 4
        return [
            pltpu.VMEM((rows, 2 * E), BF16),
            pltpu.VMEM((3, n, 2 * E), BF16),
            pltpu.VMEM((4, n, 2 * E), BF16),
            pltpu.VMEM((2, n, 2 * E), BF16),
        ]


EARLY = D + 2 * E
INV_ROOT = 1.0 / 256.0


def gradient_kernel(
    tok_in, cot_in, w_in, nb_in, rs_in, cg_in, gated_in, op_in, dup_in, dq_in, dkv_in, dfar_in,
    out_ref, gt_ref, early_all, late_all,
    tok_ref, cot_ref, w_ref, nb_ref, rs_ref, cg_ref, gated_ref, op_ref, dup_ref, dq_ref, dkv_ref, dfar_ref, ls,
    hopped, back, yvia, nvia, slope, gp, part, chip_sum, to_col, from_col, early_g, late_g, *rest,
):
    early_bufs, late_bufs = rest[:4] + (early_all,), rest[4:8] + (late_all,)
    bss, brs, sss, srs, ass, ars = rest[8:]
    me = Place()
    c, core, chip = me.c, me.core, me.chip
    behind = me.at_chip(chip - 1)
    round_to = me.at_chip(me.in_ring(1))
    source = me.in_ring(-1)
    handed_to = me.at_chip(source - 2)
    two_on = lax.rem(chip + 2, CHIPS)
    two_y = lax.rem(two_on, 4)
    hander = me.at_chip(two_on - two_y + lax.rem(two_y + 1, 4))
    early = Summed(me, EARLY, early_g, early_bufs, (ass, ars), 0)
    late = Summed(me, D, late_g, late_bufs, (ass, ars), 1)
    greet(
        [me.other, me.far, me.at_chip(chip + 1), me.at_chip(chip + 4), round_to, me.at_chip(source)]
        + [hander, me.xpeer]
        + [device for _, device in early.peers(me.y, 2) + early.peers(me.z, 8)],
        14,
    )

    base = core * T
    obase = (1 - core) * T

    order = (
        (nb_in, nb_ref), (w_in, w_ref), (dup_in, dup_ref), (dq_in, dq_ref), (gated_in, gated_ref),
        (cg_in, cg_ref), (op_in.at[:, rows_at(base, T)], op_ref), (dfar_in.at[1], dfar_ref),
        (dkv_in, dkv_ref), (rs_in, rs_ref), (tok_in, tok_ref), (cot_in, cot_ref),
    )
    loads = [pltpu.make_async_copy(src, dst, ls.at[k]) for k, (src, dst) in enumerate(order)]

    def mine_of(kind, half, i):
        if kind == 0:
            return op_ref[half, pl.ds(i * CH, CH)]
        return part[half, rows_at(base + i * CH, CH)]

    def to_core(kind, i):
        src = (op_in, part)[kind].at[:, rows_at(obase + i * CH, CH)]
        dst = chip_sum.at[kind, :, pl.ds(i * CH, CH)]
        return Copy(src, dst, (sss, srs), (kind, 0, i), me.other).start()

    def across(kind, i, copy):
        copy.wait_recv()
        here = pl.ds(i * CH, CH)
        mine = mine_of(kind, 1 - c, i).astype(F32)
        to_col[kind, here] = (mine + chip_sum[kind, 1 - c, here].astype(F32)).astype(BF16)
        return Copy(
            to_col.at[kind, here], from_col.at[kind, here], (sss, srs), (kind, 1, i), me.far
        ).start()

    def finish(kind, i, copy):
        copy.wait_recv()
        here = pl.ds(i * CH, CH)
        own, out = ((tok_ref, out_ref), (cot_ref, gt_ref))[kind]
        total = mine_of(kind, c, i).astype(F32)
        total = total + chip_sum[kind, c, here].astype(F32)
        total = total + from_col[kind, here].astype(F32)
        out[here] = (own[here].astype(F32) + total).astype(BF16)

    near, hop, direct = {}, {}, {}
    for i in range(SLOTS):
        rr = pl.ds(i * CH, CH)
        near[i] = Near(
            me, -1, dfar_in.at[1, rr] if i in AROUND else back.at[2, rr], nvia.at[i], back.at[1, rr],
            (bss, brs), (i,),
        )
        if i in AROUND:
            hop[i] = Copy(
                dfar_in.at[0, rr], yvia.at[i], (bss, brs), (2, i), round_to, chip > 1, source > 1
            )
            direct[i] = Copy(
                yvia.at[i], back.at[0, rr], (bss, brs), (3, i), handed_to, source > 1, chip < CHIPS - 2
            )
        else:
            hop[i] = Copy(
                dfar_in.at[0, rr], hopped.at[i], (bss, brs), (2, i), behind,
                chip > 1, (chip > 0) & (chip < CHIPS - 1),
            )
    joined = [i for i in range(SLOTS) if i not in AROUND]
    for i in joined:
        hop[i].start()
    for i in AROUND:
        hop[i].start()
        near[i].start()
    for copy in loads:
        copy.start()
    out_core = [to_core(0, i) for i in range(NCH)]

    SR = 512
    for copy in loads[:4]:
        copy.wait()

    @pl.loop(0, R // SR)
    def _(i):
        rr = rows_at(i * SR, SR)
        half = 0.5 * dot(nb_ref[rr, :], w_ref[...])
        tan = jnp.tanh(half)
        silu = half + half * tan
        tan = 0.5 * tan
        sl = (0.5 + tan) + silu * (0.5 - tan)
        gp[rr, :E] = (dup_ref[rr, :] * sl[:, :E]).astype(BF16)
        gp[rr, E : 2 * E] = (dq_ref[rr, :] * sl[:, E : 2 * E]).astype(BF16)
        slope[rr, :] = sl[:, 2 * E :]

    for copy in loads[4:6]:
        copy.wait()
    early_g[:D, :] = dot(nb_ref[...], gp[:, : 2 * E], TN)
    for j in range(2):
        early_g[D + j * E : D + (j + 1) * E, :] = dot(gated_ref[...], cg_ref[j], TN)
    early.start()

    for copy in loads[6:]:
        copy.wait()
    out_far = [across(0, i, out_core[i]) for i in range(NCH)]

    for i in joined:
        rr = pl.ds(i * CH, CH)
        back[2, rr] = dfar_ref[rr]

        @pl.when((chip > 0) & (chip < CHIPS - 1))
        def _():
            hop[i].copy.wait_recv()
            back[2, rr] = (dfar_ref[rr].astype(F32) + hopped[i].astype(F32)).astype(BF16)

        near[i].start()
    for i in AROUND:
        hop[i].wait_recv()
        direct[i].start()
    for i in list(AROUND) + joined:
        near[i].hand_on()
    early.over_y()

    for i in list(AROUND) + joined:
        rr = pl.ds(i * CH, CH)
        near[i].wait_recv()

        @pl.when(chip == CHIPS - 1)
        def _():
            back[1, rr] = jnp.zeros((CH, 2 * E), BF16)

        g = dkv_ref[rr, :]
        if i in AROUND:
            direct[i].wait_recv()

            @pl.when(chip >= CHIPS - 2)
            def _():
                back[0, rr] = jnp.zeros((CH, 2 * E), BF16)

            g = g + back[0, rr].astype(F32)
        gp[rr, 2 * E :] = ((g + back[1, rr].astype(F32)) * slope[rr, :]).astype(BF16)

    late_g[...] = dot(nb_ref[...], gp[:, 2 * E :], TN)
    late.start()
    early.over_x()

    def tokens_back(start):
        rr = rows_at(start, CH)
        g = dot(gp[rr, :], w_ref[...], NT)
        nb = nb_ref[rr, :].astype(F32)
        inv = rs_ref[rr, 0:1]
        g = inv * (g - jnp.mean(g, -1, keepdims=True) - nb * jnp.mean(g * nb, -1, keepdims=True))
        part[0, rr] = g[:, :HALF].astype(BF16)
        part[1, rr] = g[:, HALF:].astype(BF16)

    gt_core = []
    for i in range(NCH):
        tokens_back(obase + i * CH)
        gt_core.append(to_core(1, i))
    early.back_z()
    gt_far = []
    for i in range(NCH):
        tokens_back(base + i * CH)
        gt_far.append(across(1, i, gt_core[i]))
    late.over_y()
    for i in range(NCH):
        finish(0, i, out_far[i])
    early.back_core()
    late.over_x()
    late.back_z()
    early.finish()
    late.back_core()
    for i in range(NCH):
        finish(1, i, gt_far[i])
    late.finish()
    for copies in (near, hop, direct):
        for copy in copies.values():
            copy.wait_send()
    for copy in out_core + out_far + gt_core + gt_far + [early, late]:
        copy.wait_send()


def gradients(*operands):
    vm = pl.BlockSpec(memory_space=pltpu.VMEM)
    hbm = pl.BlockSpec(memory_space=pl.ANY)
    dma = pltpu.SemaphoreType.DMA
    loaded = [list(x.shape) for x in operands]
    loaded[7][1] = T
    loaded[11] = [R, 2 * E]
    return pl.pallas_call(
        gradient_kernel,
        out_shape=(
            jax.ShapeDtypeStruct((T, HALF), BF16),
            jax.ShapeDtypeStruct((T, HALF), BF16),
            jax.ShapeDtypeStruct((2, 4, EARLY // 4, 2 * E), BF16),
            jax.ShapeDtypeStruct((2, 4, D // 4, 2 * E), BF16),
        ),
        in_specs=[hbm] * 12,
        out_specs=(vm,) * 4,
        scratch_shapes=[pltpu.VMEM(tuple(d), x.dtype) for d, x in zip(loaded, operands)]
        + [
            dma((12,)),
            pltpu.VMEM((SLOTS, CH, 2 * E), BF16),
            pltpu.VMEM((3, R, 2 * E), BF16),
            pltpu.VMEM((SLOTS, CH, 2 * E), BF16),
            pltpu.VMEM((SLOTS, CH, 2 * E), BF16),
            pltpu.VMEM((R, 2 * E), F32),
            pltpu.VMEM((R, 4 * E), BF16),
            pltpu.VMEM((2, R, HALF), BF16),
            pltpu.VMEM((2, 2, T, HALF), BF16),
            pltpu.VMEM((2, T, HALF), BF16),
            pltpu.VMEM((2, T, HALF), BF16),
            pltpu.VMEM((EARLY, 2 * E), F32),
            pltpu.VMEM((D, 2 * E), F32),
        ]
        + Summed.scratch(EARLY)
        + Summed.scratch(D)
        + [
            dma((4, SLOTS)),
            dma((4, SLOTS)),
            dma((2, 2, NCH)),
            dma((2, 2, NCH)),
            dma((2, 5, 4)),
            dma((2, 5, 4)),
        ],
        compiler_params=pltpu.CompilerParams(
            collective_id=1, has_side_effects=True, vmem_limit_bytes=VMEM_LIMIT
        ),
        cost_estimate=pl.CostEstimate(
            flops=7 * R * D * D, bytes_accessed=16 << 20, transcendentals=R * D
        ),
        name="gradients",
    )(*operands)


def widen_kernel(out_in, gt_in, early_ref, late_ref, out_ref, gt_ref, gwi_ref, gwo_ref):
    out_ref[...] = out_in[...]
    gt_ref[...] = gt_in[...]
    n = EARLY // 4
    for h in range(2):
        for z in range(4):
            at = 0
            while at < n:
                d = z * n + at
                end = next(b for b in (D, D + E, EARLY) if b > d)
                size = min(n - at, end - d)
                piece = early_ref[h, z, at : at + size, :].astype(F32) * INV_ROOT
                if d < D:
                    for j in range(2):
                        gwi_ref[pl.ds(8 * d + 4 * j + h, size, stride=8), :] = piece[:, j * E : (j + 1) * E]
                else:
                    q, e = divmod(d - D, E)
                    gwo_ref[h, e : e + size, q * HALF : (q + 1) * HALF] = piece
                at += size
            m = D // 4
            piece = late_ref[h, z].astype(F32) * INV_ROOT
            for j in range(2):
                gwi_ref[pl.ds(8 * z * m + 4 * j + 2 + h, m, stride=8), :] = piece[:, j * E : (j + 1) * E]


def widen(out, gt, early, late):
    vm = pl.BlockSpec(memory_space=pltpu.VMEM)
    return pl.pallas_call(
        widen_kernel,
        out_shape=(
            jax.ShapeDtypeStruct((T, HALF), BF16),
            jax.ShapeDtypeStruct((T, HALF), BF16),
            jax.ShapeDtypeStruct((8 * D, E), F32),
            jax.ShapeDtypeStruct((2, E, D), F32),
        ),
        in_specs=[vm] * 4,
        out_specs=(vm,) * 4,
        compiler_params=pltpu.CompilerParams(vmem_limit_bytes=VMEM_LIMIT),
        name="widen",
    )(out, gt, early, late)


def shards(tokens, cotangent, weight_in, weight_out, history_ids):
    w, nb, inv, q, up, kv, cg = project(tokens, cotangent, weight_in.reshape(8 * D, E))
    op, gated, dup, dq, dkv, dfar = attention(
        q, kv.reshape(WIN, 2 * E), up, cg, weight_out, history_ids.reshape(-1, E)
    )
    out, gt, gwi, gwo = widen(
        *gradients(tokens, cotangent, w, nb, inv, cg, gated, op, dup, dq, dkv, dfar)
    )
    return out, gt, gwi.reshape(D, 4, 2, E), gwo


def solution(mesh):
    placed = (
        P("seq", "col"),
        P("seq", "col"),
        P(None, None, "col", None),
        P("col", None, None),
        P(),
    )
    return jax.shard_map(
        shards,
        mesh=mesh,
        in_specs=placed,
        out_specs=(
            P("seq", "col"),
            P("seq", "col"),
            P(None, None, "col", None),
            P("col", None, None),
        ),
        check_vma=False,
    )
```

```python
import functools
import math

import jax
import jax.numpy as jnp
from jax import lax
from jax.experimental import pallas as pl
from jax.experimental.pallas import tpu as pltpu
from jax.sharding import PartitionSpec as P

MESH = pl.DeviceIdType.MESH
F32 = jnp.float32
BF16 = jnp.bfloat16

T = 1024
R = 2 * T
D = 512
E = 128
HALF = D // 2
CH = 256
NCH = T // CH
TQ = 512
TK = 512
WIN = 3 * R
EPS = 1e-5
FLOOR = 1.0
SCALE = E**-0.5
OUT_OF_MASK = -32.0
SLOTS = R // CH
AROUND = (2, 3, 5, 6, 7)
BACK_AROUND = (4, 5, 6, 7, 0)
CHIPS = 32
VMEM_LIMIT = 56 * 1024 * 1024

NT = (((1,), (1,)), ((), ()))
TN = (((0,), (0,)), ((), ()))


def dot(a, b, dims=(((1,), (0,)), ((), ()))):
    return lax.dot_general(a, b, dims, preferred_element_type=F32)


def guarded(on, act):
    if on is None:
        act()
    else:
        pl.when(on)(act)


class Copy:
    def __init__(self, src, dst, sems, at, device, on=None, arrives=None):
        self.on, self.arrives = on, arrives
        self.copy = pltpu.make_async_remote_copy(
            src_ref=src,
            dst_ref=dst,
            send_sem=sems[0].at[at],
            recv_sem=sems[1].at[at],
            device_id=device,
            device_id_type=MESH,
        )

    def start(self):
        guarded(self.on, self.copy.start)
        return self

    def wait_recv(self):
        guarded(self.arrives, self.copy.wait_recv)

    def wait_send(self):
        guarded(self.on, self.copy.wait_send)


def rows_at(start, size):
    return pl.ds(pl.multiple_of(start, size), size)


class Place:
    def __init__(self):
        s, c = lax.axis_index("seq"), lax.axis_index("col")
        self.s, self.c = s, c
        self.core = lax.rem(s, 2)
        self.chip = lax.div(s, 2)
        self.y = lax.rem(self.chip, 4)
        self.z = lax.rem(lax.div(s, 8), 4)
        self.xl = lax.div(s, 32)
        self.other = (s + 1 - 2 * self.core, c)
        self.far = (s, 1 - c)
        self.xpeer = (s + 32 - 64 * self.xl, c)

    def at_chip(self, chip):
        return (2 * lax.rem(chip + 2 * CHIPS, CHIPS) + self.core, self.c)

    def in_ring(self, step):
        return self.chip - self.y + lax.rem(self.y + 4 + step, 4)


def greet(senders, count):
    barrier = pltpu.get_barrier_semaphore()
    for device in senders:
        pl.semaphore_signal(barrier, inc=1, device_id=device, device_id_type=MESH)
    pl.semaphore_wait(barrier, count)


class Near:
    def __init__(self, me, step, src, via, dst, sems, at):
        edge = 3 if step > 0 else 0
        first, last = (0, CHIPS - 1) if step > 0 else (CHIPS - 1, 0)
        cross = me.y == edge
        goes = me.chip != last
        self.comes = me.chip != first
        self.straight = Copy(src, dst, sems, (0,) + at, me.at_chip(me.chip + step), goes & ~cross, self.comes)
        beyond = me.chip > 3 if step > 0 else me.chip < CHIPS - 4
        self.aside = Copy(
            src, via, sems, (1,) + at, me.at_chip(me.chip + 4 * step), goes & cross, beyond & cross
        )
        self.onward = Copy(via, dst, sems, (0,) + at, me.at_chip(me.in_ring(step)), beyond & cross)

    def start(self):
        self.straight.start()
        self.aside.start()

    def hand_on(self):
        self.aside.wait_recv()
        self.onward.start()

    def wait_recv(self):
        self.straight.wait_recv()

    def wait_send(self):
        for copy in (self.straight, self.aside, self.onward):
            copy.wait_send()


def project_kernel(
    tok_ref, cot_ref, w_ref,
    wh_ref, nb_ref, rs_ref, q_ref, up_ref, kv_ref, cg_ref,
    xg, yvia, nvia, wv, wf, wh, nb, inv_all, qv, upv, cg, oss, ors, kss, krs, ls, lcg,
):
    me = Place()
    c, core, chip = me.c, me.core, me.chip
    ahead = me.at_chip(chip + 1)
    round_to = me.at_chip(me.in_ring(-1))
    source = me.in_ring(1)
    handed_to = me.at_chip(source + 2)
    two_back = lax.rem(chip + CHIPS - 2, CHIPS)
    two_y = lax.rem(two_back, 4)
    hander = me.at_chip(two_back - two_y + lax.rem(two_y + 3, 4))
    greet(
        [me.other, me.far, me.at_chip(chip - 1), me.at_chip(chip - 4), round_to, me.at_chip(source), hander],
        7,
    )

    base = core * T
    obase = (1 - core) * T

    bufs = (xg, cg)
    srcs = (tok_ref, cot_ref)
    x_copies, o_copies, f_copies = {}, {}, {}
    for kind in (0, 1):
        for i in range(NCH):
            rr = rows_at(base + i * CH, CH)
            x_copies[kind, i] = Copy(
                srcs[kind].at[pl.ds(i * CH, CH)], bufs[kind].at[c, rr], (oss, ors), (kind, 2, i), me.far
            )
            o_copies[kind, i] = Copy(
                srcs[kind].at[pl.ds(i * CH, CH)], bufs[kind].at[c, rr], (oss, ors), (kind, 0, i), me.other
            )
            where = bufs[kind].at[1 - c, rr]
            f_copies[kind, i] = Copy(where, where, (oss, ors), (kind, 1, i), me.other)

    for i in range(NCH):
        x_copies[0, i].start()
        o_copies[0, i].start()
    loads = [
        pltpu.make_async_copy(src, dst, lcg.at[k])
        for k, (src, dst) in enumerate(
            (
                (w_ref, wv),
                (tok_ref, xg.at[c, rows_at(base, T)]),
                (cot_ref, cg.at[c, rows_at(base, T)]),
            )
        )
    ]
    for copy in loads:
        copy.start()
    for copy in loads:
        copy.wait()
    stores = []

    def store(k, slot, src, dst):
        copy = pltpu.make_async_copy(src, dst, ls.at[k, slot])
        copy.start()
        stores.append(copy)

    wf[...] = wv[...].astype(F32)
    for place, part in enumerate((0, 2, 1, 3)):
        lanes = slice(place * E, (place + 1) * E)
        first = wf[pl.ds(2 * part, D, stride=8), :]
        second = wf[pl.ds(2 * part + 1, D, stride=8), :]
        wh[:, lanes] = jnp.where(core == 0, first, second).astype(BF16)
    store(4, 0, wh, wh_ref)

    near, hop, direct, chained = {}, {}, {}, {}
    for slot in range(SLOTS):
        rr = rows_at((base if slot < NCH else obase) + slot % NCH * CH, CH)
        mine = kv_ref.at[2, rr]
        near[slot] = Near(me, 1, mine, nvia.at[slot], kv_ref.at[1, rr], (kss, krs), (slot,))
        if slot in AROUND:
            hop[slot] = Copy(
                mine, yvia.at[slot], (kss, krs), (2, slot), round_to,
                chip < CHIPS - 2, source < CHIPS - 2,
            )
            direct[slot] = Copy(
                yvia.at[slot], kv_ref.at[0, rr], (kss, krs), (3, slot), handed_to,
                source < CHIPS - 2, chip > 1,
            )
        else:
            chained[slot] = Copy(
                kv_ref.at[1, rr], kv_ref.at[0, rr], (kss, krs), (3, slot), ahead,
                (chip > 0) & (chip < CHIPS - 1), chip > 1,
            )

    def compute(slot):
        rr = rows_at((base if slot < NCH else obase) + slot % NCH * CH, CH)
        x0 = xg[0, rr].astype(F32)
        x1 = xg[1, rr].astype(F32)
        mean = (jnp.sum(x0, -1, keepdims=True) + jnp.sum(x1, -1, keepdims=True)) * (1.0 / D)
        x0 = x0 - mean
        x1 = x1 - mean
        var = (
            jnp.sum(x0 * x0, -1, keepdims=True) + jnp.sum(x1 * x1, -1, keepdims=True)
        ) * (1.0 / D)
        inv = lax.rsqrt(var + EPS)
        n0 = (x0 * inv).astype(BF16)
        n1 = (x1 * inv).astype(BF16)
        half = 0.5 * (dot(n0, wh[:HALF]) + dot(n1, wh[HALF:]))
        proj = (half + half * jnp.tanh(half)).astype(BF16)
        kv_ref[2, rr] = proj[:, 2 * E :]
        near[slot].start()
        if slot in AROUND:
            hop[slot].start()
        nb[rr, :HALF] = n0
        nb[rr, HALF:] = n1
        inv_all[rr] = jnp.broadcast_to(inv, (CH, E))
        upv[rr] = proj[:, :E]
        qv[rr] = proj[:, E : 2 * E]
        for k, (src, dst) in enumerate(((nb, nb_ref), (inv_all, rs_ref), (upv, up_ref), (qv, q_ref))):
            store(k, slot, src.at[rr], dst.at[rr])

    def hand_on(slot):
        if slot in AROUND:
            hop[slot].wait_recv()
            direct[slot].start()
        else:
            near[slot].wait_recv()
            chained[slot].start()

    for i in range(NCH):
        x_copies[0, i].wait_recv()
        f_copies[0, i].start()
        compute(i)
        o_copies[0, i].wait_recv()
        f_copies[0, i].wait_recv()
        compute(NCH + i)
        if i:
            for slot in (i - 1, NCH + i - 1):
                near[slot].hand_on()
                if slot in AROUND:
                    hand_on(slot)
    for i in range(NCH):
        x_copies[1, i].start()
        o_copies[1, i].start()
    for slot in (NCH - 1, SLOTS - 1):
        near[slot].hand_on()
        if slot in AROUND:
            hand_on(slot)
    for slot in (0, NCH, 1):
        hand_on(slot)
    for i in range(NCH):
        x_copies[1, i].wait_recv()
        f_copies[1, i].start()
    for i in range(NCH):
        o_copies[1, i].wait_recv()
        f_copies[1, i].wait_recv()
    copy = pltpu.make_async_copy(cg, cg_ref, lcg.at[3])
    copy.start()
    stores.append(copy)
    for slot in range(SLOTS):
        if slot in AROUND:
            near[slot].wait_recv()
            direct[slot].wait_recv()
        else:
            chained[slot].wait_recv()
    for copies in (x_copies, o_copies, f_copies, near, hop, direct, chained):
        for copy in copies.values():
            copy.wait_send()
    for copy in stores:
        copy.wait()


def project(tokens, cotangent, w):
    vm = pl.BlockSpec(memory_space=pltpu.VMEM)
    hbm = pl.BlockSpec(memory_space=pl.ANY)
    dma = pltpu.SemaphoreType.DMA
    return pl.pallas_call(
        project_kernel,
        out_shape=(
            jax.ShapeDtypeStruct((D, 4 * E), BF16),
            jax.ShapeDtypeStruct((R, D), BF16),
            jax.ShapeDtypeStruct((R, E), F32),
            jax.ShapeDtypeStruct((R, E), BF16),
            jax.ShapeDtypeStruct((R, E), BF16),
            jax.ShapeDtypeStruct((3, R, 2 * E), BF16),
            jax.ShapeDtypeStruct((2, R, HALF), BF16),
        ),
        in_specs=[hbm] * 3,
        out_specs=(hbm,) * 5 + (vm, hbm),
        scratch_shapes=[
            pltpu.VMEM((2, R, HALF), BF16),
            pltpu.VMEM((SLOTS, CH, 2 * E), BF16),
            pltpu.VMEM((SLOTS, CH, 2 * E), BF16),
            pltpu.VMEM((8 * D, E), BF16),
            pltpu.VMEM((8 * D, E), F32),
            pltpu.VMEM((D, 4 * E), BF16),
            pltpu.VMEM((R, D), BF16),
            pltpu.VMEM((R, E), F32),
            pltpu.VMEM((R, E), BF16),
            pltpu.VMEM((R, E), BF16),
            pltpu.VMEM((2, R, HALF), BF16),
            dma((2, 3, NCH)),
            dma((2, 3, NCH)),
            dma((4, SLOTS)),
            dma((4, SLOTS)),
            dma((5, SLOTS)),
            dma((4,)),
        ],
        compiler_params=pltpu.CompilerParams(
            collective_id=0, has_side_effects=True, vmem_limit_bytes=VMEM_LIMIT
        ),
        cost_estimate=pl.CostEstimate(
            flops=2 * R * D * D, bytes_accessed=16 << 20, transcendentals=R * D
        ),
        name="gather_project",
    )(tokens, cotangent, w)


def attention_kernel(
    q_ref, kv_ref, up_ref, cg_ref, wo_all, all_ids,
    op_ref, gated_ref, dup_ref, dq_ref, dkv_ref, dfar_ref,
    id_ref, idc, acc, tot, tot_t,
):
    s = lax.axis_index("seq")
    chip = lax.div(s, 2)
    wo_ref = wo_all.at[lax.rem(s, 2)]
    t = pl.program_id(0)

    @pl.when(t == 0)
    def _():
        for b in range(3):
            source = chip - 2 + b
            ids = all_ids[rows_at(jnp.maximum(source, 0) * (R // E), R // E), :]
            ids = jnp.where(source >= 0, ids, -1)
            for j in range(R // E):
                at = b * R + j * E
                row = ids[j : j + 1, :]
                id_ref[0:1, at : at + E] = row
                idc[at : at + E, :] = jnp.broadcast_to(row, (E, E)).T

        @pl.loop(0, WIN // TK)
        def _(j):
            acc[rows_at(j * TK, TK), :] = jnp.zeros((TK, 2 * E), F32)

    def spread(column, width):
        return jnp.concatenate([column] * (width // E), axis=1)

    first = 2 * R // TK
    q = q_ref[...]
    wr = rows_at(2 * R + t * TQ, TQ)
    idq_col = idc[wr, :]
    idq_row = id_ref[0:1, wr]
    start = idq_row[0, 0]
    before = (id_ref[...] < start).astype(jnp.int32)
    low = jnp.sum(before) // TK
    last = first + t * TQ // TK
    uniform = start == idq_row[0, TQ - 1]
    mid = jnp.where(uniform, jnp.minimum(low + 1, last), last)

    def masked(half, ok, kt, causal, row_axis):
        if causal:
            ri = lax.broadcasted_iota(jnp.int32, half.shape, row_axis) + t * TQ
            ci = lax.broadcasted_iota(jnp.int32, half.shape, 1 - row_axis) + (kt - first) * TK
            ok = ok & (ci <= ri)
        return jnp.where(ok, half, OUT_OF_MASK)

    def forward(kt, mask=True, causal=False):
        kr = rows_at(kt * TK, TK)
        half = dot(q, kv_ref[kr, E:], NT) * (0.5 * SCALE)
        if mask:
            half = masked(half, spread(idq_col, TK) == id_ref[0:1, kr], kt, causal, 0)
        weights = (half + half * jnp.tanh(half)).astype(BF16)
        tot[...] += dot(weights, kv_ref[kr, :E])

    def backward(kt, mask=True, causal=False):
        kr = rows_at(kt * TK, TK)
        k = kv_ref[kr, E:]
        half = dot(k, q, NT) * (0.5 * SCALE)
        if mask:
            half = masked(half, spread(idc[kr, :], TQ) == idq_row, kt, causal, 1)
        tan = jnp.tanh(half)
        weights = half + half * tan
        tan = 0.5 * tan
        slope = (0.5 + tan) + weights * (0.5 - tan)
        ds = (slope * dot(kv_ref[kr, :E], grad, NT)).astype(BF16)
        acc[kr, E:] += dot(ds, q)
        acc[kr, :E] += dot(weights.astype(BF16), grad)
        tot_t[...] += dot(k.T, ds)

    def over_keys(step, total):
        total[...] = jnp.zeros_like(total)

        @pl.loop(low, mid)
        def _(kt):
            step(kt)

        @pl.loop(mid, last)
        def _(kt):
            step(kt, mask=False)

        for j in range(max(1, TQ // TK)):
            step(last + j, causal=True)
        return total[...]

    att = over_keys(forward, tot)
    center = att - jnp.mean(att, -1, keepdims=True)
    scale = lax.rsqrt(jnp.mean(center * center, -1, keepdims=True) + FLOOR)
    hn = center * scale
    up = up_ref[...].astype(F32)
    gated = (hn * up).astype(BF16)
    gated_ref[...] = gated
    op_ref[0] = dot(gated, wo_ref[:, :HALF]).astype(BF16)
    op_ref[1] = dot(gated, wo_ref[:, HALF:]).astype(BF16)
    gg = dot(cg_ref[0], wo_ref[:, :HALF], NT) + dot(cg_ref[1], wo_ref[:, HALF:], NT)
    dup_ref[...] = gg * hn
    b = gg * up
    grad = (
        scale * (b - jnp.mean(b, -1, keepdims=True) - hn * jnp.mean(b * hn, -1, keepdims=True))
    ).astype(BF16)
    dq_ref[...] = over_keys(backward, tot_t).T * SCALE

    @pl.when(t == R // TQ - 1)
    def _():
        @pl.loop(0, R // TK)
        def _(j):
            rr = rows_at(j * TK, TK)
            own = rows_at(2 * R + j * TK, TK)
            dkv_ref[rr, :E] = acc[own, :E]
            dkv_ref[rr, E:] = acc[own, E:] * SCALE
            for k in range(2):
                src = rows_at(k * R + j * TK, TK)
                dfar_ref[k, rr, :E] = acc[src, :E].astype(BF16)
                dfar_ref[k, rr, E:] = (acc[src, E:] * SCALE).astype(BF16)


def attention(q, kv, up, cg, wo, ids):
    vm = pl.BlockSpec(memory_space=pltpu.VMEM)
    tile = pl.BlockSpec((TQ, E), lambda t: (t, 0))
    halves = pl.BlockSpec((2, TQ, HALF), lambda t: (0, t, 0))
    return pl.pallas_call(
        attention_kernel,
        grid=(R // TQ,),
        out_shape=(
            jax.ShapeDtypeStruct((2, R, HALF), BF16),
            jax.ShapeDtypeStruct((R, E), BF16),
            jax.ShapeDtypeStruct((R, E), F32),
            jax.ShapeDtypeStruct((R, E), F32),
            jax.ShapeDtypeStruct((R, 2 * E), F32),
            jax.ShapeDtypeStruct((2, R, 2 * E), BF16),
        ),
        in_specs=[tile, vm, tile, halves, vm, vm],
        out_specs=(
            halves,
            tile,
            tile,
            tile,
            pl.BlockSpec((R, 2 * E), lambda t: (0, 0)),
            pl.BlockSpec((2, R, 2 * E), lambda t: (0, 0, 0)),
        ),
        scratch_shapes=[
            pltpu.VMEM((1, WIN), jnp.int32),
            pltpu.VMEM((WIN, E), jnp.int32),
            pltpu.VMEM((WIN, 2 * E), F32),
            pltpu.VMEM((TQ, E), F32),
            pltpu.VMEM((E, TQ), F32),
        ],
        compiler_params=pltpu.CompilerParams(vmem_limit_bytes=VMEM_LIMIT),
        cost_estimate=pl.CostEstimate(
            flops=7 * 2 * R * R * 2 * E, bytes_accessed=16 << 20, transcendentals=4 * R * R
        ),
        name="attention",
    )(q, kv, up, cg, wo, ids)


class Summed:
    def __init__(self, me, rows, grads, bufs, sems, at):
        self.me, self.rows, self.grads, self.bufs = me, rows, grads, bufs
        self.sems, self.at = sems, at
        self.done = []

    def copy(self, src, dst, stage, k, device):
        copy = Copy(src, dst, self.sems, (self.at, stage, k), device).start()
        self.done.append(copy)
        return copy

    def peers(self, here, step):
        s, c = self.me.s, self.me.c
        there = [lax.rem(here + k, 4) for k in (1, 2, 3)]
        return [(v, (s + step * (v - here), c)) for v in there]

    def start(self):
        zbuf, zrecv = self.bufs[0:2]
        n = self.rows // 4
        zbuf[...] = self.grads[...].astype(BF16)
        self.zc = [
            self.copy(zbuf.at[rows_at(v * n, n)], zrecv.at[k], 0, k, device)
            for k, (v, device) in enumerate(self.peers(self.me.z, 8))
        ]

    def over_y(self):
        zrecv, yall = self.bufs[1:3]
        n = self.rows // 4
        for copy in self.zc:
            copy.wait_recv()
        total = self.grads[rows_at(self.me.z * n, n), :]
        for k in range(3):
            total = total + zrecv[k].astype(F32)
        spot = yall.at[self.me.y]
        spot[...] = total.astype(BF16)
        self.yc = [
            self.copy(spot, spot, 1, k, device) for k, (_, device) in enumerate(self.peers(self.me.y, 2))
        ]

    def over_x(self):
        yall, xall = self.bufs[2:4]
        for copy in self.yc:
            copy.wait_recv()
        total = (yall[0].astype(F32) + yall[1].astype(F32)) + (yall[2].astype(F32) + yall[3].astype(F32))
        spot = xall.at[self.me.xl]
        spot[...] = total.astype(BF16)
        self.xc = self.copy(spot, spot, 2, 0, self.me.xpeer)

    def back_z(self):
        xall, whole = self.bufs[3:5]
        me = self.me
        self.xc.wait_recv()
        spot = whole.at[me.core, me.z]
        spot[...] = (xall[0].astype(F32) + xall[1].astype(F32)).astype(BF16)
        self.gz = [
            self.copy(spot, spot, 3, k, device) for k, (_, device) in enumerate(self.peers(me.z, 8))
        ]
        self.gc = [self.copy(spot, spot, 4, 0, me.other)]

    def back_core(self):
        me = self.me
        for k in range(3):
            self.gz[k].wait_recv()
            spot = self.bufs[4].at[me.core, lax.rem(me.z + 3 - k, 4)]
            self.gc.append(self.copy(spot, spot, 4, k + 1, me.other))

    def finish(self):
        for copy in self.gc:
            copy.wait_recv()

    def wait_send(self):
        for copy in self.done:
            copy.wait_send()

    @staticmethod
    def scratch(rows):
        n = rows // 4
        return [
            pltpu.VMEM((rows, 2 * E), BF16),
            pltpu.VMEM((3, n, 2 * E), BF16),
            pltpu.VMEM((4, n, 2 * E), BF16),
            pltpu.VMEM((2, n, 2 * E), BF16),
        ]


EARLY = D + 2 * E
INV_ROOT = 1.0 / 256.0


def gradient_kernel(
    tok_in, cot_in, w_in, nb_in, rs_in, cg_in, gated_in, op_in, dup_in, dq_in, dkv_in, dfar_in,
    out_ref, gt_ref, early_all, late_all,
    tok_ref, cot_ref, w_ref, nb_ref, rs_ref, cg_ref, gated_ref, op_ref, dup_ref, dq_ref, dkv_ref, dfar_ref, ls,
    hopped, back, yvia, nvia, slope, gp, part, chip_sum, to_col, from_col, early_g, late_g, *rest,
):
    early_bufs, late_bufs = rest[:4] + (early_all,), rest[4:8] + (late_all,)
    bss, brs, sss, srs, ass, ars = rest[8:]
    me = Place()
    c, core, chip = me.c, me.core, me.chip
    behind = me.at_chip(chip - 1)
    round_to = me.at_chip(me.in_ring(1))
    source = me.in_ring(-1)
    handed_to = me.at_chip(source - 2)
    two_on = lax.rem(chip + 2, CHIPS)
    two_y = lax.rem(two_on, 4)
    hander = me.at_chip(two_on - two_y + lax.rem(two_y + 1, 4))
    early = Summed(me, EARLY, early_g, early_bufs, (ass, ars), 0)
    late = Summed(me, D, late_g, late_bufs, (ass, ars), 1)
    greet(
        [me.other, me.far, me.at_chip(chip + 1), me.at_chip(chip + 4), round_to, me.at_chip(source)]
        + [hander, me.xpeer]
        + [device for _, device in early.peers(me.y, 2) + early.peers(me.z, 8)],
        14,
    )

    base = core * T
    obase = (1 - core) * T

    order = (
        (nb_in, nb_ref), (w_in, w_ref), (dup_in, dup_ref), (dq_in, dq_ref), (gated_in, gated_ref),
        (cg_in, cg_ref), (op_in.at[:, rows_at(base, T)], op_ref), (dfar_in.at[1], dfar_ref),
        (dkv_in, dkv_ref), (rs_in, rs_ref), (tok_in, tok_ref), (cot_in, cot_ref),
    )
    loads = [pltpu.make_async_copy(src, dst, ls.at[k]) for k, (src, dst) in enumerate(order)]

    def mine_of(kind, half, i):
        if kind == 0:
            return op_ref[half, pl.ds(i * CH, CH)]
        return part[half, rows_at(base + i * CH, CH)]

    def to_core(kind, i):
        src = (op_in, part)[kind].at[:, rows_at(obase + i * CH, CH)]
        dst = chip_sum.at[kind, :, pl.ds(i * CH, CH)]
        return Copy(src, dst, (sss, srs), (kind, 0, i), me.other).start()

    def across(kind, i, copy):
        copy.wait_recv()
        here = pl.ds(i * CH, CH)
        mine = mine_of(kind, 1 - c, i).astype(F32)
        to_col[kind, here] = (mine + chip_sum[kind, 1 - c, here].astype(F32)).astype(BF16)
        return Copy(
            to_col.at[kind, here], from_col.at[kind, here], (sss, srs), (kind, 1, i), me.far
        ).start()

    def finish(kind, i, copy):
        copy.wait_recv()
        here = pl.ds(i * CH, CH)
        own, out = ((tok_ref, out_ref), (cot_ref, gt_ref))[kind]
        total = mine_of(kind, c, i).astype(F32)
        total = total + chip_sum[kind, c, here].astype(F32)
        total = total + from_col[kind, here].astype(F32)
        out[here] = (own[here].astype(F32) + total).astype(BF16)

    def slot_rows(i):
        return rows_at((base if i < NCH else obase) + i % NCH * CH, CH)

    near, hop, direct = {}, {}, {}
    for i in range(SLOTS):
        rr = slot_rows(i)
        near[i] = Near(
            me, -1, dfar_in.at[1, rr] if i in BACK_AROUND else back.at[2, rr], nvia.at[i], back.at[1, rr],
            (bss, brs), (i,),
        )
        if i in BACK_AROUND:
            hop[i] = Copy(
                dfar_in.at[0, rr], yvia.at[i], (bss, brs), (2, i), round_to, chip > 1, source > 1
            )
            direct[i] = Copy(
                yvia.at[i], back.at[0, rr], (bss, brs), (3, i), handed_to, source > 1, chip < CHIPS - 2
            )
        else:
            hop[i] = Copy(
                dfar_in.at[0, rr], hopped.at[i], (bss, brs), (2, i), behind,
                chip > 1, (chip > 0) & (chip < CHIPS - 1),
            )
    joined = [i for i in range(SLOTS) if i not in BACK_AROUND]
    for i in joined:
        hop[i].start()
    for i in BACK_AROUND:
        hop[i].start()
        near[i].start()
    for copy in loads:
        copy.start()
    out_core = [to_core(0, i) for i in range(NCH)]

    SR = 512
    for copy in loads[:4]:
        copy.wait()

    @pl.loop(0, R // SR)
    def _(i):
        rr = rows_at(i * SR, SR)
        half = 0.5 * dot(nb_ref[rr, :], w_ref[...])
        tan = jnp.tanh(half)
        silu = half + half * tan
        tan = 0.5 * tan
        sl = (0.5 + tan) + silu * (0.5 - tan)
        gp[rr, :E] = (dup_ref[rr, :] * sl[:, :E]).astype(BF16)
        gp[rr, E : 2 * E] = (dq_ref[rr, :] * sl[:, E : 2 * E]).astype(BF16)
        slope[rr, :] = sl[:, 2 * E :]

    for copy in loads[4:6]:
        copy.wait()
    early_g[:D, :] = dot(nb_ref[...], gp[:, : 2 * E], TN)
    for j in range(2):
        early_g[D + j * E : D + (j + 1) * E, :] = dot(gated_ref[...], cg_ref[j], TN)
    early.start()

    for copy in loads[6:]:
        copy.wait()
    out_far = [across(0, i, out_core[i]) for i in range(NCH)]

    for i in joined:
        rr = slot_rows(i)
        back[2, rr] = dfar_ref[rr]

        @pl.when((chip > 0) & (chip < CHIPS - 1))
        def _():
            hop[i].copy.wait_recv()
            back[2, rr] = (dfar_ref[rr].astype(F32) + hopped[i].astype(F32)).astype(BF16)

        near[i].start()
    for i in BACK_AROUND:
        hop[i].wait_recv()
        direct[i].start()
    for i in list(BACK_AROUND) + joined:
        near[i].hand_on()
    early.over_y()

    gt_core = {}
    gt_far = []
    for turn, i in enumerate(list(BACK_AROUND) + joined):
        rr = slot_rows(i)
        near[i].wait_recv()

        @pl.when(chip == CHIPS - 1)
        def _():
            back[1, rr] = jnp.zeros((CH, 2 * E), BF16)

        g = dkv_ref[rr, :]
        if i in BACK_AROUND:
            direct[i].wait_recv()

            @pl.when(chip >= CHIPS - 2)
            def _():
                back[0, rr] = jnp.zeros((CH, 2 * E), BF16)

            g = g + back[0, rr].astype(F32)
        g = ((g + back[1, rr].astype(F32)) * slope[rr, :]).astype(BF16)
        gp[rr, 2 * E :] = g
        nb = nb_ref[rr, :]
        if turn == 0:
            late_g[...] = dot(nb, g, TN)
        else:
            late_g[...] += dot(nb, g, TN)
        if turn == SLOTS - 1:
            late.start()
        g = dot(gp[rr, :], w_ref[...], NT)
        nb = nb.astype(F32)
        inv = rs_ref[rr, 0:1]
        g = inv * (g - jnp.mean(g, -1, keepdims=True) - nb * jnp.mean(g * nb, -1, keepdims=True))
        part[0, rr] = g[:, :HALF].astype(BF16)
        part[1, rr] = g[:, HALF:].astype(BF16)
        if i >= NCH:
            gt_core[i - NCH] = to_core(1, i - NCH)
        else:
            gt_far.append(across(1, i, gt_core[i]))
        if turn == 3:
            early.over_x()
        if turn == 6:
            early.back_z()
    late.over_y()
    for i in range(NCH):
        finish(0, i, out_far[i])
    early.back_core()
    late.over_x()
    late.back_z()
    early.finish()
    late.back_core()
    for i in range(NCH):
        finish(1, i, gt_far[i])
    late.finish()
    for copies in (near, hop, direct):
        for copy in copies.values():
            copy.wait_send()
    for copy in out_core + out_far + list(gt_core.values()) + gt_far + [early, late]:
        copy.wait_send()


def gradients(*operands):
    vm = pl.BlockSpec(memory_space=pltpu.VMEM)
    hbm = pl.BlockSpec(memory_space=pl.ANY)
    dma = pltpu.SemaphoreType.DMA
    loaded = [list(x.shape) for x in operands]
    loaded[7][1] = T
    loaded[11] = [R, 2 * E]
    return pl.pallas_call(
        gradient_kernel,
        out_shape=(
            jax.ShapeDtypeStruct((T, HALF), BF16),
            jax.ShapeDtypeStruct((T, HALF), BF16),
            jax.ShapeDtypeStruct((2, 4, EARLY // 4, 2 * E), BF16),
            jax.ShapeDtypeStruct((2, 4, D // 4, 2 * E), BF16),
        ),
        in_specs=[hbm] * 12,
        out_specs=(vm,) * 4,
        scratch_shapes=[pltpu.VMEM(tuple(d), x.dtype) for d, x in zip(loaded, operands)]
        + [
            dma((12,)),
            pltpu.VMEM((SLOTS, CH, 2 * E), BF16),
            pltpu.VMEM((3, R, 2 * E), BF16),
            pltpu.VMEM((SLOTS, CH, 2 * E), BF16),
            pltpu.VMEM((SLOTS, CH, 2 * E), BF16),
            pltpu.VMEM((R, 2 * E), F32),
            pltpu.VMEM((R, 4 * E), BF16),
            pltpu.VMEM((2, R, HALF), BF16),
            pltpu.VMEM((2, 2, T, HALF), BF16),
            pltpu.VMEM((2, T, HALF), BF16),
            pltpu.VMEM((2, T, HALF), BF16),
            pltpu.VMEM((EARLY, 2 * E), F32),
            pltpu.VMEM((D, 2 * E), F32),
        ]
        + Summed.scratch(EARLY)
        + Summed.scratch(D)
        + [
            dma((4, SLOTS)),
            dma((4, SLOTS)),
            dma((2, 2, NCH)),
            dma((2, 2, NCH)),
            dma((2, 5, 4)),
            dma((2, 5, 4)),
        ],
        compiler_params=pltpu.CompilerParams(
            collective_id=1, has_side_effects=True, vmem_limit_bytes=VMEM_LIMIT
        ),
        cost_estimate=pl.CostEstimate(
            flops=7 * R * D * D, bytes_accessed=16 << 20, transcendentals=R * D
        ),
        name="gradients",
    )(*operands)


def widen_kernel(out_in, gt_in, early_ref, late_ref, out_ref, gt_ref, gwi_ref, gwo_ref):
    out_ref[...] = out_in[...]
    gt_ref[...] = gt_in[...]
    n = EARLY // 4
    for h in range(2):
        for z in range(4):
            at = 0
            while at < n:
                d = z * n + at
                end = next(b for b in (D, D + E, EARLY) if b > d)
                size = min(n - at, end - d)
                piece = early_ref[h, z, at : at + size, :].astype(F32) * INV_ROOT
                if d < D:
                    for j in range(2):
                        gwi_ref[pl.ds(8 * d + 4 * j + h, size, stride=8), :] = piece[:, j * E : (j + 1) * E]
                else:
                    q, e = divmod(d - D, E)
                    gwo_ref[h, e : e + size, q * HALF : (q + 1) * HALF] = piece
                at += size
            m = D // 4
            piece = late_ref[h, z].astype(F32) * INV_ROOT
            for j in range(2):
                gwi_ref[pl.ds(8 * z * m + 4 * j + 2 + h, m, stride=8), :] = piece[:, j * E : (j + 1) * E]


def widen(out, gt, early, late):
    vm = pl.BlockSpec(memory_space=pltpu.VMEM)
    return pl.pallas_call(
        widen_kernel,
        out_shape=(
            jax.ShapeDtypeStruct((T, HALF), BF16),
            jax.ShapeDtypeStruct((T, HALF), BF16),
            jax.ShapeDtypeStruct((8 * D, E), F32),
            jax.ShapeDtypeStruct((2, E, D), F32),
        ),
        in_specs=[vm] * 4,
        out_specs=(vm,) * 4,
        compiler_params=pltpu.CompilerParams(vmem_limit_bytes=VMEM_LIMIT),
        name="widen",
    )(out, gt, early, late)


def shards(tokens, cotangent, weight_in, weight_out, history_ids):
    w, nb, inv, q, up, kv, cg = project(tokens, cotangent, weight_in.reshape(8 * D, E))
    op, gated, dup, dq, dkv, dfar = attention(
        q, kv.reshape(WIN, 2 * E), up, cg, weight_out, history_ids.reshape(-1, E)
    )
    out, gt, gwi, gwo = widen(
        *gradients(tokens, cotangent, w, nb, inv, cg, gated, op, dup, dq, dkv, dfar)
    )
    return out, gt, gwi.reshape(D, 4, 2, E), gwo


def solution(mesh):
    placed = (
        P("seq", "col"),
        P("seq", "col"),
        P(None, None, "col", None),
        P("col", None, None),
        P(),
    )
    return jax.shard_map(
        shards,
        mesh=mesh,
        in_specs=placed,
        out_specs=(
            P("seq", "col"),
            P("seq", "col"),
            P(None, None, "col", None),
            P("col", None, None),
        ),
        check_vma=False,
    )
```

```python
import functools
import math

import jax
import jax.numpy as jnp
from jax import lax
from jax.experimental import pallas as pl
from jax.experimental.pallas import tpu as pltpu
from jax.sharding import PartitionSpec as P

MESH = pl.DeviceIdType.MESH
F32 = jnp.float32
BF16 = jnp.bfloat16

T = 1024
R = 2 * T
D = 512
E = 128
HALF = D // 2
CH = 256
NCH = T // CH
TQ = 512
TK = 512
WIN = 3 * R
EPS = 1e-5
FLOOR = 1.0
SCALE = E**-0.5
OUT_OF_MASK = -32.0
SLOTS = R // CH
AROUND = (0, 1, 2, 4, 5)
BACK_AROUND = (4, 5, 6, 7, 0)
CHIPS = 32
VMEM_LIMIT = 56 * 1024 * 1024

NT = (((1,), (1,)), ((), ()))
TN = (((0,), (0,)), ((), ()))


def dot(a, b, dims=(((1,), (0,)), ((), ()))):
    return lax.dot_general(a, b, dims, preferred_element_type=F32)


def guarded(on, act):
    if on is None:
        act()
    else:
        pl.when(on)(act)


class Copy:
    def __init__(self, src, dst, sems, at, device, on=None, arrives=None):
        self.on, self.arrives = on, arrives
        self.copy = pltpu.make_async_remote_copy(
            src_ref=src,
            dst_ref=dst,
            send_sem=sems[0].at[at],
            recv_sem=sems[1].at[at],
            device_id=device,
            device_id_type=MESH,
        )

    def start(self):
        guarded(self.on, self.copy.start)
        return self

    def wait_recv(self):
        guarded(self.arrives, self.copy.wait_recv)

    def wait_send(self):
        guarded(self.on, self.copy.wait_send)


def rows_at(start, size):
    return pl.ds(pl.multiple_of(start, size), size)


class Place:
    def __init__(self):
        s, c = lax.axis_index("seq"), lax.axis_index("col")
        self.s, self.c = s, c
        self.core = lax.rem(s, 2)
        self.chip = lax.div(s, 2)
        self.y = lax.rem(self.chip, 4)
        self.z = lax.rem(lax.div(s, 8), 4)
        self.xl = lax.div(s, 32)
        self.other = (s + 1 - 2 * self.core, c)
        self.far = (s, 1 - c)
        self.xpeer = (s + 32 - 64 * self.xl, c)

    def at_chip(self, chip):
        return (2 * lax.rem(chip + 2 * CHIPS, CHIPS) + self.core, self.c)

    def in_ring(self, step):
        return self.chip - self.y + lax.rem(self.y + 4 + step, 4)


def greet(senders, count):
    barrier = pltpu.get_barrier_semaphore()
    for device in senders:
        pl.semaphore_signal(barrier, inc=1, device_id=device, device_id_type=MESH)
    pl.semaphore_wait(barrier, count)


class Near:
    def __init__(self, me, step, src, via, dst, sems, at, x_last):
        edge = 3 if step > 0 else 0
        first, last = (0, CHIPS - 1) if step > 0 else (CHIPS - 1, 0)
        cross = me.y == edge
        goes = me.chip != last
        self.comes = me.chip != first
        self.straight = Copy(src, dst, sems, (0,) + at, me.at_chip(me.chip + step), goes & ~cross, self.comes)
        relay = me.chip + 4 * step
        target = me.in_ring(step)
        hands_on = cross & (me.chip > 3 if step > 0 else me.chip < CHIPS - 4)
        if x_last:
            before = 15 if step > 0 else 16
            relay = jnp.where(me.chip == before, first, relay)
            hands_on = (hands_on & (me.chip != before + 4 * step)) | (me.chip == first)
            target = jnp.where(me.chip == first, before + step, target)
        self.aside = Copy(src, via, sems, (1,) + at, me.at_chip(relay), goes & cross, hands_on)
        self.onward = Copy(via, dst, sems, (0,) + at, me.at_chip(target), hands_on)

    def start(self):
        self.straight.start()
        self.aside.start()

    def hand_on(self):
        self.aside.wait_recv()
        self.onward.start()

    def wait_recv(self):
        self.straight.wait_recv()

    def wait_send(self):
        for copy in (self.straight, self.aside, self.onward):
            copy.wait_send()


def project_kernel(
    tok_ref, cot_ref, w_ref,
    wt_ref, nb_ref, rs_ref, q_ref, up_ref, kv_ref, cg_ref, nt_ref, sl_ref,
    xg, yvia, nvia, wv, wf, wh, nb, inv_all, qv, upv, cg, wt, nt, sl, oss, ors, kss, krs, ls, lcg,
):
    me = Place()
    c, core, chip = me.c, me.core, me.chip
    ahead = me.at_chip(chip + 1)
    round_to = me.at_chip(me.in_ring(-1))
    source = me.in_ring(1)
    handed_to = me.at_chip(source + 2)
    two_back = lax.rem(chip + CHIPS - 2, CHIPS)
    two_y = lax.rem(two_back, 4)
    hander = me.at_chip(two_back - two_y + lax.rem(two_y + 3, 4))
    greet(
        [me.other, me.far, me.at_chip(chip - 1), me.at_chip(chip - 4), round_to, me.at_chip(source), hander]
        + [me.at_chip(chip + 15), me.xpeer],
        9,
    )

    base = core * T
    obase = (1 - core) * T

    bufs = (xg, cg)
    srcs = (tok_ref, cot_ref)
    x_copies, o_copies, f_copies = {}, {}, {}
    for kind in (0, 1):
        for i in range(NCH):
            rr = rows_at(base + i * CH, CH)
            x_copies[kind, i] = Copy(
                srcs[kind].at[pl.ds(i * CH, CH)], bufs[kind].at[c, rr], (oss, ors), (kind, 2, i), me.far
            )
            o_copies[kind, i] = Copy(
                srcs[kind].at[pl.ds(i * CH, CH)], bufs[kind].at[c, rr], (oss, ors), (kind, 0, i), me.other
            )
            where = bufs[kind].at[1 - c, rr]
            f_copies[kind, i] = Copy(where, where, (oss, ors), (kind, 1, i), me.other)

    for i in range(NCH):
        x_copies[0, i].start()
        o_copies[0, i].start()
    loads = [
        pltpu.make_async_copy(src, dst, lcg.at[k])
        for k, (src, dst) in enumerate(
            (
                (w_ref, wv),
                (tok_ref, xg.at[c, rows_at(base, T)]),
                (cot_ref, cg.at[c, rows_at(base, T)]),
            )
        )
    ]
    for copy in loads:
        copy.start()
    for copy in loads:
        copy.wait()
    stores = []

    def store(k, slot, src, dst):
        copy = pltpu.make_async_copy(src, dst, ls.at[k, slot])
        copy.start()
        stores.append(copy)

    wf[...] = wv[...].astype(F32)
    for place, part in enumerate((0, 2, 1, 3)):
        lanes = slice(place * E, (place + 1) * E)
        first = wf[pl.ds(2 * part, D, stride=8), :]
        second = wf[pl.ds(2 * part + 1, D, stride=8), :]
        wh[:, lanes] = jnp.where(core == 0, first, second).astype(BF16)
    near, hop, direct, chained = {}, {}, {}, {}
    for slot in range(SLOTS):
        rr = rows_at((base if slot < NCH else obase) + slot % NCH * CH, CH)
        mine = kv_ref.at[2, rr]
        near[slot] = Near(me, 1, mine, nvia.at[slot], kv_ref.at[1, rr], (kss, krs), (slot,), slot % 2 == 0)
        if slot in AROUND:
            hop[slot] = Copy(
                mine, yvia.at[slot], (kss, krs), (2, slot), round_to,
                chip < CHIPS - 2, source < CHIPS - 2,
            )
            direct[slot] = Copy(
                yvia.at[slot], kv_ref.at[0, rr], (kss, krs), (3, slot), handed_to,
                source < CHIPS - 2, chip > 1,
            )
        else:
            chained[slot] = Copy(
                kv_ref.at[1, rr], kv_ref.at[0, rr], (kss, krs), (3, slot), ahead,
                (chip > 0) & (chip < CHIPS - 1), chip > 1,
            )

    def compute(slot):
        rr = rows_at((base if slot < NCH else obase) + slot % NCH * CH, CH)
        x0 = xg[0, rr].astype(F32)
        x1 = xg[1, rr].astype(F32)
        mean = (jnp.sum(x0, -1, keepdims=True) + jnp.sum(x1, -1, keepdims=True)) * (1.0 / D)
        x0 = x0 - mean
        x1 = x1 - mean
        var = (
            jnp.sum(x0 * x0, -1, keepdims=True) + jnp.sum(x1 * x1, -1, keepdims=True)
        ) * (1.0 / D)
        inv = lax.rsqrt(var + EPS)
        n0 = (x0 * inv).astype(BF16)
        n1 = (x1 * inv).astype(BF16)
        half = 0.5 * (dot(n0, wh[:HALF]) + dot(n1, wh[HALF:]))
        proj = (half + half * jnp.tanh(half)).astype(BF16)
        kv_ref[2, rr] = proj[:, 2 * E :]
        near[slot].start()
        if slot in AROUND:
            hop[slot].start()
        sl[rr] = half
        nb[rr, :HALF] = n0
        nb[rr, HALF:] = n1
        inv_all[rr] = jnp.broadcast_to(inv, (CH, E))
        upv[rr] = proj[:, :E]
        qv[rr] = proj[:, E : 2 * E]
        for k, (src, dst) in enumerate(((nb, nb_ref), (inv_all, rs_ref), (upv, up_ref), (qv, q_ref))):
            store(k, slot, src.at[rr], dst.at[rr])

    def hand_on(slot):
        if slot in AROUND:
            hop[slot].wait_recv()
            direct[slot].start()
        else:
            near[slot].wait_recv()
            chained[slot].start()

    for i in range(NCH):
        x_copies[0, i].wait_recv()
        f_copies[0, i].start()
        compute(i)
        o_copies[0, i].wait_recv()
        f_copies[0, i].wait_recv()
        compute(NCH + i)
        if i == 2:
            for j in range(NCH):
                x_copies[1, j].start()
                o_copies[1, j].start()
        if i:
            for slot in (i - 1, NCH + i - 1):
                near[slot].hand_on()
                if slot in AROUND:
                    hand_on(slot)
    for slot in (NCH - 1, SLOTS - 1):
        near[slot].hand_on()
    late = (NCH - 1, SLOTS - 1)
    for slot in [i for i in range(SLOTS) if i not in AROUND] + [i for i in late if i in AROUND]:
        hand_on(slot)
    wt[...] = wh[...].T
    store(4, 0, wt, wt_ref)
    for i in range(SLOTS):
        rr = pl.ds(i * CH, CH)
        half = sl[rr]
        tan = jnp.tanh(half)
        silu = half + half * tan
        tan = 0.5 * tan
        sl[rr] = (0.5 + tan) + silu * (0.5 - tan)
        store(5, i, sl.at[rr], sl_ref.at[rr])
        nt[:, i * CH : (i + 1) * CH] = nb[rr].T
    store(4, 1, nt, nt_ref)
    for i in range(NCH):
        x_copies[1, i].wait_recv()
        f_copies[1, i].start()
    for i in range(NCH):
        o_copies[1, i].wait_recv()
        f_copies[1, i].wait_recv()
    copy = pltpu.make_async_copy(cg, cg_ref, lcg.at[3])
    copy.start()
    stores.append(copy)
    for slot in range(SLOTS):
        if slot in AROUND:
            near[slot].wait_recv()
            direct[slot].wait_recv()
        else:
            chained[slot].wait_recv()
    for copies in (x_copies, o_copies, f_copies, near, hop, direct, chained):
        for copy in copies.values():
            copy.wait_send()
    for copy in stores:
        copy.wait()


def project(tokens, cotangent, w):
    vm = pl.BlockSpec(memory_space=pltpu.VMEM)
    hbm = pl.BlockSpec(memory_space=pl.ANY)
    dma = pltpu.SemaphoreType.DMA
    return pl.pallas_call(
        project_kernel,
        out_shape=(
            jax.ShapeDtypeStruct((D, 4 * E), BF16),
            jax.ShapeDtypeStruct((R, D), BF16),
            jax.ShapeDtypeStruct((R, E), F32),
            jax.ShapeDtypeStruct((R, E), BF16),
            jax.ShapeDtypeStruct((R, E), BF16),
            jax.ShapeDtypeStruct((3, R, 2 * E), BF16),
            jax.ShapeDtypeStruct((2, R, HALF), BF16),
            jax.ShapeDtypeStruct((D, R), BF16),
            jax.ShapeDtypeStruct((R, 4 * E), F32),
        ),
        in_specs=[hbm] * 3,
        out_specs=(hbm,) * 5 + (vm,) + (hbm,) * 3,
        scratch_shapes=[
            pltpu.VMEM((2, R, HALF), BF16),
            pltpu.VMEM((SLOTS, CH, 2 * E), BF16),
            pltpu.VMEM((SLOTS, CH, 2 * E), BF16),
            pltpu.VMEM((8 * D, E), BF16),
            pltpu.VMEM((8 * D, E), F32),
            pltpu.VMEM((D, 4 * E), BF16),
            pltpu.VMEM((R, D), BF16),
            pltpu.VMEM((R, E), F32),
            pltpu.VMEM((R, E), BF16),
            pltpu.VMEM((R, E), BF16),
            pltpu.VMEM((2, R, HALF), BF16),
            pltpu.VMEM((4 * E, D), BF16),
            pltpu.VMEM((D, R), BF16),
            pltpu.VMEM((R, 4 * E), F32),
            dma((2, 3, NCH)),
            dma((2, 3, NCH)),
            dma((4, SLOTS)),
            dma((4, SLOTS)),
            dma((6, SLOTS)),
            dma((4,)),
        ],
        compiler_params=pltpu.CompilerParams(
            collective_id=0, has_side_effects=True, vmem_limit_bytes=VMEM_LIMIT
        ),
        cost_estimate=pl.CostEstimate(
            flops=2 * R * D * D, bytes_accessed=16 << 20, transcendentals=R * D
        ),
        name="gather_project",
    )(tokens, cotangent, w)


def attention_kernel(
    q_ref, kv_ref, up_ref, cg_ref, wo_all, all_ids,
    op_ref, gated_ref, dup_ref, dq_ref, dkv_ref, dfar_ref,
    id_ref, idc, acc, tot, tot_t,
):
    s = lax.axis_index("seq")
    chip = lax.div(s, 2)
    wo_ref = wo_all.at[lax.rem(s, 2)]
    t = pl.program_id(0)

    @pl.when(t == 0)
    def _():
        for b in range(3):
            source = chip - 2 + b
            ids = all_ids[rows_at(jnp.maximum(source, 0) * (R // E), R // E), :]
            ids = jnp.where(source >= 0, ids, -1)
            for j in range(R // E):
                at = b * R + j * E
                row = ids[j : j + 1, :]
                id_ref[0:1, at : at + E] = row
                idc[at : at + E, :] = jnp.broadcast_to(row, (E, E)).T

        @pl.loop(0, WIN // TK)
        def _(j):
            acc[rows_at(j * TK, TK), :] = jnp.zeros((TK, 2 * E), F32)

    def spread(column, width):
        return jnp.concatenate([column] * (width // E), axis=1)

    first = 2 * R // TK
    q = q_ref[...]
    wr = rows_at(2 * R + t * TQ, TQ)
    idq_col = idc[wr, :]
    idq_row = id_ref[0:1, wr]
    start = idq_row[0, 0]
    before = (id_ref[...] < start).astype(jnp.int32)
    low = jnp.sum(before) // TK
    last = first + t * TQ // TK
    uniform = start == idq_row[0, TQ - 1]
    mid = jnp.where(uniform, jnp.minimum(low + 1, last), last)

    def masked(half, ok, kt, causal, row_axis):
        if causal:
            ri = lax.broadcasted_iota(jnp.int32, half.shape, row_axis) + t * TQ
            ci = lax.broadcasted_iota(jnp.int32, half.shape, 1 - row_axis) + (kt - first) * TK
            ok = ok & (ci <= ri)
        return jnp.where(ok, half, OUT_OF_MASK)

    def forward(kt, mask=True, causal=False):
        kr = rows_at(kt * TK, TK)
        half = dot(q, kv_ref[kr, E:], NT) * (0.5 * SCALE)
        if mask:
            half = masked(half, spread(idq_col, TK) == id_ref[0:1, kr], kt, causal, 0)
        weights = (half + half * jnp.tanh(half)).astype(BF16)
        tot[...] += dot(weights, kv_ref[kr, :E])

    def backward(kt, mask=True, causal=False):
        kr = rows_at(kt * TK, TK)
        k = kv_ref[kr, E:]
        half = dot(k, q, NT) * (0.5 * SCALE)
        if mask:
            half = masked(half, spread(idc[kr, :], TQ) == idq_row, kt, causal, 1)
        tan = jnp.tanh(half)
        weights = half + half * tan
        tan = 0.5 * tan
        slope = (0.5 + tan) + weights * (0.5 - tan)
        ds = (slope * dot(kv_ref[kr, :E], grad, NT)).astype(BF16)
        acc[kr, E:] += dot(ds, q)
        acc[kr, :E] += dot(weights.astype(BF16), grad)
        tot_t[...] += dot(k.T, ds)

    def over_keys(step, total):
        total[...] = jnp.zeros_like(total)

        @pl.loop(low, mid)
        def _(kt):
            step(kt)

        @pl.loop(mid, last)
        def _(kt):
            step(kt, mask=False)

        for j in range(max(1, TQ // TK)):
            step(last + j, causal=True)
        return total[...]

    att = over_keys(forward, tot)
    center = att - jnp.mean(att, -1, keepdims=True)
    scale = lax.rsqrt(jnp.mean(center * center, -1, keepdims=True) + FLOOR)
    hn = center * scale
    up = up_ref[...].astype(F32)
    gated = (hn * up).astype(BF16)
    gated_ref[...] = gated
    op_ref[0] = dot(gated, wo_ref[:, :HALF]).astype(BF16)
    op_ref[1] = dot(gated, wo_ref[:, HALF:]).astype(BF16)
    gg = dot(cg_ref[0], wo_ref[:, :HALF], NT) + dot(cg_ref[1], wo_ref[:, HALF:], NT)
    dup_ref[...] = gg * hn
    b = gg * up
    grad = (
        scale * (b - jnp.mean(b, -1, keepdims=True) - hn * jnp.mean(b * hn, -1, keepdims=True))
    ).astype(BF16)
    dq_ref[...] = over_keys(backward, tot_t).T * SCALE

    @pl.when(t == R // TQ - 1)
    def _():
        @pl.loop(0, R // TK)
        def _(j):
            rr = rows_at(j * TK, TK)
            own = rows_at(2 * R + j * TK, TK)
            dkv_ref[rr, :E] = acc[own, :E]
            dkv_ref[rr, E:] = acc[own, E:] * SCALE
            for k in range(2):
                src = rows_at(k * R + j * TK, TK)
                dfar_ref[k, rr, :E] = acc[src, :E].astype(BF16)
                dfar_ref[k, rr, E:] = (acc[src, E:] * SCALE).astype(BF16)


def attention(q, kv, up, cg, wo, ids):
    vm = pl.BlockSpec(memory_space=pltpu.VMEM)
    tile = pl.BlockSpec((TQ, E), lambda t: (t, 0))
    halves = pl.BlockSpec((2, TQ, HALF), lambda t: (0, t, 0))
    return pl.pallas_call(
        attention_kernel,
        grid=(R // TQ,),
        out_shape=(
            jax.ShapeDtypeStruct((2, R, HALF), BF16),
            jax.ShapeDtypeStruct((R, E), BF16),
            jax.ShapeDtypeStruct((R, E), F32),
            jax.ShapeDtypeStruct((R, E), F32),
            jax.ShapeDtypeStruct((R, 2 * E), F32),
            jax.ShapeDtypeStruct((2, R, 2 * E), BF16),
        ),
        in_specs=[tile, vm, tile, halves, vm, vm],
        out_specs=(
            halves,
            tile,
            tile,
            tile,
            pl.BlockSpec((R, 2 * E), lambda t: (0, 0)),
            pl.BlockSpec((2, R, 2 * E), lambda t: (0, 0, 0)),
        ),
        scratch_shapes=[
            pltpu.VMEM((1, WIN), jnp.int32),
            pltpu.VMEM((WIN, E), jnp.int32),
            pltpu.VMEM((WIN, 2 * E), F32),
            pltpu.VMEM((TQ, E), F32),
            pltpu.VMEM((E, TQ), F32),
        ],
        compiler_params=pltpu.CompilerParams(vmem_limit_bytes=VMEM_LIMIT),
        cost_estimate=pl.CostEstimate(
            flops=7 * 2 * R * R * 2 * E, bytes_accessed=16 << 20, transcendentals=4 * R * R
        ),
        name="attention",
    )(q, kv, up, cg, wo, ids)


class Summed:
    def __init__(self, me, rows, grads, bufs, sems, at):
        self.me, self.rows, self.grads, self.bufs = me, rows, grads, bufs
        self.sems, self.at = sems, at
        self.done = []

    def copy(self, src, dst, stage, k, device):
        copy = Copy(src, dst, self.sems, (self.at, stage, k), device).start()
        self.done.append(copy)
        return copy

    def peers(self, here, step):
        s, c = self.me.s, self.me.c
        there = [lax.rem(here + k, 4) for k in (1, 2, 3)]
        return [(v, (s + step * (v - here), c)) for v in there]

    def start(self):
        zbuf, zrecv = self.bufs[0:2]
        n = self.rows // 4
        zbuf[...] = self.grads[...].astype(BF16)
        self.zc = [
            self.copy(zbuf.at[rows_at(v * n, n)], zrecv.at[k], 0, k, device)
            for k, (v, device) in enumerate(self.peers(self.me.z, 8))
        ]

    def over_y(self):
        zrecv, yall = self.bufs[1:3]
        n = self.rows // 4
        for copy in self.zc:
            copy.wait_recv()
        total = self.grads[rows_at(self.me.z * n, n), :]
        for k in range(3):
            total = total + zrecv[k].astype(F32)
        spot = yall.at[self.me.y]
        spot[...] = total.astype(BF16)
        self.yc = [
            self.copy(spot, spot, 1, k, device) for k, (_, device) in enumerate(self.peers(self.me.y, 2))
        ]

    def over_x(self):
        yall, xall = self.bufs[2:4]
        for copy in self.yc:
            copy.wait_recv()
        total = (yall[0].astype(F32) + yall[1].astype(F32)) + (yall[2].astype(F32) + yall[3].astype(F32))
        spot = xall.at[self.me.xl]
        spot[...] = total.astype(BF16)
        self.xc = self.copy(spot, spot, 2, 0, self.me.xpeer)

    def back_z(self):
        xall, whole = self.bufs[3:5]
        me = self.me
        self.xc.wait_recv()
        spot = whole.at[me.core, me.z]
        spot[...] = (xall[0].astype(F32) + xall[1].astype(F32)).astype(BF16)
        self.gz = [
            self.copy(spot, spot, 3, k, device) for k, (_, device) in enumerate(self.peers(me.z, 8))
        ]
        self.gc = [self.copy(spot, spot, 4, 0, me.other)]

    def back_core(self):
        me = self.me
        for k in range(3):
            self.gz[k].wait_recv()
            spot = self.bufs[4].at[me.core, lax.rem(me.z + 3 - k, 4)]
            self.gc.append(self.copy(spot, spot, 4, k + 1, me.other))

    def finish(self):
        for copy in self.gc:
            copy.wait_recv()

    def wait_send(self):
        for copy in self.done:
            copy.wait_send()

    @staticmethod
    def scratch(rows):
        n = rows // 4
        return [
            pltpu.VMEM((rows, 2 * E), BF16),
            pltpu.VMEM((3, n, 2 * E), BF16),
            pltpu.VMEM((4, n, 2 * E), BF16),
            pltpu.VMEM((2, n, 2 * E), BF16),
        ]


EARLY = D + 2 * E
INV_ROOT = 1.0 / 256.0


def gradient_kernel(
    tok_in, cot_in, w_in, nb_in, rs_in, cg_in, gated_in, op_in, dup_in, dq_in, dkv_in, dfar_in, nt_in, sl_in,
    out_ref, gt_ref, early_all, late_all,
    tok_ref, cot_ref, w_ref, nb_ref, rs_ref, cg_ref, gated_ref, op_ref, dup_ref, dq_ref, dkv_ref, dfar_ref, nt_ref, slope, ls,
    hopped, back, yvia, nvia, gp, part, chip_sum, to_col, from_col, early_g, late_g, *rest,
):
    early_bufs, late_bufs = rest[:4] + (early_all,), rest[4:8] + (late_all,)
    bss, brs, sss, srs, ass, ars = rest[8:]
    me = Place()
    c, core, chip = me.c, me.core, me.chip
    behind = me.at_chip(chip - 1)
    round_to = me.at_chip(me.in_ring(1))
    source = me.in_ring(-1)
    handed_to = me.at_chip(source - 2)
    two_on = lax.rem(chip + 2, CHIPS)
    two_y = lax.rem(two_on, 4)
    hander = me.at_chip(two_on - two_y + lax.rem(two_y + 1, 4))
    early = Summed(me, EARLY, early_g, early_bufs, (ass, ars), 0)
    late = Summed(me, D, late_g, late_bufs, (ass, ars), 1)
    greet(
        [me.other, me.far, me.at_chip(chip + 1), me.at_chip(chip + 4), round_to, me.at_chip(source)]
        + [hander, me.xpeer, me.at_chip(chip - 15)]
        + [device for _, device in early.peers(me.y, 2) + early.peers(me.z, 8)],
        15,
    )

    base = core * T
    obase = (1 - core) * T

    order = (
        (sl_in, slope), (dup_in, dup_ref), (dq_in, dq_ref), (nt_in, nt_ref), (gated_in, gated_ref),
        (cg_in, cg_ref), (op_in.at[:, rows_at(base, T)], op_ref), (dfar_in.at[1], dfar_ref),
        (dkv_in, dkv_ref), (nb_in, nb_ref), (w_in, w_ref), (rs_in, rs_ref), (tok_in, tok_ref), (cot_in, cot_ref),
    )
    loads = [pltpu.make_async_copy(src, dst, ls.at[k]) for k, (src, dst) in enumerate(order)]

    def mine_of(kind, half, i):
        if kind == 0:
            return op_ref[half, pl.ds(i * CH, CH)]
        return part[half, rows_at(base + i * CH, CH)]

    def to_core(kind, i):
        src = (op_in, part)[kind].at[:, rows_at(obase + i * CH, CH)]
        dst = chip_sum.at[kind, :, pl.ds(i * CH, CH)]
        return Copy(src, dst, (sss, srs), (kind, 0, i), me.other).start()

    def across(kind, i, copy):
        copy.wait_recv()
        here = pl.ds(i * CH, CH)
        mine = mine_of(kind, 1 - c, i).astype(F32)
        to_col[kind, here] = (mine + chip_sum[kind, 1 - c, here].astype(F32)).astype(BF16)
        return Copy(
            to_col.at[kind, here], from_col.at[kind, here], (sss, srs), (kind, 1, i), me.far
        ).start()

    def finish(kind, i, copy):
        copy.wait_recv()
        here = pl.ds(i * CH, CH)
        own, out = ((tok_ref, out_ref), (cot_ref, gt_ref))[kind]
        total = mine_of(kind, c, i).astype(F32)
        total = total + chip_sum[kind, c, here].astype(F32)
        total = total + from_col[kind, here].astype(F32)
        out[here] = (own[here].astype(F32) + total).astype(BF16)

    def slot_rows(i):
        return rows_at((base if i < NCH else obase) + i % NCH * CH, CH)

    near, hop, direct = {}, {}, {}
    for i in range(SLOTS):
        rr = slot_rows(i)
        near[i] = Near(
            me, -1, dfar_in.at[1, rr] if i in BACK_AROUND else back.at[2, rr], nvia.at[i], back.at[1, rr],
            (bss, brs), (i,), i % 2 == 0,
        )
        if i in BACK_AROUND:
            hop[i] = Copy(
                dfar_in.at[0, rr], yvia.at[i], (bss, brs), (2, i), round_to, chip > 1, source > 1
            )
            direct[i] = Copy(
                yvia.at[i], back.at[0, rr], (bss, brs), (3, i), handed_to, source > 1, chip < CHIPS - 2
            )
        else:
            hop[i] = Copy(
                dfar_in.at[0, rr], hopped.at[i], (bss, brs), (2, i), behind,
                chip > 1, (chip > 0) & (chip < CHIPS - 1),
            )
    joined = [i for i in range(SLOTS) if i not in BACK_AROUND]
    for i in joined:
        hop[i].start()
    for i in BACK_AROUND:
        hop[i].start()
        near[i].start()
    for copy in loads:
        copy.start()
    out_core = [to_core(0, i) for i in range(NCH)]

    SR = 512
    for copy in loads[:3]:
        copy.wait()

    @pl.loop(0, R // SR)
    def _(i):
        rr = rows_at(i * SR, SR)
        gp[rr, :E] = (dup_ref[rr, :] * slope[rr, :E]).astype(BF16)
        gp[rr, E : 2 * E] = (dq_ref[rr, :] * slope[rr, E : 2 * E]).astype(BF16)

    for copy in loads[3:6]:
        copy.wait()
    early_g[:D, :] = dot(nt_ref[...], gp[:, : 2 * E])
    for j in range(2):
        early_g[D + j * E : D + (j + 1) * E, :] = dot(gated_ref[...], cg_ref[j], TN)
    early.start()

    for copy in loads[6:]:
        copy.wait()
    out_far = [across(0, i, out_core[i]) for i in range(NCH)]

    for i in joined:
        rr = slot_rows(i)
        back[2, rr] = dfar_ref[rr]

        @pl.when((chip > 0) & (chip < CHIPS - 1))
        def _():
            hop[i].copy.wait_recv()
            back[2, rr] = (dfar_ref[rr].astype(F32) + hopped[i].astype(F32)).astype(BF16)

        near[i].start()
    for i in BACK_AROUND:
        hop[i].wait_recv()
        direct[i].start()
    for i in list(BACK_AROUND) + joined:
        near[i].hand_on()
    early.over_y()

    gt_core = {}
    gt_far = []
    for turn, i in enumerate(list(BACK_AROUND) + joined):
        rr = slot_rows(i)
        near[i].wait_recv()

        @pl.when(chip == CHIPS - 1)
        def _():
            back[1, rr] = jnp.zeros((CH, 2 * E), BF16)

        g = dkv_ref[rr, :]
        if i in BACK_AROUND:
            direct[i].wait_recv()

            @pl.when(chip >= CHIPS - 2)
            def _():
                back[0, rr] = jnp.zeros((CH, 2 * E), BF16)

            g = g + back[0, rr].astype(F32)
        g = ((g + back[1, rr].astype(F32)) * slope[rr, 2 * E :]).astype(BF16)
        gp[rr, 2 * E :] = g
        tokens_of = nt_ref[:, rr]
        if turn == 0:
            late_g[...] = dot(tokens_of, g)
        else:
            late_g[...] += dot(tokens_of, g)
        if turn == SLOTS - 1:
            late.start()
        g = dot(gp[rr, :], w_ref[...])
        nb = nb_ref[rr, :].astype(F32)
        inv = rs_ref[rr, 0:1]
        g = inv * (g - jnp.mean(g, -1, keepdims=True) - nb * jnp.mean(g * nb, -1, keepdims=True))
        part[0, rr] = g[:, :HALF].astype(BF16)
        part[1, rr] = g[:, HALF:].astype(BF16)
        if i >= NCH:
            gt_core[i - NCH] = to_core(1, i - NCH)
        else:
            gt_far.append(across(1, i, gt_core[i]))
        if turn == 3:
            early.over_x()
        if turn == 6:
            early.back_z()
    late.over_y()
    for i in range(NCH):
        finish(0, i, out_far[i])
    early.back_core()
    late.over_x()
    late.back_z()
    early.finish()
    late.back_core()
    for i in range(NCH):
        finish(1, i, gt_far[i])
    late.finish()
    for copies in (near, hop, direct):
        for copy in copies.values():
            copy.wait_send()
    for copy in out_core + out_far + list(gt_core.values()) + gt_far + [early, late]:
        copy.wait_send()


def gradients(*operands):
    vm = pl.BlockSpec(memory_space=pltpu.VMEM)
    hbm = pl.BlockSpec(memory_space=pl.ANY)
    dma = pltpu.SemaphoreType.DMA
    loaded = [list(x.shape) for x in operands]
    loaded[7][1] = T
    loaded[11] = [R, 2 * E]
    return pl.pallas_call(
        gradient_kernel,
        out_shape=(
            jax.ShapeDtypeStruct((T, HALF), BF16),
            jax.ShapeDtypeStruct((T, HALF), BF16),
            jax.ShapeDtypeStruct((2, 4, EARLY // 4, 2 * E), BF16),
            jax.ShapeDtypeStruct((2, 4, D // 4, 2 * E), BF16),
        ),
        in_specs=[hbm] * 14,
        out_specs=(vm,) * 4,
        scratch_shapes=[pltpu.VMEM(tuple(d), x.dtype) for d, x in zip(loaded, operands)]
        + [
            dma((14,)),
            pltpu.VMEM((SLOTS, CH, 2 * E), BF16),
            pltpu.VMEM((3, R, 2 * E), BF16),
            pltpu.VMEM((SLOTS, CH, 2 * E), BF16),
            pltpu.VMEM((SLOTS, CH, 2 * E), BF16),
            pltpu.VMEM((R, 4 * E), BF16),
            pltpu.VMEM((2, R, HALF), BF16),
            pltpu.VMEM((2, 2, T, HALF), BF16),
            pltpu.VMEM((2, T, HALF), BF16),
            pltpu.VMEM((2, T, HALF), BF16),
            pltpu.VMEM((EARLY, 2 * E), F32),
            pltpu.VMEM((D, 2 * E), F32),
        ]
        + Summed.scratch(EARLY)
        + Summed.scratch(D)
        + [
            dma((4, SLOTS)),
            dma((4, SLOTS)),
            dma((2, 2, NCH)),
            dma((2, 2, NCH)),
            dma((2, 5, 4)),
            dma((2, 5, 4)),
        ],
        compiler_params=pltpu.CompilerParams(
            collective_id=1, has_side_effects=True, vmem_limit_bytes=VMEM_LIMIT
        ),
        cost_estimate=pl.CostEstimate(
            flops=7 * R * D * D, bytes_accessed=16 << 20, transcendentals=R * D
        ),
        name="gradients",
    )(*operands)


def widen_kernel(out_in, gt_in, early_ref, late_ref, out_ref, gt_ref, gwi_ref, gwo_ref):
    out_ref[...] = out_in[...]
    gt_ref[...] = gt_in[...]
    n = EARLY // 4
    for h in range(2):
        for z in range(4):
            at = 0
            while at < n:
                d = z * n + at
                end = next(b for b in (D, D + E, EARLY) if b > d)
                size = min(n - at, end - d)
                piece = early_ref[h, z, at : at + size, :].astype(F32) * INV_ROOT
                if d < D:
                    for j in range(2):
                        gwi_ref[pl.ds(8 * d + 4 * j + h, size, stride=8), :] = piece[:, j * E : (j + 1) * E]
                else:
                    q, e = divmod(d - D, E)
                    gwo_ref[h, e : e + size, q * HALF : (q + 1) * HALF] = piece
                at += size
            m = D // 4
            piece = late_ref[h, z].astype(F32) * INV_ROOT
            for j in range(2):
                gwi_ref[pl.ds(8 * z * m + 4 * j + 2 + h, m, stride=8), :] = piece[:, j * E : (j + 1) * E]


def widen(out, gt, early, late):
    vm = pl.BlockSpec(memory_space=pltpu.VMEM)
    return pl.pallas_call(
        widen_kernel,
        out_shape=(
            jax.ShapeDtypeStruct((T, HALF), BF16),
            jax.ShapeDtypeStruct((T, HALF), BF16),
            jax.ShapeDtypeStruct((8 * D, E), F32),
            jax.ShapeDtypeStruct((2, E, D), F32),
        ),
        in_specs=[vm] * 4,
        out_specs=(vm,) * 4,
        compiler_params=pltpu.CompilerParams(vmem_limit_bytes=VMEM_LIMIT),
        name="widen",
    )(out, gt, early, late)


def shards(tokens, cotangent, weight_in, weight_out, history_ids):
    wt, nb, inv, q, up, kv, cg, nt, slope = project(tokens, cotangent, weight_in.reshape(8 * D, E))
    op, gated, dup, dq, dkv, dfar = attention(
        q, kv.reshape(WIN, 2 * E), up, cg, weight_out, history_ids.reshape(-1, E)
    )
    out, gt, gwi, gwo = widen(
        *gradients(
            tokens, cotangent, wt, nb, inv, cg, gated, op, dup, dq, dkv, dfar, nt, slope
        )
    )
    return out, gt, gwi.reshape(D, 4, 2, E), gwo


def solution(mesh):
    placed = (
        P("seq", "col"),
        P("seq", "col"),
        P(None, None, "col", None),
        P("col", None, None),
        P(),
    )
    return jax.shard_map(
        shards,
        mesh=mesh,
        in_specs=placed,
        out_specs=(
            P("seq", "col"),
            P("seq", "col"),
            P(None, None, "col", None),
            P("col", None, None),
        ),
        check_vma=False,
    )
```

```python
import functools
import math

import jax
import jax.numpy as jnp
from jax import lax
from jax.experimental import pallas as pl
from jax.experimental.pallas import tpu as pltpu
from jax.sharding import PartitionSpec as P

MESH = pl.DeviceIdType.MESH
F32 = jnp.float32
BF16 = jnp.bfloat16

T = 1024
R = 2 * T
D = 512
E = 128
HALF = D // 2
CH = 256
NCH = T // CH
TQ = 512
TK = 512
WIN = 3 * R
EPS = 1e-5
FLOOR = 1.0
SCALE = E**-0.5
OUT_OF_MASK = -32.0
SLOTS = R // CH
AROUND = (0, 1, 2, 4, 5)
BACK_AROUND = (4, 5, 6, 7, 0)
CHIPS = 32
VMEM_LIMIT = 56 * 1024 * 1024

NT = (((1,), (1,)), ((), ()))
TN = (((0,), (0,)), ((), ()))


def dot(a, b, dims=(((1,), (0,)), ((), ()))):
    return lax.dot_general(a, b, dims, preferred_element_type=F32)


def guarded(on, act):
    if on is None:
        act()
    else:
        pl.when(on)(act)


class Copy:
    def __init__(self, src, dst, sems, at, device, on=None, arrives=None):
        self.on, self.arrives = on, arrives
        self.copy = pltpu.make_async_remote_copy(
            src_ref=src,
            dst_ref=dst,
            send_sem=sems[0].at[at],
            recv_sem=sems[1].at[at],
            device_id=device,
            device_id_type=MESH,
        )

    def start(self):
        guarded(self.on, self.copy.start)
        return self

    def wait_recv(self):
        guarded(self.arrives, self.copy.wait_recv)

    def wait_send(self):
        guarded(self.on, self.copy.wait_send)


def rows_at(start, size):
    return pl.ds(pl.multiple_of(start, size), size)


class Place:
    def __init__(self):
        s, c = lax.axis_index("seq"), lax.axis_index("col")
        self.s, self.c = s, c
        self.core = lax.rem(s, 2)
        self.chip = lax.div(s, 2)
        self.y = lax.rem(self.chip, 4)
        self.z = lax.rem(lax.div(s, 8), 4)
        self.xl = lax.div(s, 32)
        self.other = (s + 1 - 2 * self.core, c)
        self.far = (s, 1 - c)
        self.xpeer = (s + 32 - 64 * self.xl, c)

    def at_chip(self, chip):
        return (2 * lax.rem(chip + 2 * CHIPS, CHIPS) + self.core, self.c)

    def in_ring(self, step):
        return self.chip - self.y + lax.rem(self.y + 4 + step, 4)


def greet(senders, count):
    barrier = pltpu.get_barrier_semaphore()
    for device in senders:
        pl.semaphore_signal(barrier, inc=1, device_id=device, device_id_type=MESH)
    pl.semaphore_wait(barrier, count)


class Near:
    def __init__(self, me, step, src, via, dst, sems, at, x_last):
        edge = 3 if step > 0 else 0
        first, last = (0, CHIPS - 1) if step > 0 else (CHIPS - 1, 0)
        cross = me.y == edge
        goes = me.chip != last
        self.comes = me.chip != first
        self.straight = Copy(src, dst, sems, (0,) + at, me.at_chip(me.chip + step), goes & ~cross, self.comes)
        relay = me.chip + 4 * step
        target = me.in_ring(step)
        hands_on = cross & (me.chip > 3 if step > 0 else me.chip < CHIPS - 4)
        if x_last:
            before = 15 if step > 0 else 16
            relay = jnp.where(me.chip == before, first, relay)
            hands_on = (hands_on & (me.chip != before + 4 * step)) | (me.chip == first)
            target = jnp.where(me.chip == first, before + step, target)
        self.aside = Copy(src, via, sems, (1,) + at, me.at_chip(relay), goes & cross, hands_on)
        self.onward = Copy(via, dst, sems, (0,) + at, me.at_chip(target), hands_on)

    def start(self):
        self.straight.start()
        self.aside.start()

    def hand_on(self):
        self.aside.wait_recv()
        self.onward.start()

    def wait_recv(self):
        self.straight.wait_recv()

    def wait_send(self):
        for copy in (self.straight, self.aside, self.onward):
            copy.wait_send()


def project_kernel(
    tok_ref, cot_ref, w_ref,
    wt_ref, nb_ref, rs_ref, q_ref, up_ref, kv_ref, cg_ref, nt_ref, sl_ref,
    xg, yvia, nvia, wv, wf, wh, nb, inv_all, qv, upv, cg, wt, nt, sl, oss, ors, kss, krs, ls, lcg,
):
    me = Place()
    c, core, chip = me.c, me.core, me.chip
    ahead = me.at_chip(chip + 1)
    round_to = me.at_chip(me.in_ring(-1))
    source = me.in_ring(1)
    handed_to = me.at_chip(source + 2)
    two_back = lax.rem(chip + CHIPS - 2, CHIPS)
    two_y = lax.rem(two_back, 4)
    hander = me.at_chip(two_back - two_y + lax.rem(two_y + 3, 4))
    greet(
        [me.other, me.far, me.at_chip(chip - 1), me.at_chip(chip - 4), round_to, me.at_chip(source), hander]
        + [me.at_chip(chip + 15), me.xpeer],
        9,
    )

    base = core * T
    obase = (1 - core) * T

    bufs = (xg, cg)
    srcs = (tok_ref, cot_ref)
    x_copies, o_copies, f_copies = {}, {}, {}
    for kind in (0, 1):
        for i in range(NCH):
            rr = rows_at(base + i * CH, CH)
            x_copies[kind, i] = Copy(
                srcs[kind].at[pl.ds(i * CH, CH)], bufs[kind].at[c, rr], (oss, ors), (kind, 2, i), me.far
            )
            o_copies[kind, i] = Copy(
                srcs[kind].at[pl.ds(i * CH, CH)], bufs[kind].at[c, rr], (oss, ors), (kind, 0, i), me.other
            )
            where = bufs[kind].at[1 - c, rr]
            f_copies[kind, i] = Copy(where, where, (oss, ors), (kind, 1, i), me.other)

    for i in range(NCH):
        x_copies[0, i].start()
        o_copies[0, i].start()
    loads = [
        pltpu.make_async_copy(src, dst, lcg.at[k])
        for k, (src, dst) in enumerate(
            (
                (w_ref, wv),
                (tok_ref, xg.at[c, rows_at(base, T)]),
                (cot_ref, cg.at[c, rows_at(base, T)]),
            )
        )
    ]
    for copy in loads:
        copy.start()
    for copy in loads:
        copy.wait()
    stores = []

    def store(k, slot, src, dst):
        copy = pltpu.make_async_copy(src, dst, ls.at[k, slot])
        copy.start()
        stores.append(copy)

    wf[...] = wv[...].astype(F32)
    for place, part in enumerate((0, 2, 1, 3)):
        lanes = slice(place * E, (place + 1) * E)
        first = wf[pl.ds(2 * part, D, stride=8), :]
        second = wf[pl.ds(2 * part + 1, D, stride=8), :]
        wh[:, lanes] = jnp.where(core == 0, first, second).astype(BF16)
    near, hop, direct, chained = {}, {}, {}, {}
    for slot in range(SLOTS):
        rr = rows_at((base if slot < NCH else obase) + slot % NCH * CH, CH)
        mine = kv_ref.at[2, rr]
        near[slot] = Near(me, 1, mine, nvia.at[slot], kv_ref.at[1, rr], (kss, krs), (slot,), slot % 2 == 0)
        if slot in AROUND:
            hop[slot] = Copy(
                mine, yvia.at[slot], (kss, krs), (2, slot), round_to,
                chip < CHIPS - 2, source < CHIPS - 2,
            )
            direct[slot] = Copy(
                yvia.at[slot], kv_ref.at[0, rr], (kss, krs), (3, slot), handed_to,
                source < CHIPS - 2, chip > 1,
            )
        else:
            chained[slot] = Copy(
                kv_ref.at[1, rr], kv_ref.at[0, rr], (kss, krs), (3, slot), ahead,
                (chip > 0) & (chip < CHIPS - 1), chip > 1,
            )

    def compute(slot):
        rr = rows_at((base if slot < NCH else obase) + slot % NCH * CH, CH)
        x0 = xg[0, rr].astype(F32)
        x1 = xg[1, rr].astype(F32)
        mean = (jnp.sum(x0, -1, keepdims=True) + jnp.sum(x1, -1, keepdims=True)) * (1.0 / D)
        x0 = x0 - mean
        x1 = x1 - mean
        var = (
            jnp.sum(x0 * x0, -1, keepdims=True) + jnp.sum(x1 * x1, -1, keepdims=True)
        ) * (1.0 / D)
        inv = lax.rsqrt(var + EPS)
        n0 = (x0 * inv).astype(BF16)
        n1 = (x1 * inv).astype(BF16)
        half = 0.5 * (dot(n0, wh[:HALF]) + dot(n1, wh[HALF:]))
        proj = (half + half * jnp.tanh(half)).astype(BF16)
        kv_ref[2, rr] = proj[:, 2 * E :]
        near[slot].start()
        if slot in AROUND:
            hop[slot].start()
        sl[rr] = half
        nb[rr, :HALF] = n0
        nb[rr, HALF:] = n1
        inv_all[rr] = jnp.broadcast_to(inv, (CH, E))
        upv[rr] = proj[:, :E]
        qv[rr] = proj[:, E : 2 * E]
        for k, (src, dst) in enumerate(((nb, nb_ref), (inv_all, rs_ref), (upv, up_ref), (qv, q_ref))):
            store(k, slot, src.at[rr], dst.at[rr])

    def hand_on(slot):
        if slot in AROUND:
            hop[slot].wait_recv()
            direct[slot].start()
        else:
            near[slot].wait_recv()
            chained[slot].start()

    for i in range(NCH):
        x_copies[0, i].wait_recv()
        f_copies[0, i].start()
        compute(i)
        o_copies[0, i].wait_recv()
        f_copies[0, i].wait_recv()
        compute(NCH + i)
        if i == 2:
            for j in range(NCH):
                x_copies[1, j].start()
                o_copies[1, j].start()
        if i:
            for slot in (i - 1, NCH + i - 1):
                near[slot].hand_on()
                if slot in AROUND:
                    hand_on(slot)
    for slot in (NCH - 1, SLOTS - 1):
        near[slot].hand_on()
    late = (NCH - 1, SLOTS - 1)
    for slot in [i for i in range(SLOTS) if i not in AROUND] + [i for i in late if i in AROUND]:
        hand_on(slot)
    wt[...] = wh[...].T
    store(4, 0, wt, wt_ref)
    for i in range(SLOTS):
        rr = pl.ds(i * CH, CH)
        half = sl[rr]
        tan = jnp.tanh(half)
        silu = half + half * tan
        tan = 0.5 * tan
        sl[rr] = (0.5 + tan) + silu * (0.5 - tan)
        store(5, i, sl.at[rr], sl_ref.at[rr])
        nt[:, i * CH : (i + 1) * CH] = nb[rr].T
    store(4, 1, nt, nt_ref)
    for i in range(NCH):
        x_copies[1, i].wait_recv()
        f_copies[1, i].start()
    for i in range(NCH):
        o_copies[1, i].wait_recv()
        f_copies[1, i].wait_recv()
    copy = pltpu.make_async_copy(cg, cg_ref, lcg.at[3])
    copy.start()
    stores.append(copy)
    for slot in range(SLOTS):
        if slot in AROUND:
            near[slot].wait_recv()
            direct[slot].wait_recv()
        else:
            chained[slot].wait_recv()
    for copies in (x_copies, o_copies, f_copies, near, hop, direct, chained):
        for copy in copies.values():
            copy.wait_send()
    for copy in stores:
        copy.wait()


def project(tokens, cotangent, w):
    vm = pl.BlockSpec(memory_space=pltpu.VMEM)
    hbm = pl.BlockSpec(memory_space=pl.ANY)
    dma = pltpu.SemaphoreType.DMA
    return pl.pallas_call(
        project_kernel,
        out_shape=(
            jax.ShapeDtypeStruct((D, 4 * E), BF16),
            jax.ShapeDtypeStruct((R, D), BF16),
            jax.ShapeDtypeStruct((R, E), F32),
            jax.ShapeDtypeStruct((R, E), BF16),
            jax.ShapeDtypeStruct((R, E), BF16),
            jax.ShapeDtypeStruct((3, R, 2 * E), BF16),
            jax.ShapeDtypeStruct((2, R, HALF), BF16),
            jax.ShapeDtypeStruct((D, R), BF16),
            jax.ShapeDtypeStruct((R, 4 * E), F32),
        ),
        in_specs=[hbm] * 3,
        out_specs=(hbm,) * 5 + (vm,) + (hbm,) * 3,
        scratch_shapes=[
            pltpu.VMEM((2, R, HALF), BF16),
            pltpu.VMEM((SLOTS, CH, 2 * E), BF16),
            pltpu.VMEM((SLOTS, CH, 2 * E), BF16),
            pltpu.VMEM((8 * D, E), BF16),
            pltpu.VMEM((8 * D, E), F32),
            pltpu.VMEM((D, 4 * E), BF16),
            pltpu.VMEM((R, D), BF16),
            pltpu.VMEM((R, E), F32),
            pltpu.VMEM((R, E), BF16),
            pltpu.VMEM((R, E), BF16),
            pltpu.VMEM((2, R, HALF), BF16),
            pltpu.VMEM((4 * E, D), BF16),
            pltpu.VMEM((D, R), BF16),
            pltpu.VMEM((R, 4 * E), F32),
            dma((2, 3, NCH)),
            dma((2, 3, NCH)),
            dma((4, SLOTS)),
            dma((4, SLOTS)),
            dma((6, SLOTS)),
            dma((4,)),
        ],
        compiler_params=pltpu.CompilerParams(
            collective_id=0, has_side_effects=True, vmem_limit_bytes=VMEM_LIMIT
        ),
        cost_estimate=pl.CostEstimate(
            flops=2 * R * D * D, bytes_accessed=16 << 20, transcendentals=R * D
        ),
        name="gather_project",
    )(tokens, cotangent, w)


def attention_kernel(
    q_ref, kv_ref, up_ref, cg_ref, wo_all, all_ids,
    op_ref, gated_ref, dup_ref, dq_ref, dkv_ref, dfar_ref,
    id_ref, idc, acc, tot, tot_t,
):
    s = lax.axis_index("seq")
    chip = lax.div(s, 2)
    wo_ref = wo_all.at[lax.rem(s, 2)]
    t = pl.program_id(0)

    @pl.when(t == 0)
    def _():
        for b in range(3):
            source = chip - 2 + b
            ids = all_ids[rows_at(jnp.maximum(source, 0) * (R // E), R // E), :]
            ids = jnp.where(source >= 0, ids, -1)
            for j in range(R // E):
                at = b * R + j * E
                row = ids[j : j + 1, :]
                id_ref[0:1, at : at + E] = row
                idc[at : at + E, :] = jnp.broadcast_to(row, (E, E)).T

        @pl.loop(0, WIN // TK)
        def _(j):
            acc[rows_at(j * TK, TK), :] = jnp.zeros((TK, 2 * E), F32)

    def spread(column, width):
        return jnp.concatenate([column] * (width // E), axis=1)

    first = 2 * R // TK
    q = q_ref[...]
    wr = rows_at(2 * R + t * TQ, TQ)
    idq_col = idc[wr, :]
    idq_row = id_ref[0:1, wr]
    start = idq_row[0, 0]
    before = (id_ref[...] < start).astype(jnp.int32)
    low = jnp.sum(before) // TK
    last = first + t * TQ // TK
    uniform = start == idq_row[0, TQ - 1]
    mid = jnp.where(uniform, jnp.minimum(low + 1, last), last)

    def masked(half, ok, kt, causal, row_axis):
        if causal:
            ri = lax.broadcasted_iota(jnp.int32, half.shape, row_axis) + t * TQ
            ci = lax.broadcasted_iota(jnp.int32, half.shape, 1 - row_axis) + (kt - first) * TK
            ok = ok & (ci <= ri)
        return jnp.where(ok, half, OUT_OF_MASK)

    def forward(kt, mask=True, causal=False):
        kr = rows_at(kt * TK, TK)
        half = dot(q, kv_ref[kr, E:], NT) * (0.5 * SCALE)
        if mask:
            half = masked(half, spread(idq_col, TK) == id_ref[0:1, kr], kt, causal, 0)
        weights = (half + half * jnp.tanh(half)).astype(BF16)
        tot[...] += dot(weights, kv_ref[kr, :E])

    def backward(kt, mask=True, causal=False):
        kr = rows_at(kt * TK, TK)
        k = kv_ref[kr, E:]
        half = dot(k, q, NT) * (0.5 * SCALE)
        if mask:
            half = masked(half, spread(idc[kr, :], TQ) == idq_row, kt, causal, 1)
        tan = jnp.tanh(half)
        weights = half + half * tan
        tan = 0.5 * tan
        slope = (0.5 + tan) + weights * (0.5 - tan)
        ds = (slope * dot(kv_ref[kr, :E], grad, NT)).astype(BF16)
        acc[kr, E:] += dot(ds, q)
        acc[kr, :E] += dot(weights.astype(BF16), grad)
        tot_t[...] += dot(k.T, ds)

    def over_keys(step, total):
        total[...] = jnp.zeros_like(total)

        @pl.loop(low, mid)
        def _(kt):
            step(kt)

        @pl.loop(mid, last)
        def _(kt):
            step(kt, mask=False)

        for j in range(max(1, TQ // TK)):
            step(last + j, causal=True)
        return total[...]

    att = over_keys(forward, tot)
    center = att - jnp.mean(att, -1, keepdims=True)
    scale = lax.rsqrt(jnp.mean(center * center, -1, keepdims=True) + FLOOR)
    hn = center * scale
    up = up_ref[...].astype(F32)
    gated = (hn * up).astype(BF16)
    gated_ref[...] = gated
    op_ref[0] = dot(gated, wo_ref[:, :HALF]).astype(BF16)
    op_ref[1] = dot(gated, wo_ref[:, HALF:]).astype(BF16)
    gg = dot(cg_ref[0], wo_ref[:, :HALF], NT) + dot(cg_ref[1], wo_ref[:, HALF:], NT)
    dup_ref[...] = gg * hn
    b = gg * up
    grad = (
        scale * (b - jnp.mean(b, -1, keepdims=True) - hn * jnp.mean(b * hn, -1, keepdims=True))
    ).astype(BF16)
    dq_ref[...] = over_keys(backward, tot_t).T * SCALE

    @pl.when(t == R // TQ - 1)
    def _():
        @pl.loop(0, R // TK)
        def _(j):
            rr = rows_at(j * TK, TK)
            own = rows_at(2 * R + j * TK, TK)
            dkv_ref[rr, :E] = acc[own, :E]
            dkv_ref[rr, E:] = acc[own, E:] * SCALE
            for k in range(2):
                src = rows_at(k * R + j * TK, TK)
                dfar_ref[k, rr, :E] = acc[src, :E].astype(BF16)
                dfar_ref[k, rr, E:] = (acc[src, E:] * SCALE).astype(BF16)


def attention(q, kv, up, cg, wo, ids):
    vm = pl.BlockSpec(memory_space=pltpu.VMEM)
    tile = pl.BlockSpec((TQ, E), lambda t: (t, 0))
    halves = pl.BlockSpec((2, TQ, HALF), lambda t: (0, t, 0))
    return pl.pallas_call(
        attention_kernel,
        grid=(R // TQ,),
        out_shape=(
            jax.ShapeDtypeStruct((2, R, HALF), BF16),
            jax.ShapeDtypeStruct((R, E), BF16),
            jax.ShapeDtypeStruct((R, E), F32),
            jax.ShapeDtypeStruct((R, E), F32),
            jax.ShapeDtypeStruct((R, 2 * E), F32),
            jax.ShapeDtypeStruct((2, R, 2 * E), BF16),
        ),
        in_specs=[tile, vm, tile, halves, vm, vm],
        out_specs=(
            halves,
            tile,
            tile,
            tile,
            pl.BlockSpec((R, 2 * E), lambda t: (0, 0)),
            pl.BlockSpec((2, R, 2 * E), lambda t: (0, 0, 0)),
        ),
        scratch_shapes=[
            pltpu.VMEM((1, WIN), jnp.int32),
            pltpu.VMEM((WIN, E), jnp.int32),
            pltpu.VMEM((WIN, 2 * E), F32),
            pltpu.VMEM((TQ, E), F32),
            pltpu.VMEM((E, TQ), F32),
        ],
        compiler_params=pltpu.CompilerParams(vmem_limit_bytes=VMEM_LIMIT),
        cost_estimate=pl.CostEstimate(
            flops=7 * 2 * R * R * 2 * E, bytes_accessed=16 << 20, transcendentals=4 * R * R
        ),
        name="attention",
    )(q, kv, up, cg, wo, ids)


class Summed:
    def __init__(self, me, rows, grads, bufs, sems, at):
        self.me, self.rows, self.grads, self.bufs = me, rows, grads, bufs
        self.sems, self.at = sems, at
        self.done = []

    def copy(self, src, dst, stage, k, device):
        copy = Copy(src, dst, self.sems, (self.at, stage, k), device).start()
        self.done.append(copy)
        return copy

    def peers(self, here, step):
        s, c = self.me.s, self.me.c
        there = [lax.rem(here + k, 4) for k in (1, 2, 3)]
        return [(v, (s + step * (v - here), c)) for v in there]

    def start(self):
        zbuf, zrecv = self.bufs[0:2]
        n = self.rows // 4
        zbuf[...] = self.grads[...].astype(BF16)
        self.zc = [
            self.copy(zbuf.at[rows_at(v * n, n)], zrecv.at[k], 0, k, device)
            for k, (v, device) in enumerate(self.peers(self.me.z, 8))
        ]

    def over_y(self):
        zrecv, yall = self.bufs[1:3]
        n = self.rows // 4
        for copy in self.zc:
            copy.wait_recv()
        total = self.grads[rows_at(self.me.z * n, n), :]
        for k in range(3):
            total = total + zrecv[k].astype(F32)
        spot = yall.at[self.me.y]
        spot[...] = total.astype(BF16)
        self.yc = [
            self.copy(spot, spot, 1, k, device) for k, (_, device) in enumerate(self.peers(self.me.y, 2))
        ]

    def over_x(self):
        yall, xall = self.bufs[2:4]
        for copy in self.yc:
            copy.wait_recv()
        total = (yall[0].astype(F32) + yall[1].astype(F32)) + (yall[2].astype(F32) + yall[3].astype(F32))
        spot = xall.at[self.me.xl]
        spot[...] = total.astype(BF16)
        self.xc = self.copy(spot, spot, 2, 0, self.me.xpeer)

    def back_z(self):
        xall, whole = self.bufs[3:5]
        me = self.me
        self.xc.wait_recv()
        spot = whole.at[me.core, me.z]
        spot[...] = (xall[0].astype(F32) + xall[1].astype(F32)).astype(BF16)
        self.gz = [
            self.copy(spot, spot, 3, k, device) for k, (_, device) in enumerate(self.peers(me.z, 8))
        ]
        self.gc = [self.copy(spot, spot, 4, 0, me.other)]

    def back_core(self):
        me = self.me
        for k in range(3):
            self.gz[k].wait_recv()
            spot = self.bufs[4].at[me.core, lax.rem(me.z + 3 - k, 4)]
            self.gc.append(self.copy(spot, spot, 4, k + 1, me.other))

    def finish(self):
        for copy in self.gc:
            copy.wait_recv()

    def wait_send(self):
        for copy in self.done:
            copy.wait_send()

    @staticmethod
    def scratch(rows):
        n = rows // 4
        return [
            pltpu.VMEM((rows, 2 * E), BF16),
            pltpu.VMEM((3, n, 2 * E), BF16),
            pltpu.VMEM((4, n, 2 * E), BF16),
            pltpu.VMEM((2, n, 2 * E), BF16),
        ]


EARLY = D + 2 * E
INV_ROOT = 1.0 / 256.0


def gradient_kernel(
    tok_in, cot_in, w_in, nb_in, rs_in, cg_in, gated_in, op_in, dup_in, dq_in, dkv_in, dfar_in, nt_in, sl_in,
    out_ref, gt_ref, early_all, late_all,
    tok_ref, cot_ref, w_ref, nb_ref, rs_ref, cg_ref, gated_ref, op_ref, dup_ref, dq_ref, dkv_ref, dfar_ref, nt_ref, slope, ls,
    hopped, back, yvia, nvia, gp, part, chip_sum, to_col, from_col, early_g, late_g, *rest,
):
    early_bufs, late_bufs = rest[:4] + (early_all,), rest[4:8] + (late_all,)
    bss, brs, sss, srs, ass, ars = rest[8:]
    me = Place()
    c, core, chip = me.c, me.core, me.chip
    behind = me.at_chip(chip - 1)
    round_to = me.at_chip(me.in_ring(1))
    source = me.in_ring(-1)
    handed_to = me.at_chip(source - 2)
    two_on = lax.rem(chip + 2, CHIPS)
    two_y = lax.rem(two_on, 4)
    hander = me.at_chip(two_on - two_y + lax.rem(two_y + 1, 4))
    early = Summed(me, EARLY, early_g, early_bufs, (ass, ars), 0)
    late = Summed(me, D, late_g, late_bufs, (ass, ars), 1)
    greet(
        [me.other, me.far, me.at_chip(chip + 1), me.at_chip(chip + 4), round_to, me.at_chip(source)]
        + [hander, me.xpeer, me.at_chip(chip - 15)]
        + [device for _, device in early.peers(me.y, 2) + early.peers(me.z, 8)],
        15,
    )

    base = core * T
    obase = (1 - core) * T

    order = (
        (dfar_in.at[1], dfar_ref), (sl_in, slope), (dup_in, dup_ref), (dq_in, dq_ref), (nt_in, nt_ref), (gated_in, gated_ref),
        (cg_in, cg_ref), (op_in.at[:, rows_at(base, T)], op_ref),
        (dkv_in, dkv_ref), (nb_in, nb_ref), (w_in, w_ref), (rs_in, rs_ref), (tok_in, tok_ref), (cot_in, cot_ref),
    )
    loads = [pltpu.make_async_copy(src, dst, ls.at[k]) for k, (src, dst) in enumerate(order)]

    def mine_of(kind, half, i):
        if kind == 0:
            return op_ref[half, pl.ds(i * CH, CH)]
        return part[half, rows_at(base + i * CH, CH)]

    def to_core(kind, i):
        src = (op_in, part)[kind].at[:, rows_at(obase + i * CH, CH)]
        dst = chip_sum.at[kind, :, pl.ds(i * CH, CH)]
        return Copy(src, dst, (sss, srs), (kind, 0, i), me.other).start()

    def across(kind, i, copy):
        copy.wait_recv()
        here = pl.ds(i * CH, CH)
        mine = mine_of(kind, 1 - c, i).astype(F32)
        to_col[kind, here] = (mine + chip_sum[kind, 1 - c, here].astype(F32)).astype(BF16)
        return Copy(
            to_col.at[kind, here], from_col.at[kind, here], (sss, srs), (kind, 1, i), me.far
        ).start()

    def finish(kind, i, copy):
        copy.wait_recv()
        here = pl.ds(i * CH, CH)
        own, out = ((tok_ref, out_ref), (cot_ref, gt_ref))[kind]
        total = mine_of(kind, c, i).astype(F32)
        total = total + chip_sum[kind, c, here].astype(F32)
        total = total + from_col[kind, here].astype(F32)
        out[here] = (own[here].astype(F32) + total).astype(BF16)

    def slot_rows(i):
        return rows_at((base if i < NCH else obase) + i % NCH * CH, CH)

    near, hop, direct = {}, {}, {}
    for i in range(SLOTS):
        rr = slot_rows(i)
        near[i] = Near(
            me, -1, dfar_in.at[1, rr] if i in BACK_AROUND else back.at[2, rr], nvia.at[i], back.at[1, rr],
            (bss, brs), (i,), i % 2 == 0,
        )
        if i in BACK_AROUND:
            hop[i] = Copy(
                dfar_in.at[0, rr], yvia.at[i], (bss, brs), (2, i), round_to, chip > 1, source > 1
            )
            direct[i] = Copy(
                yvia.at[i], back.at[0, rr], (bss, brs), (3, i), handed_to, source > 1, chip < CHIPS - 2
            )
        else:
            hop[i] = Copy(
                dfar_in.at[0, rr], hopped.at[i], (bss, brs), (2, i), behind,
                chip > 1, (chip > 0) & (chip < CHIPS - 1),
            )
    joined = [i for i in range(SLOTS) if i not in BACK_AROUND]
    for i in joined:
        hop[i].start()
    for i in BACK_AROUND:
        hop[i].start()
        near[i].start()
    for copy in loads:
        copy.start()
    out_core = [to_core(0, i) for i in range(NCH)]

    SR = 512
    for copy in loads[:4]:
        copy.wait()

    @pl.loop(0, R // SR)
    def _(i):
        rr = rows_at(i * SR, SR)
        gp[rr, :E] = (dup_ref[rr, :] * slope[rr, :E]).astype(BF16)
        gp[rr, E : 2 * E] = (dq_ref[rr, :] * slope[rr, E : 2 * E]).astype(BF16)

    for i in BACK_AROUND:
        near[i].hand_on()
    for i in BACK_AROUND:
        hop[i].wait_recv()
        direct[i].start()
    for i in joined:
        rr = slot_rows(i)
        back[2, rr] = dfar_ref[rr]

        @pl.when((chip > 0) & (chip < CHIPS - 1))
        def _():
            hop[i].copy.wait_recv()
            back[2, rr] = (dfar_ref[rr].astype(F32) + hopped[i].astype(F32)).astype(BF16)

        near[i].start()
    for copy in loads[4:7]:
        copy.wait()
    early_g[:D, :] = dot(nt_ref[...], gp[:, : 2 * E])
    for j in range(2):
        early_g[D + j * E : D + (j + 1) * E, :] = dot(gated_ref[...], cg_ref[j], TN)
    early.start()

    for copy in loads[7:]:
        copy.wait()
    out_far = [across(0, i, out_core[i]) for i in range(NCH)]

    for i in joined:
        near[i].hand_on()
    gt_core = {}
    gt_far = []
    for turn, i in enumerate(list(BACK_AROUND) + joined):
        rr = slot_rows(i)
        near[i].wait_recv()

        @pl.when(chip == CHIPS - 1)
        def _():
            back[1, rr] = jnp.zeros((CH, 2 * E), BF16)

        g = dkv_ref[rr, :]
        if i in BACK_AROUND:
            direct[i].wait_recv()

            @pl.when(chip >= CHIPS - 2)
            def _():
                back[0, rr] = jnp.zeros((CH, 2 * E), BF16)

            g = g + back[0, rr].astype(F32)
        g = ((g + back[1, rr].astype(F32)) * slope[rr, 2 * E :]).astype(BF16)
        gp[rr, 2 * E :] = g
        tokens_of = nt_ref[:, rr]
        if turn == 0:
            late_g[...] = dot(tokens_of, g)
        else:
            late_g[...] += dot(tokens_of, g)
        if turn == SLOTS - 1:
            late.start()
        g = dot(gp[rr, :], w_ref[...])
        nb = nb_ref[rr, :].astype(F32)
        inv = rs_ref[rr, 0:1]
        g = inv * (g - jnp.mean(g, -1, keepdims=True) - nb * jnp.mean(g * nb, -1, keepdims=True))
        part[0, rr] = g[:, :HALF].astype(BF16)
        part[1, rr] = g[:, HALF:].astype(BF16)
        if i >= NCH:
            gt_core[i - NCH] = to_core(1, i - NCH)
        else:
            gt_far.append(across(1, i, gt_core[i]))
        if turn == 4:
            early.over_y()
    early.over_x()
    late.over_y()
    early.back_z()
    late.over_x()
    for i in range(NCH):
        finish(0, i, out_far[i])
    late.back_z()
    early.back_core()
    early.finish()
    late.back_core()
    for i in range(NCH):
        finish(1, i, gt_far[i])
    late.finish()
    for copies in (near, hop, direct):
        for copy in copies.values():
            copy.wait_send()
    for copy in out_core + out_far + list(gt_core.values()) + gt_far + [early, late]:
        copy.wait_send()


def gradients(*operands):
    vm = pl.BlockSpec(memory_space=pltpu.VMEM)
    hbm = pl.BlockSpec(memory_space=pl.ANY)
    dma = pltpu.SemaphoreType.DMA
    loaded = [list(x.shape) for x in operands]
    loaded[7][1] = T
    loaded[11] = [R, 2 * E]
    return pl.pallas_call(
        gradient_kernel,
        out_shape=(
            jax.ShapeDtypeStruct((T, HALF), BF16),
            jax.ShapeDtypeStruct((T, HALF), BF16),
            jax.ShapeDtypeStruct((2, 4, EARLY // 4, 2 * E), BF16),
            jax.ShapeDtypeStruct((2, 4, D // 4, 2 * E), BF16),
        ),
        in_specs=[hbm] * 14,
        out_specs=(vm,) * 4,
        scratch_shapes=[pltpu.VMEM(tuple(d), x.dtype) for d, x in zip(loaded, operands)]
        + [
            dma((14,)),
            pltpu.VMEM((SLOTS, CH, 2 * E), BF16),
            pltpu.VMEM((3, R, 2 * E), BF16),
            pltpu.VMEM((SLOTS, CH, 2 * E), BF16),
            pltpu.VMEM((SLOTS, CH, 2 * E), BF16),
            pltpu.VMEM((R, 4 * E), BF16),
            pltpu.VMEM((2, R, HALF), BF16),
            pltpu.VMEM((2, 2, T, HALF), BF16),
            pltpu.VMEM((2, T, HALF), BF16),
            pltpu.VMEM((2, T, HALF), BF16),
            pltpu.VMEM((EARLY, 2 * E), F32),
            pltpu.VMEM((D, 2 * E), F32),
        ]
        + Summed.scratch(EARLY)
        + Summed.scratch(D)
        + [
            dma((4, SLOTS)),
            dma((4, SLOTS)),
            dma((2, 2, NCH)),
            dma((2, 2, NCH)),
            dma((2, 5, 4)),
            dma((2, 5, 4)),
        ],
        compiler_params=pltpu.CompilerParams(
            collective_id=1, has_side_effects=True, vmem_limit_bytes=VMEM_LIMIT
        ),
        cost_estimate=pl.CostEstimate(
            flops=7 * R * D * D, bytes_accessed=16 << 20, transcendentals=R * D
        ),
        name="gradients",
    )(*operands)


def widen_kernel(out_in, gt_in, early_ref, late_ref, out_ref, gt_ref, gwi_ref, gwo_ref):
    out_ref[...] = out_in[...]
    gt_ref[...] = gt_in[...]
    n = EARLY // 4
    for h in range(2):
        for z in range(4):
            at = 0
            while at < n:
                d = z * n + at
                end = next(b for b in (D, D + E, EARLY) if b > d)
                size = min(n - at, end - d)
                piece = early_ref[h, z, at : at + size, :].astype(F32) * INV_ROOT
                if d < D:
                    for j in range(2):
                        gwi_ref[pl.ds(8 * d + 4 * j + h, size, stride=8), :] = piece[:, j * E : (j + 1) * E]
                else:
                    q, e = divmod(d - D, E)
                    gwo_ref[h, e : e + size, q * HALF : (q + 1) * HALF] = piece
                at += size
            m = D // 4
            piece = late_ref[h, z].astype(F32) * INV_ROOT
            for j in range(2):
                gwi_ref[pl.ds(8 * z * m + 4 * j + 2 + h, m, stride=8), :] = piece[:, j * E : (j + 1) * E]


def widen(out, gt, early, late):
    vm = pl.BlockSpec(memory_space=pltpu.VMEM)
    return pl.pallas_call(
        widen_kernel,
        out_shape=(
            jax.ShapeDtypeStruct((T, HALF), BF16),
            jax.ShapeDtypeStruct((T, HALF), BF16),
            jax.ShapeDtypeStruct((8 * D, E), F32),
            jax.ShapeDtypeStruct((2, E, D), F32),
        ),
        in_specs=[vm] * 4,
        out_specs=(vm,) * 4,
        compiler_params=pltpu.CompilerParams(vmem_limit_bytes=VMEM_LIMIT),
        name="widen",
    )(out, gt, early, late)


def shards(tokens, cotangent, weight_in, weight_out, history_ids):
    wt, nb, inv, q, up, kv, cg, nt, slope = project(tokens, cotangent, weight_in.reshape(8 * D, E))
    op, gated, dup, dq, dkv, dfar = attention(
        q, kv.reshape(WIN, 2 * E), up, cg, weight_out, history_ids.reshape(-1, E)
    )
    out, gt, gwi, gwo = widen(
        *gradients(
            tokens, cotangent, wt, nb, inv, cg, gated, op, dup, dq, dkv, dfar, nt, slope
        )
    )
    return out, gt, gwi.reshape(D, 4, 2, E), gwo


def solution(mesh):
    placed = (
        P("seq", "col"),
        P("seq", "col"),
        P(None, None, "col", None),
        P("col", None, None),
        P(),
    )
    return jax.shard_map(
        shards,
        mesh=mesh,
        in_specs=placed,
        out_specs=(
            P("seq", "col"),
            P("seq", "col"),
            P(None, None, "col", None),
            P("col", None, None),
        ),
        check_vma=False,
    )
```

```python
import functools
import math

import jax
import jax.numpy as jnp
from jax import lax
from jax.experimental import pallas as pl
from jax.experimental.pallas import tpu as pltpu
from jax.sharding import PartitionSpec as P

MESH = pl.DeviceIdType.MESH
F32 = jnp.float32
BF16 = jnp.bfloat16

T = 1024
R = 2 * T
D = 512
E = 128
HALF = D // 2
CH = 256
NCH = T // CH
TQ = 512
TK = 512
WIN = 3 * R
EPS = 1e-5
FLOOR = 1.0
SCALE = E**-0.5
OUT_OF_MASK = -32.0
SLOTS = R // CH
AROUND = (0, 1, 2, 4, 5)
BACK_AROUND = (4, 5, 6, 7, 0)
CHIPS = 32
VMEM_LIMIT = 56 * 1024 * 1024

NT = (((1,), (1,)), ((), ()))
TN = (((0,), (0,)), ((), ()))


def dot(a, b, dims=(((1,), (0,)), ((), ()))):
    return lax.dot_general(a, b, dims, preferred_element_type=F32)


def guarded(on, act):
    if on is None:
        act()
    else:
        pl.when(on)(act)


class Copy:
    def __init__(self, src, dst, sems, at, device, on=None, arrives=None):
        self.on, self.arrives = on, arrives
        self.copy = pltpu.make_async_remote_copy(
            src_ref=src,
            dst_ref=dst,
            send_sem=sems[0].at[at],
            recv_sem=sems[1].at[at],
            device_id=device,
            device_id_type=MESH,
        )

    def start(self):
        guarded(self.on, self.copy.start)
        return self

    def wait_recv(self):
        guarded(self.arrives, self.copy.wait_recv)

    def wait_send(self):
        guarded(self.on, self.copy.wait_send)


def rows_at(start, size):
    return pl.ds(pl.multiple_of(start, size), size)


class Place:
    def __init__(self):
        s, c = lax.axis_index("seq"), lax.axis_index("col")
        self.s, self.c = s, c
        self.core = lax.rem(s, 2)
        self.chip = lax.div(s, 2)
        self.y = lax.rem(self.chip, 4)
        self.z = lax.rem(lax.div(s, 8), 4)
        self.xl = lax.div(s, 32)
        self.other = (s + 1 - 2 * self.core, c)
        self.far = (s, 1 - c)
        self.xpeer = (s + 32 - 64 * self.xl, c)

    def at_chip(self, chip):
        return (2 * lax.rem(chip + 2 * CHIPS, CHIPS) + self.core, self.c)

    def in_ring(self, step):
        return self.chip - self.y + lax.rem(self.y + 4 + step, 4)


def greet(senders, count):
    barrier = pltpu.get_barrier_semaphore()
    for device in senders:
        pl.semaphore_signal(barrier, inc=1, device_id=device, device_id_type=MESH)
    pl.semaphore_wait(barrier, count)


class Near:
    def __init__(self, me, step, src, via, dst, sems, at, x_last):
        edge = 3 if step > 0 else 0
        first, last = (0, CHIPS - 1) if step > 0 else (CHIPS - 1, 0)
        cross = me.y == edge
        goes = me.chip != last
        self.comes = me.chip != first
        self.straight = Copy(src, dst, sems, (0,) + at, me.at_chip(me.chip + step), goes & ~cross, self.comes)
        relay = me.chip + 4 * step
        target = me.in_ring(step)
        hands_on = cross & (me.chip > 3 if step > 0 else me.chip < CHIPS - 4)
        if x_last:
            before = 15 if step > 0 else 16
            relay = jnp.where(me.chip == before, first, relay)
            hands_on = (hands_on & (me.chip != before + 4 * step)) | (me.chip == first)
            target = jnp.where(me.chip == first, before + step, target)
        self.aside = Copy(src, via, sems, (1,) + at, me.at_chip(relay), goes & cross, hands_on)
        self.onward = Copy(via, dst, sems, (0,) + at, me.at_chip(target), hands_on)

    def start(self):
        self.straight.start()
        self.aside.start()

    def hand_on(self):
        self.aside.wait_recv()
        self.onward.start()

    def wait_recv(self):
        self.straight.wait_recv()

    def wait_send(self):
        for copy in (self.straight, self.aside, self.onward):
            copy.wait_send()


def project_kernel(
    tok_ref, cot_ref, w_ref,
    wt_ref, nb_ref, rs_ref, q_ref, up_ref, kv_ref, cg_ref, nt_ref, sl_ref,
    xg, yvia, nvia, wv, wf, wh, nb, inv_all, qv, upv, cg, wt, nt, sl, oss, ors, kss, krs, ls, lcg,
):
    me = Place()
    c, core, chip = me.c, me.core, me.chip
    ahead = me.at_chip(chip + 1)
    round_to = me.at_chip(me.in_ring(-1))
    source = me.in_ring(1)
    handed_to = me.at_chip(source + 2)
    two_back = lax.rem(chip + CHIPS - 2, CHIPS)
    two_y = lax.rem(two_back, 4)
    hander = me.at_chip(two_back - two_y + lax.rem(two_y + 3, 4))
    greet(
        [me.other, me.far, me.at_chip(chip - 1), me.at_chip(chip - 4), round_to, me.at_chip(source), hander]
        + [me.at_chip(chip + 15), me.xpeer],
        9,
    )

    base = core * T
    obase = (1 - core) * T

    bufs = (xg, cg)
    srcs = (tok_ref, cot_ref)
    x_copies, o_copies, f_copies = {}, {}, {}
    for kind in (0, 1):
        for i in range(NCH):
            rr = rows_at(base + i * CH, CH)
            x_copies[kind, i] = Copy(
                srcs[kind].at[pl.ds(i * CH, CH)], bufs[kind].at[c, rr], (oss, ors), (kind, 2, i), me.far
            )
            o_copies[kind, i] = Copy(
                srcs[kind].at[pl.ds(i * CH, CH)], bufs[kind].at[c, rr], (oss, ors), (kind, 0, i), me.other
            )
            where = bufs[kind].at[1 - c, rr]
            f_copies[kind, i] = Copy(where, where, (oss, ors), (kind, 1, i), me.other)

    for i in range(NCH):
        x_copies[0, i].start()
        o_copies[0, i].start()
    loads = [
        pltpu.make_async_copy(src, dst, lcg.at[k])
        for k, (src, dst) in enumerate(
            (
                (w_ref, wv),
                (tok_ref, xg.at[c, rows_at(base, T)]),
                (cot_ref, cg.at[c, rows_at(base, T)]),
            )
        )
    ]
    for copy in loads:
        copy.start()
    for copy in loads:
        copy.wait()
    stores = []

    def store(k, slot, src, dst):
        copy = pltpu.make_async_copy(src, dst, ls.at[k, slot])
        copy.start()
        stores.append(copy)

    wf[...] = wv[...].astype(F32)
    for place, part in enumerate((0, 2, 1, 3)):
        lanes = slice(place * E, (place + 1) * E)
        first = wf[pl.ds(2 * part, D, stride=8), :]
        second = wf[pl.ds(2 * part + 1, D, stride=8), :]
        wh[:, lanes] = jnp.where(core == 0, first, second).astype(BF16)
    near, hop, direct, chained = {}, {}, {}, {}
    for slot in range(SLOTS):
        rr = rows_at((base if slot < NCH else obase) + slot % NCH * CH, CH)
        mine = kv_ref.at[2, rr]
        near[slot] = Near(me, 1, mine, nvia.at[slot], kv_ref.at[1, rr], (kss, krs), (slot,), slot % 2 == 0)
        if slot in AROUND:
            hop[slot] = Copy(
                mine, yvia.at[slot], (kss, krs), (2, slot), round_to,
                chip < CHIPS - 2, source < CHIPS - 2,
            )
            direct[slot] = Copy(
                yvia.at[slot], kv_ref.at[0, rr], (kss, krs), (3, slot), handed_to,
                source < CHIPS - 2, chip > 1,
            )
        else:
            chained[slot] = Copy(
                kv_ref.at[1, rr], kv_ref.at[0, rr], (kss, krs), (3, slot), ahead,
                (chip > 0) & (chip < CHIPS - 1), chip > 1,
            )

    def compute(slot):
        rr = rows_at((base if slot < NCH else obase) + slot % NCH * CH, CH)
        x0 = xg[0, rr].astype(F32)
        x1 = xg[1, rr].astype(F32)
        mean = (jnp.sum(x0, -1, keepdims=True) + jnp.sum(x1, -1, keepdims=True)) * (1.0 / D)
        x0 = x0 - mean
        x1 = x1 - mean
        var = (
            jnp.sum(x0 * x0, -1, keepdims=True) + jnp.sum(x1 * x1, -1, keepdims=True)
        ) * (1.0 / D)
        inv = lax.rsqrt(var + EPS)
        n0 = (x0 * inv).astype(BF16)
        n1 = (x1 * inv).astype(BF16)
        half = 0.5 * (dot(n0, wh[:HALF]) + dot(n1, wh[HALF:]))
        proj = (half + half * jnp.tanh(half)).astype(BF16)
        kv_ref[2, rr] = proj[:, 2 * E :]
        near[slot].start()
        if slot in AROUND:
            hop[slot].start()
        sl[rr] = half
        nb[rr, :HALF] = n0
        nb[rr, HALF:] = n1
        inv_all[rr] = jnp.broadcast_to(inv, (CH, E))
        upv[rr] = proj[:, :E]
        qv[rr] = proj[:, E : 2 * E]
        for k, (src, dst) in enumerate(((nb, nb_ref), (inv_all, rs_ref), (upv, up_ref), (qv, q_ref))):
            store(k, slot, src.at[rr], dst.at[rr])

    def hand_on(slot):
        if slot in AROUND:
            hop[slot].wait_recv()
            direct[slot].start()
        else:
            near[slot].wait_recv()
            chained[slot].start()

    for i in range(NCH):
        x_copies[0, i].wait_recv()
        f_copies[0, i].start()
        compute(i)
        o_copies[0, i].wait_recv()
        f_copies[0, i].wait_recv()
        compute(NCH + i)
        if i == 2:
            for j in range(NCH):
                x_copies[1, j].start()
                o_copies[1, j].start()
        if i:
            for slot in (i - 1, NCH + i - 1):
                near[slot].hand_on()
                if slot in AROUND:
                    hand_on(slot)
    for slot in (NCH - 1, SLOTS - 1):
        near[slot].hand_on()
    late = (NCH - 1, SLOTS - 1)
    for slot in [i for i in range(SLOTS) if i not in AROUND] + [i for i in late if i in AROUND]:
        hand_on(slot)
    wt[...] = wh[...].T
    store(4, 0, wt, wt_ref)
    for i in range(SLOTS):
        rr = pl.ds(i * CH, CH)
        half = sl[rr]
        tan = jnp.tanh(half)
        silu = half + half * tan
        tan = 0.5 * tan
        sl[rr] = (0.5 + tan) + silu * (0.5 - tan)
        store(5, i, sl.at[rr], sl_ref.at[rr])
        nt[:, i * CH : (i + 1) * CH] = nb[rr].T
    store(4, 1, nt, nt_ref)
    for i in range(NCH):
        x_copies[1, i].wait_recv()
        f_copies[1, i].start()
    for i in range(NCH):
        o_copies[1, i].wait_recv()
        f_copies[1, i].wait_recv()
    copy = pltpu.make_async_copy(cg, cg_ref, lcg.at[3])
    copy.start()
    stores.append(copy)
    for slot in range(SLOTS):
        if slot in AROUND:
            near[slot].wait_recv()
            direct[slot].wait_recv()
        else:
            chained[slot].wait_recv()
    for copies in (x_copies, o_copies, f_copies, near, hop, direct, chained):
        for copy in copies.values():
            copy.wait_send()
    for copy in stores:
        copy.wait()


def project(tokens, cotangent, w):
    vm = pl.BlockSpec(memory_space=pltpu.VMEM)
    hbm = pl.BlockSpec(memory_space=pl.ANY)
    dma = pltpu.SemaphoreType.DMA
    return pl.pallas_call(
        project_kernel,
        out_shape=(
            jax.ShapeDtypeStruct((D, 4 * E), BF16),
            jax.ShapeDtypeStruct((R, D), BF16),
            jax.ShapeDtypeStruct((R, E), F32),
            jax.ShapeDtypeStruct((R, E), BF16),
            jax.ShapeDtypeStruct((R, E), BF16),
            jax.ShapeDtypeStruct((3, R, 2 * E), BF16),
            jax.ShapeDtypeStruct((2, R, HALF), BF16),
            jax.ShapeDtypeStruct((D, R), BF16),
            jax.ShapeDtypeStruct((R, 4 * E), F32),
        ),
        in_specs=[hbm] * 3,
        out_specs=(hbm,) * 5 + (vm,) + (hbm,) * 3,
        scratch_shapes=[
            pltpu.VMEM((2, R, HALF), BF16),
            pltpu.VMEM((SLOTS, CH, 2 * E), BF16),
            pltpu.VMEM((SLOTS, CH, 2 * E), BF16),
            pltpu.VMEM((8 * D, E), BF16),
            pltpu.VMEM((8 * D, E), F32),
            pltpu.VMEM((D, 4 * E), BF16),
            pltpu.VMEM((R, D), BF16),
            pltpu.VMEM((R, E), F32),
            pltpu.VMEM((R, E), BF16),
            pltpu.VMEM((R, E), BF16),
            pltpu.VMEM((2, R, HALF), BF16),
            pltpu.VMEM((4 * E, D), BF16),
            pltpu.VMEM((D, R), BF16),
            pltpu.VMEM((R, 4 * E), F32),
            dma((2, 3, NCH)),
            dma((2, 3, NCH)),
            dma((4, SLOTS)),
            dma((4, SLOTS)),
            dma((6, SLOTS)),
            dma((4,)),
        ],
        compiler_params=pltpu.CompilerParams(
            collective_id=0, has_side_effects=True, vmem_limit_bytes=VMEM_LIMIT
        ),
        cost_estimate=pl.CostEstimate(
            flops=2 * R * D * D, bytes_accessed=16 << 20, transcendentals=R * D
        ),
        name="gather_project",
    )(tokens, cotangent, w)


def attention_kernel(
    q_ref, kv_ref, up_ref, cg_ref, wo_all, all_ids,
    op_ref, gated_ref, dup_ref, dq_ref, dkv_ref, dfar_ref,
    id_ref, idc, acc, tot, tot_t,
):
    s = lax.axis_index("seq")
    chip = lax.div(s, 2)
    wo_ref = wo_all.at[lax.rem(s, 2)]
    t = pl.program_id(0)

    @pl.when(t == 0)
    def _():
        for b in range(3):
            source = chip - 2 + b
            ids = all_ids[rows_at(jnp.maximum(source, 0) * (R // E), R // E), :]
            ids = jnp.where(source >= 0, ids, -1)
            for j in range(R // E):
                at = b * R + j * E
                row = ids[j : j + 1, :]
                id_ref[0:1, at : at + E] = row
                idc[at : at + E, :] = jnp.broadcast_to(row, (E, E)).T

        @pl.loop(0, WIN // TK)
        def _(j):
            acc[rows_at(j * TK, TK), :] = jnp.zeros((TK, 2 * E), F32)

    def spread(column, width):
        return jnp.concatenate([column] * (width // E), axis=1)

    first = 2 * R // TK
    q = q_ref[...]
    wr = rows_at(2 * R + t * TQ, TQ)
    idq_col = idc[wr, :]
    idq_row = id_ref[0:1, wr]
    start = idq_row[0, 0]
    before = (id_ref[...] < start).astype(jnp.int32)
    low = jnp.sum(before) // TK
    last = first + t * TQ // TK
    uniform = start == idq_row[0, TQ - 1]
    mid = jnp.where(uniform, jnp.minimum(low + 1, last), last)

    def masked(half, ok, kt, causal, row_axis):
        if causal:
            ri = lax.broadcasted_iota(jnp.int32, half.shape, row_axis) + t * TQ
            ci = lax.broadcasted_iota(jnp.int32, half.shape, 1 - row_axis) + (kt - first) * TK
            ok = ok & (ci <= ri)
        return jnp.where(ok, half, OUT_OF_MASK)

    def forward(kt, mask=True, causal=False):
        kr = rows_at(kt * TK, TK)
        half = dot(q, kv_ref[kr, E:], NT) * (0.5 * SCALE)
        if mask:
            half = masked(half, spread(idq_col, TK) == id_ref[0:1, kr], kt, causal, 0)
        weights = (half + half * jnp.tanh(half)).astype(BF16)
        tot[...] += dot(weights, kv_ref[kr, :E])

    def backward(kt, mask=True, causal=False):
        kr = rows_at(kt * TK, TK)
        k = kv_ref[kr, E:]
        half = dot(k, q, NT) * (0.5 * SCALE)
        if mask:
            half = masked(half, spread(idc[kr, :], TQ) == idq_row, kt, causal, 1)
        tan = jnp.tanh(half)
        weights = half + half * tan
        tan = 0.5 * tan
        slope = (0.5 + tan) + weights * (0.5 - tan)
        ds = (slope * dot(kv_ref[kr, :E], grad, NT)).astype(BF16)
        acc[kr, E:] += dot(ds, q)
        acc[kr, :E] += dot(weights.astype(BF16), grad)
        tot_t[...] += dot(k.T, ds)

    def over_keys(step, total):
        total[...] = jnp.zeros_like(total)

        @pl.loop(low, mid)
        def _(kt):
            step(kt)

        @pl.loop(mid, last)
        def _(kt):
            step(kt, mask=False)

        for j in range(max(1, TQ // TK)):
            step(last + j, causal=True)
        return total[...]

    att = over_keys(forward, tot)
    center = att - jnp.mean(att, -1, keepdims=True)
    scale = lax.rsqrt(jnp.mean(center * center, -1, keepdims=True) + FLOOR)
    hn = center * scale
    up = up_ref[...].astype(F32)
    gated = (hn * up).astype(BF16)
    gated_ref[...] = gated
    op_ref[0] = dot(gated, wo_ref[:, :HALF]).astype(BF16)
    op_ref[1] = dot(gated, wo_ref[:, HALF:]).astype(BF16)
    gg = dot(cg_ref[0], wo_ref[:, :HALF], NT) + dot(cg_ref[1], wo_ref[:, HALF:], NT)
    dup_ref[...] = gg * hn
    b = gg * up
    grad = (
        scale * (b - jnp.mean(b, -1, keepdims=True) - hn * jnp.mean(b * hn, -1, keepdims=True))
    ).astype(BF16)
    dq_ref[...] = over_keys(backward, tot_t).T * SCALE

    @pl.when(t == R // TQ - 1)
    def _():
        @pl.loop(0, R // TK)
        def _(j):
            rr = rows_at(j * TK, TK)
            own = rows_at(2 * R + j * TK, TK)
            dkv_ref[rr, :E] = acc[own, :E]
            dkv_ref[rr, E:] = acc[own, E:] * SCALE
            for k in range(2):
                src = rows_at(k * R + j * TK, TK)
                dfar_ref[k, rr, :E] = acc[src, :E].astype(BF16)
                dfar_ref[k, rr, E:] = (acc[src, E:] * SCALE).astype(BF16)


def attention(q, kv, up, cg, wo, ids):
    vm = pl.BlockSpec(memory_space=pltpu.VMEM)
    tile = pl.BlockSpec((TQ, E), lambda t: (t, 0))
    halves = pl.BlockSpec((2, TQ, HALF), lambda t: (0, t, 0))
    return pl.pallas_call(
        attention_kernel,
        grid=(R // TQ,),
        out_shape=(
            jax.ShapeDtypeStruct((2, R, HALF), BF16),
            jax.ShapeDtypeStruct((R, E), BF16),
            jax.ShapeDtypeStruct((R, E), F32),
            jax.ShapeDtypeStruct((R, E), F32),
            jax.ShapeDtypeStruct((R, 2 * E), F32),
            jax.ShapeDtypeStruct((2, R, 2 * E), BF16),
        ),
        in_specs=[tile, vm, tile, halves, vm, vm],
        out_specs=(
            halves,
            tile,
            tile,
            tile,
            pl.BlockSpec((R, 2 * E), lambda t: (0, 0)),
            pl.BlockSpec((2, R, 2 * E), lambda t: (0, 0, 0)),
        ),
        scratch_shapes=[
            pltpu.VMEM((1, WIN), jnp.int32),
            pltpu.VMEM((WIN, E), jnp.int32),
            pltpu.VMEM((WIN, 2 * E), F32),
            pltpu.VMEM((TQ, E), F32),
            pltpu.VMEM((E, TQ), F32),
        ],
        compiler_params=pltpu.CompilerParams(vmem_limit_bytes=VMEM_LIMIT),
        cost_estimate=pl.CostEstimate(
            flops=7 * 2 * R * R * 2 * E, bytes_accessed=16 << 20, transcendentals=4 * R * R
        ),
        name="attention",
    )(q, kv, up, cg, wo, ids)


class Summed:
    def __init__(self, me, rows, grads, bufs, sems, at):
        self.me, self.rows, self.grads, self.bufs = me, rows, grads, bufs
        self.sems, self.at = sems, at
        self.done = []

    def copy(self, src, dst, stage, k, device):
        copy = Copy(src, dst, self.sems, (self.at, stage, k), device).start()
        self.done.append(copy)
        return copy

    def peers(self, here, step):
        s, c = self.me.s, self.me.c
        there = [lax.rem(here + k, 4) for k in (1, 2, 3)]
        return [(v, (s + step * (v - here), c)) for v in there]

    def start(self):
        zbuf, zrecv = self.bufs[0:2]
        n = self.rows // 4
        zbuf[...] = self.grads[...].astype(BF16)
        self.zc = [
            self.copy(zbuf.at[rows_at(v * n, n)], zrecv.at[k], 0, k, device)
            for k, (v, device) in enumerate(self.peers(self.me.z, 8))
        ]

    def over_y(self):
        zrecv, yall = self.bufs[1:3]
        n = self.rows // 4
        for copy in self.zc:
            copy.wait_recv()
        total = self.grads[rows_at(self.me.z * n, n), :]
        for k in range(3):
            total = total + zrecv[k].astype(F32)
        spot = yall.at[self.me.y]
        spot[...] = total.astype(BF16)
        self.yc = [
            self.copy(spot, spot, 1, k, device) for k, (_, device) in enumerate(self.peers(self.me.y, 2))
        ]

    def over_x(self):
        yall, xall = self.bufs[2:4]
        for copy in self.yc:
            copy.wait_recv()
        total = (yall[0].astype(F32) + yall[1].astype(F32)) + (yall[2].astype(F32) + yall[3].astype(F32))
        spot = xall.at[self.me.xl]
        spot[...] = total.astype(BF16)
        self.xc = self.copy(spot, spot, 2, 0, self.me.xpeer)

    def back_z(self):
        xall, whole = self.bufs[3:5]
        me = self.me
        self.xc.wait_recv()
        spot = whole.at[me.core, me.z]
        spot[...] = (xall[0].astype(F32) + xall[1].astype(F32)).astype(BF16)
        self.gz = [
            self.copy(spot, spot, 3, k, device) for k, (_, device) in enumerate(self.peers(me.z, 8))
        ]
        self.gc = [self.copy(spot, spot, 4, 0, me.other)]

    def back_core(self):
        me = self.me
        for k in range(3):
            self.gz[k].wait_recv()
            spot = self.bufs[4].at[me.core, lax.rem(me.z + 3 - k, 4)]
            self.gc.append(self.copy(spot, spot, 4, k + 1, me.other))

    def finish(self):
        for copy in self.gc:
            copy.wait_recv()

    def wait_send(self):
        for copy in self.done:
            copy.wait_send()

    @staticmethod
    def scratch(rows):
        n = rows // 4
        return [
            pltpu.VMEM((rows, 2 * E), BF16),
            pltpu.VMEM((3, n, 2 * E), BF16),
            pltpu.VMEM((4, n, 2 * E), BF16),
            pltpu.VMEM((2, n, 2 * E), BF16),
        ]


EARLY = D + 2 * E
INV_ROOT = 1.0 / 256.0


def gradient_kernel(
    tok_in, cot_in, w_in, nb_in, rs_in, cg_in, gated_in, op_in, dup_in, dq_in, dkv_in, dfar_in, nt_in, sl_in,
    out_ref, gt_ref, early_all, late_all,
    tok_ref, cot_ref, w_ref, nb_ref, rs_ref, cg_ref, gated_ref, op_ref, dup_ref, dq_ref, dkv_ref, dfar_ref, nt_ref, slope, ls,
    hopped, back, yvia, nvia, gp, part, chip_sum, to_col, from_col, early_g, late_g, *rest,
):
    early_bufs, late_bufs = rest[:4] + (early_all,), rest[4:8] + (late_all,)
    bss, brs, sss, srs, ass, ars = rest[8:]
    me = Place()
    c, core, chip = me.c, me.core, me.chip
    behind = me.at_chip(chip - 1)
    round_to = me.at_chip(me.in_ring(1))
    source = me.in_ring(-1)
    handed_to = me.at_chip(source - 2)
    two_on = lax.rem(chip + 2, CHIPS)
    two_y = lax.rem(two_on, 4)
    hander = me.at_chip(two_on - two_y + lax.rem(two_y + 1, 4))
    early = Summed(me, EARLY, early_g, early_bufs, (ass, ars), 0)
    late = Summed(me, D, late_g, late_bufs, (ass, ars), 1)
    greet(
        [me.other, me.far, me.at_chip(chip + 1), me.at_chip(chip + 4), round_to, me.at_chip(source)]
        + [hander, me.xpeer, me.at_chip(chip - 15)]
        + [device for _, device in early.peers(me.y, 2) + early.peers(me.z, 8)],
        15,
    )

    base = core * T
    obase = (1 - core) * T

    order = (
        (dfar_in.at[1], dfar_ref), (sl_in, slope), (dup_in, dup_ref), (dq_in, dq_ref), (nt_in, nt_ref), (gated_in, gated_ref),
        (cg_in, cg_ref), (op_in.at[:, rows_at(base, T)], op_ref),
        (dkv_in, dkv_ref), (nb_in, nb_ref), (w_in, w_ref), (rs_in, rs_ref), (tok_in, tok_ref), (cot_in, cot_ref),
    )
    loads = [pltpu.make_async_copy(src, dst, ls.at[k]) for k, (src, dst) in enumerate(order)]

    def mine_of(kind, half, i):
        if kind == 0:
            return op_ref[half, pl.ds(i * CH, CH)]
        return part[half, rows_at(base + i * CH, CH)]

    def to_core(kind, i):
        src = (op_in, part)[kind].at[:, rows_at(obase + i * CH, CH)]
        dst = chip_sum.at[kind, :, pl.ds(i * CH, CH)]
        return Copy(src, dst, (sss, srs), (kind, 0, i), me.other).start()

    def across(kind, i, copy):
        copy.wait_recv()
        here = pl.ds(i * CH, CH)
        mine = mine_of(kind, 1 - c, i).astype(F32)
        to_col[kind, here] = (mine + chip_sum[kind, 1 - c, here].astype(F32)).astype(BF16)
        return Copy(
            to_col.at[kind, here], from_col.at[kind, here], (sss, srs), (kind, 1, i), me.far
        ).start()

    def finish(kind, i, copy):
        copy.wait_recv()
        here = pl.ds(i * CH, CH)
        own, out = ((tok_ref, out_ref), (cot_ref, gt_ref))[kind]
        total = mine_of(kind, c, i).astype(F32)
        total = total + chip_sum[kind, c, here].astype(F32)
        total = total + from_col[kind, here].astype(F32)
        out[here] = (own[here].astype(F32) + total).astype(BF16)

    def slot_rows(i):
        return rows_at((base if i < NCH else obase) + i % NCH * CH, CH)

    near, hop, direct = {}, {}, {}
    for i in range(SLOTS):
        rr = slot_rows(i)
        near[i] = Near(
            me, -1, dfar_in.at[1, rr] if i in BACK_AROUND else back.at[2, rr], nvia.at[i], back.at[1, rr],
            (bss, brs), (i,), i % 2 == 0,
        )
        if i in BACK_AROUND:
            hop[i] = Copy(
                dfar_in.at[0, rr], yvia.at[i], (bss, brs), (2, i), round_to, chip > 1, source > 1
            )
            direct[i] = Copy(
                yvia.at[i], back.at[0, rr], (bss, brs), (3, i), handed_to, source > 1, chip < CHIPS - 2
            )
        else:
            hop[i] = Copy(
                dfar_in.at[0, rr], hopped.at[i], (bss, brs), (2, i), behind,
                chip > 1, (chip > 0) & (chip < CHIPS - 1),
            )
    joined = [i for i in range(SLOTS) if i not in BACK_AROUND]
    for i in joined:
        hop[i].start()
    for i in BACK_AROUND:
        hop[i].start()
        near[i].start()
    for copy in loads:
        copy.start()
    out_core = [to_core(0, i) for i in range(NCH)]

    SR = 512
    for copy in loads[:4]:
        copy.wait()

    @pl.loop(0, R // SR)
    def _(i):
        rr = rows_at(i * SR, SR)
        gp[rr, :E] = (dup_ref[rr, :] * slope[rr, :E]).astype(BF16)
        gp[rr, E : 2 * E] = (dq_ref[rr, :] * slope[rr, E : 2 * E]).astype(BF16)

    for i in BACK_AROUND:
        near[i].hand_on()
    for i in BACK_AROUND:
        hop[i].wait_recv()
        direct[i].start()
    for i in joined:
        rr = slot_rows(i)
        back[2, rr] = dfar_ref[rr]

        @pl.when((chip > 0) & (chip < CHIPS - 1))
        def _():
            hop[i].copy.wait_recv()
            back[2, rr] = (dfar_ref[rr].astype(F32) + hopped[i].astype(F32)).astype(BF16)

        near[i].start()
    for copy in loads[4:7]:
        copy.wait()
    early_g[:D, :] = dot(nt_ref[...], gp[:, : 2 * E])
    for j in range(2):
        early_g[D + j * E : D + (j + 1) * E, :] = dot(gated_ref[...], cg_ref[j], TN)
    early.start()

    for copy in loads[7:]:
        copy.wait()
    out_far = [across(0, i, out_core[i]) for i in range(NCH)]

    for i in joined:
        near[i].hand_on()
    gt_core = {}
    gt_far = []

    def tokens_back(i):
        rr = slot_rows(i)
        g = dot(gp[rr, :], w_ref[...])
        nb = nb_ref[rr, :].astype(F32)
        inv = rs_ref[rr, 0:1]
        g = inv * (g - jnp.mean(g, -1, keepdims=True) - nb * jnp.mean(g * nb, -1, keepdims=True))
        part[0, rr] = g[:, :HALF].astype(BF16)
        part[1, rr] = g[:, HALF:].astype(BF16)
        if i >= NCH:
            gt_core[i - NCH] = to_core(1, i - NCH)
        else:
            gt_far.append(across(1, i, gt_core[i]))

    for turn, i in enumerate(list(BACK_AROUND) + joined):
        rr = slot_rows(i)
        near[i].wait_recv()

        @pl.when(chip == CHIPS - 1)
        def _():
            back[1, rr] = jnp.zeros((CH, 2 * E), BF16)

        g = dkv_ref[rr, :]
        if i in BACK_AROUND:
            direct[i].wait_recv()

            @pl.when(chip >= CHIPS - 2)
            def _():
                back[0, rr] = jnp.zeros((CH, 2 * E), BF16)

            g = g + back[0, rr].astype(F32)
        g = ((g + back[1, rr].astype(F32)) * slope[rr, 2 * E :]).astype(BF16)
        gp[rr, 2 * E :] = g
        tokens_of = nt_ref[:, rr]
        if turn == 0:
            late_g[...] = dot(tokens_of, g)
        else:
            late_g[...] += dot(tokens_of, g)
        if turn == SLOTS - 1:
            late.start()
        if turn < 5:
            tokens_back(i)
        if turn == 3:
            early.over_y()
    early.over_x()
    for i in (list(BACK_AROUND) + joined)[5:]:
        tokens_back(i)
    late.over_y()
    early.back_z()
    late.over_x()
    for i in range(NCH):
        finish(0, i, out_far[i])
    late.back_z()
    early.back_core()
    early.finish()
    late.back_core()
    for i in range(NCH):
        finish(1, i, gt_far[i])
    late.finish()
    for copies in (near, hop, direct):
        for copy in copies.values():
            copy.wait_send()
    for copy in out_core + out_far + list(gt_core.values()) + gt_far + [early, late]:
        copy.wait_send()


def gradients(*operands):
    vm = pl.BlockSpec(memory_space=pltpu.VMEM)
    hbm = pl.BlockSpec(memory_space=pl.ANY)
    dma = pltpu.SemaphoreType.DMA
    loaded = [list(x.shape) for x in operands]
    loaded[7][1] = T
    loaded[11] = [R, 2 * E]
    return pl.pallas_call(
        gradient_kernel,
        out_shape=(
            jax.ShapeDtypeStruct((T, HALF), BF16),
            jax.ShapeDtypeStruct((T, HALF), BF16),
            jax.ShapeDtypeStruct((2, 4, EARLY // 4, 2 * E), BF16),
            jax.ShapeDtypeStruct((2, 4, D // 4, 2 * E), BF16),
        ),
        in_specs=[hbm] * 14,
        out_specs=(vm,) * 4,
        scratch_shapes=[pltpu.VMEM(tuple(d), x.dtype) for d, x in zip(loaded, operands)]
        + [
            dma((14,)),
            pltpu.VMEM((SLOTS, CH, 2 * E), BF16),
            pltpu.VMEM((3, R, 2 * E), BF16),
            pltpu.VMEM((SLOTS, CH, 2 * E), BF16),
            pltpu.VMEM((SLOTS, CH, 2 * E), BF16),
            pltpu.VMEM((R, 4 * E), BF16),
            pltpu.VMEM((2, R, HALF), BF16),
            pltpu.VMEM((2, 2, T, HALF), BF16),
            pltpu.VMEM((2, T, HALF), BF16),
            pltpu.VMEM((2, T, HALF), BF16),
            pltpu.VMEM((EARLY, 2 * E), F32),
            pltpu.VMEM((D, 2 * E), F32),
        ]
        + Summed.scratch(EARLY)
        + Summed.scratch(D)
        + [
            dma((4, SLOTS)),
            dma((4, SLOTS)),
            dma((2, 2, NCH)),
            dma((2, 2, NCH)),
            dma((2, 5, 4)),
            dma((2, 5, 4)),
        ],
        compiler_params=pltpu.CompilerParams(
            collective_id=1, has_side_effects=True, vmem_limit_bytes=VMEM_LIMIT
        ),
        cost_estimate=pl.CostEstimate(
            flops=7 * R * D * D, bytes_accessed=16 << 20, transcendentals=R * D
        ),
        name="gradients",
    )(*operands)


def widen_kernel(out_in, gt_in, early_ref, late_ref, out_ref, gt_ref, gwi_ref, gwo_ref):
    out_ref[...] = out_in[...]
    gt_ref[...] = gt_in[...]
    n = EARLY // 4
    for h in range(2):
        for z in range(4):
            at = 0
            while at < n:
                d = z * n + at
                end = next(b for b in (D, D + E, EARLY) if b > d)
                size = min(n - at, end - d)
                piece = early_ref[h, z, at : at + size, :].astype(F32) * INV_ROOT
                if d < D:
                    for j in range(2):
                        gwi_ref[pl.ds(8 * d + 4 * j + h, size, stride=8), :] = piece[:, j * E : (j + 1) * E]
                else:
                    q, e = divmod(d - D, E)
                    gwo_ref[h, e : e + size, q * HALF : (q + 1) * HALF] = piece
                at += size
            m = D // 4
            piece = late_ref[h, z].astype(F32) * INV_ROOT
            for j in range(2):
                gwi_ref[pl.ds(8 * z * m + 4 * j + 2 + h, m, stride=8), :] = piece[:, j * E : (j + 1) * E]


def widen(out, gt, early, late):
    vm = pl.BlockSpec(memory_space=pltpu.VMEM)
    return pl.pallas_call(
        widen_kernel,
        out_shape=(
            jax.ShapeDtypeStruct((T, HALF), BF16),
            jax.ShapeDtypeStruct((T, HALF), BF16),
            jax.ShapeDtypeStruct((8 * D, E), F32),
            jax.ShapeDtypeStruct((2, E, D), F32),
        ),
        in_specs=[vm] * 4,
        out_specs=(vm,) * 4,
        compiler_params=pltpu.CompilerParams(vmem_limit_bytes=VMEM_LIMIT),
        name="widen",
    )(out, gt, early, late)


def shards(tokens, cotangent, weight_in, weight_out, history_ids):
    wt, nb, inv, q, up, kv, cg, nt, slope = project(tokens, cotangent, weight_in.reshape(8 * D, E))
    op, gated, dup, dq, dkv, dfar = attention(
        q, kv.reshape(WIN, 2 * E), up, cg, weight_out, history_ids.reshape(-1, E)
    )
    out, gt, gwi, gwo = widen(
        *gradients(
            tokens, cotangent, wt, nb, inv, cg, gated, op, dup, dq, dkv, dfar, nt, slope
        )
    )
    return out, gt, gwi.reshape(D, 4, 2, E), gwo


def solution(mesh):
    placed = (
        P("seq", "col"),
        P("seq", "col"),
        P(None, None, "col", None),
        P("col", None, None),
        P(),
    )
    return jax.shard_map(
        shards,
        mesh=mesh,
        in_specs=placed,
        out_specs=(
            P("seq", "col"),
            P("seq", "col"),
            P(None, None, "col", None),
            P("col", None, None),
        ),
        check_vma=False,
    )
```
